128 devices in a mesh: dp: 128 (over y, x, z, core).
Axes of the slice: x: 4, y: 4, z: 4, core: 2. Of those that a mesh axis runs over, the one named last changes fastest.
Arguments:
- tokens: bfloat16 [32768, 1024], P('dp'), may hold values from -6 to 6
- norm_gain: float32 [1024], replicated, may hold values from 0.5 to 1.5
- qkv_weight: bfloat16 [1024, 3072], replicated, may hold values from -0.1875 to 0.1875
- out_weight: bfloat16 [1024, 1024], replicated, may hold values from -0.5 to 0.5
- ln_gain: float32 [1024], replicated, may hold values from 0.5 to 1.5
- ln_bias: float32 [1024], replicated, may hold values from -1 to 1
- up_weight: bfloat16 [1024, 4096], replicated, may hold values from -0.1875 to 0.1875
- down_weight: bfloat16 [4096, 1024], replicated, may hold values from -0.125 to 0.125
- buckets: int32 [32768, 1], P('dp'), may hold values from 0 to 3, as said below
- router_prob: float32 [32768], P('dp'), may hold values from 0.5 to 1
- heads_active: int32 [128, 3], P('dp'), may hold values from 8 to 16
- doc_lengths: int32 [128, 3], P('dp'), may hold values from 1 to 128, 256 in all within a row
- cotangent: bfloat16 [32768, 1024], P('dp'), may hold values from -24 to 24
Outputs:
- mixed: bfloat16 [32768, 1024], P('dp')
- input_grad: float32 [32768, 1024], P('dp')
- norm_gain_grad: float32 [1024], P('dp')
- qkv_grad: float32 [1024, 3072], P('dp')
- out_grad: float32 [1024, 1024], P('dp')
- ln_gain_grad: float32 [1024], P('dp')
- ln_bias_grad: float32 [1024], P('dp')
- up_grad: float32 [1024, 4096], P('dp')
- down_grad: float32 [4096, 1024], P('dp')
- bucket_counts: int32 [4], replicated
The draws below stay inside these ranges and needn't reach their ends.
Inputs may be any that keep to these rules, and one draw needn't show every extreme that they name: `buckets`: among the tokens of one device no width level is named by more than 128 tokens, and in every draw some level of some device is named by exactly 128. `doc_lengths`: each row sums to 256 and its largest entry is 128.
All inputs are finite; a program needn't handle non-finite values.
Results may differ from the reference program's by a relative error of at most 0.014.
Values may be sent and summed in bfloat16 or wider, within the bound.
No kernel may reach another device: no remote copies, remote signals or barrier semaphores. Data moves between devices by JAX's collectives and lax.ppermute only.
A program may use at most 320 MiB of HBM per device.

```python
import math
import jax
import jax.numpy as jnp
import numpy as np
from jax import lax

D = 1024
HEADS = 16
HD = 64
FF = 4096
NEST = 4
TOK_DEV = 256
DOCS = 3
SEQ_MAX = 128
MAXB = 128
TOKENS = 32768
N_DP = 128


def draw_buckets(key, part):
    key = jax.random.fold_in(key, 11)
    device_ids = jnp.arange(N_DP, dtype=jnp.int32)
    leading = device_ids * NEST // N_DP
    other_keys = jax.random.split(jax.random.fold_in(key, 1), N_DP)
    order_keys = jax.random.split(jax.random.fold_in(key, 2), N_DP)

    def one_device(lead, other_key, order_key):
        picked = jax.random.randint(other_key, (TOK_DEV - MAXB,), 0, NEST - 1).astype(jnp.int32)
        picked = picked + (picked >= lead).astype(jnp.int32)
        levels = jnp.concatenate([jnp.full((MAXB,), lead, jnp.int32), picked])
        return levels[jax.random.permutation(order_key, TOK_DEV)]
    rows = jax.vmap(one_device)(leading, other_keys, order_keys)
    return rows.reshape(N_DP * TOK_DEV, 1).astype(jnp.int32)


def with_ends(values, key, low, high):
    longest = values.shape.index(max(values.shape))
    spots = []
    for shift in (0, 1):
        where = [jax.random.randint(jax.random.fold_in(key, axis), (), 0, length) for axis, length in enumerate(values.shape)]
        where[longest] = (where[longest] + shift) % values.shape[longest]
        spots.append(tuple(where))
    return values.at[spots[0]].set(low).at[spots[1]].set(high)


def spiked(values, key, source, target, shards_of, factor):
    owner, partner = [(jnp.arange(values.shape[dim]) // (values.shape[dim] // shards_of)).reshape([-1 if axis == dim else 1 for axis in range(values.ndim)]) for dim in (source, target)]
    chosen = jax.random.permutation(key, shards_of)[partner]
    strong = (owner == chosen) | (owner == (partner + shards_of // 2) % shards_of)
    return jnp.where(strong, factor * values, values)


def shard_levels(own_key, extent, shards, least, largest):
    def one(axis_at, shards_of):
        steps = jax.random.uniform(jax.random.fold_in(jax.random.fold_in(own_key, 6), axis_at), (shards_of,), jnp.float32, least / len(shards), largest / len(shards))
        return jnp.repeat(jnp.exp(steps), extent[axis_at] // shards_of).reshape((-1,) + (1,) * (len(extent) - axis_at - 1))

    gain = one(*shards[0])
    for cut in shards[1:]:
        gain = gain * one(*cut)
    return gain


def length_profile(number_of, total, reach, lean):
    weights = [(1 << 20) // math.isqrt(standing ** lean) + 1 for standing in range(2, number_of + 1)]
    spare, given = total - reach - (number_of - 1), [1] * (number_of - 1)
    while spare > 0:
        candidates = [i for i in range(number_of - 1) if given[i] < reach]
        whole, remaining = sum([weights[i] for i in candidates]), spare
        for i in candidates:
            more = min(reach - given[i], max(1, remaining * weights[i] // whole), spare)
            given[i] = given[i] + more
            spare = spare - more
    return np.array([reach] + given)


def uneven(rng, number_of, total, most, slope):
    if number_of == 2:
        one = jax.random.randint(rng, (), max(1, total - most), min(most, total - 1) + 1)
        return jnp.stack([one, total - one])
    lengths = jnp.asarray(length_profile(number_of, total, most, slope), jnp.int32)
    pairs = (number_of - 1) // 2
    giver, sink = lengths[1:1 + 2 * pairs:2], lengths[2:2 + 2 * pairs:2]
    room = jnp.minimum(giver - 1, most - sink)
    moved = jax.random.randint(jax.random.fold_in(rng, 1), (pairs,), 0, 1 << 20) % (room + 1)
    lengths = lengths.at[1:1 + 2 * pairs:2].set(giver - moved).at[2:2 + 2 * pairs:2].set(sink + moved)
    return lengths[jax.random.permutation(jax.random.fold_in(rng, 2), number_of)]


def bell_draw(stream_key, extent, width, limit, cuts=(), held_as=jnp.bfloat16):
    entries = jax.random.normal(stream_key, extent, jnp.float32) * width
    if len(cuts) > 0:
        entries = shard_levels(stream_key, extent, cuts, -0.22, 0.18) * entries
    return jnp.clip(entries, min=-limit, max=limit).astype(held_as)


def bell_draw_with(stream_key, dims, width, bound, pieces, heavy, kind=jnp.bfloat16):
    array = width * jax.random.normal(stream_key, dims, jnp.float32)
    if pieces:
        array = array * shard_levels(stream_key, dims, pieces, -0.22, 0.18)
    return jnp.clip(spiked(array, jax.random.fold_in(stream_key, 3), *heavy), -bound, bound).astype(kind)


def setup_inputs(seed: int = 0) -> dict:
    arg_keys = jax.random.split(jax.random.key(seed), 14)
    return {
        "tokens": bell_draw(arg_keys[0], (TOKENS, D), 1.0, 6.0, ((0, 128),)),
        "norm_gain": jnp.clip(1.0 + 0.1 * jax.random.normal(arg_keys[1], (D,), jnp.float32), 0.5, 1.5),
        "qkv_weight": bell_draw(arg_keys[2], (D, 3 * D), D ** -0.5, 0.1875),
        "out_weight": bell_draw(arg_keys[3], (D, D), (D // 8) ** -0.5, 0.5),
        "ln_gain": jnp.clip(1.0 + 0.1 * jax.random.normal(arg_keys[4], (D,), jnp.float32), 0.5, 1.5),
        "ln_bias": bell_draw(arg_keys[5], (D,), 0.2, 1.0, (), jnp.float32),
        "up_weight": bell_draw(arg_keys[6], (D, FF), D ** -0.5, 0.1875),
        "down_weight": bell_draw(arg_keys[7], (FF, D), (FF // 2) ** -0.5, 0.125),
        "buckets": draw_buckets(jax.random.fold_in(arg_keys[13], 71), 0),
        "router_prob": jnp.clip(0.5 + 0.5 * jax.random.uniform(arg_keys[9], (TOKENS,), jnp.float32) ** shard_levels(arg_keys[9], (TOKENS,), ((0, 128),), -0.2, 0.2), 0.5, 1.0),
        "heads_active": with_ends(jax.random.randint(arg_keys[10], (N_DP, DOCS), HEADS // 2, HEADS + 1), jax.random.fold_in(arg_keys[10], 1), HEADS // 2, HEADS).astype(jnp.int32),
        "doc_lengths": jax.vmap(lambda own: uneven(own, DOCS, TOK_DEV, SEQ_MAX, 1))(jax.random.split(arg_keys[11], N_DP)).reshape((N_DP, DOCS)).astype(jnp.int32),
        "cotangent": bell_draw_with(arg_keys[12], (TOKENS, D), 1.0, 24.0, ((0, 128),), (0, 1, 128, 5.5)),
    }


@jax.custom_vjp
def low(v):
    return lax.optimization_barrier(v.astype(jnp.bfloat16)).astype(jnp.float32)

@jax.custom_vjp
def low_back(v):
    return v

def low_keep(v):
    return (low(v), None)

def low_pass(kept, grad):
    return (grad,)

def back_keep(v):
    return (v, None)

def back_low(kept, grad):
    return (low(grad),)
low.defvjp(low_keep, low_pass)
low_back.defvjp(back_keep, back_low)
NEG = -1e+30
EPS = 1e-05
HIGH = lax.Precision.HIGHEST

def matmul(left, right):
    return jnp.dot(left, right, precision=HIGH, preferred_element_type=jnp.float32)

def layout(length_row, head_row, count, heads):
    ends_at = jnp.cumsum(length_row).astype(jnp.int32)
    starts_at = ends_at - length_row
    places = jnp.arange(count, dtype=jnp.int32)
    owner_doc = lax.optimization_barrier(jnp.sum((places[:, None] >= ends_at[None, :]).astype(jnp.int32), -1))
    doc_pick = (owner_doc[:, None] == jnp.arange(length_row.shape[0], dtype=jnp.int32)[None, :]).astype(jnp.int32)
    position = places - lax.optimization_barrier(jnp.sum(doc_pick * starts_at[None, :], -1))
    active = lax.optimization_barrier(jnp.sum(doc_pick * head_row[None, :], -1))
    head_mask = (jnp.arange(heads, dtype=jnp.int32)[None, :] < active[:, None]).astype(jnp.float32)
    visible = (owner_doc[:, None] == owner_doc[None, :]) & (places[None, :] <= places[:, None])
    return (position, head_mask, visible)

def angles(position, head_dim):
    inverse = 10000.0 ** (-2.0 * jnp.arange(head_dim // 2, dtype=jnp.float32) / head_dim)
    phase = position.astype(jnp.float32)[:, None] * inverse[None, :]
    return (jnp.cos(phase)[:, None, :], jnp.sin(phase)[:, None, :])

def rotate(values, cosine, sine):
    half_dim = values.shape[-1] // 2
    first_half = values[..., :half_dim]
    second_half = values[..., half_dim:]
    return jnp.concatenate([first_half * cosine - second_half * sine, second_half * cosine + first_half * sine], -1)

def device_forward(params, inputs):
    norm_gain, qkv_weight, out_weight, ln_gain, ln_bias, up_weight, down_weight = params
    resid, prob_row, bucket_row, length_row, head_row = inputs
    count = resid.shape[0]
    position, head_mask, visible = layout(length_row, head_row, count, HEADS)
    cosine, sine = angles(position, HD)
    rscale = lax.rsqrt(lax.optimization_barrier(jnp.mean(resid * resid, -1, keepdims=True)) + EPS)
    normed_in = low(resid * rscale * norm_gain)
    qkv = low_back(matmul(normed_in, qkv_weight))
    query_r = low(rotate(qkv[:, :D].reshape(count, HEADS, HD), cosine, sine))
    key_r = low(rotate(qkv[:, D:2 * D].reshape(count, HEADS, HD), cosine, sine))
    values = low(qkv[:, 2 * D:].reshape(count, HEADS, HD))
    scores = low_back(jnp.einsum('qhd,khd->hqk', query_r, key_r, precision=HIGH) * HD ** (-0.5))
    scores = jnp.where(visible[None], scores, NEG)
    peak = lax.optimization_barrier(jnp.max(scores, -1, keepdims=True))
    expd = jnp.exp(scores - peak)
    probs = low(expd / lax.optimization_barrier(jnp.sum(expd, -1, keepdims=True)))
    heads_out = jnp.einsum('hqk,khd->qhd', probs, values, precision=HIGH)
    merged = low_back(low((heads_out * head_mask[:, :, None]).reshape(count, D)))
    middle = resid + low_back(matmul(merged, out_weight))
    center = lax.optimization_barrier(jnp.mean(middle, -1, keepdims=True))
    shifted = middle - center
    rstd = lax.rsqrt(lax.optimization_barrier(jnp.mean(shifted * shifted, -1, keepdims=True)) + EPS)
    zed = low_back(low(shifted * rstd * ln_gain + ln_bias))
    pre = low_back(matmul(zed, up_weight))
    width_mask = (jnp.arange(FF, dtype=jnp.int32)[None, :] < (bucket_row[:, None] + 1) * (FF // NEST)).astype(jnp.float32)
    act = low(jnp.square(jax.nn.relu(pre)) * width_mask)
    branch = low_back(low(matmul(act, down_weight)))
    return middle + prob_row[:, None] * branch

def reference(tokens, norm_gain, qkv_weight, out_weight, ln_gain, ln_bias, up_weight, down_weight, buckets, router_prob, heads_active, doc_lengths, cotangent):
    params = (norm_gain.astype(jnp.float32), qkv_weight.astype(jnp.float32), out_weight.astype(jnp.float32), ln_gain.astype(jnp.float32), ln_bias.astype(jnp.float32), up_weight.astype(jnp.float32), down_weight.astype(jnp.float32))
    resid = tokens.astype(jnp.float32).reshape(N_DP, TOK_DEV, D)
    prob_rows = router_prob.astype(jnp.float32).reshape(N_DP, TOK_DEV)
    bucket_rows = buckets[:, 0].reshape(N_DP, TOK_DEV)
    step_fn = jax.checkpoint(device_forward)

    def whole(params, resid):
        return lax.map(lambda inputs: step_fn(params, inputs), (resid, prob_rows, bucket_rows, doc_lengths, heads_active))
    output, pullback = jax.vjp(whole, params, resid)
    grads, grad_resid = pullback(cotangent.astype(jnp.float32).reshape(N_DP, TOK_DEV, D))
    counts = lax.optimization_barrier(jnp.sum((buckets[:, 0][:, None] == jnp.arange(NEST, dtype=jnp.int32)[None, :]).astype(jnp.int32), 0))
    return (output.reshape(TOKENS, D).astype(jnp.bfloat16), grad_resid.reshape(TOKENS, D), grads[0], grads[1], grads[2], grads[3], grads[4], grads[5], grads[6], counts)
```

```python
import jax
import jax.numpy as jnp
from jax import lax
from jax.sharding import Mesh
from jax.sharding import PartitionSpec as P

HEADS = 16
HD = 64
NEST = 4
AX = ("y", "x", "z", "c")

NEG = -1e30
EPS = 1e-05
F32 = jnp.float32
BF16 = jnp.bfloat16


def contract(left, right, left_dim, right_dim):
    return lax.dot_general(
        left, right, (((left_dim,), (right_dim,)), ((), ())), preferred_element_type=F32
    )


def layout(length_row, head_row, count, heads):
    ends_at = jnp.cumsum(length_row)
    starts_at = ends_at - length_row
    places = jnp.arange(count, dtype=jnp.int32)
    owner_doc = jnp.sum((places[:, None] >= ends_at[None, :]).astype(jnp.int32), -1)
    doc_pick = (
        owner_doc[:, None] == jnp.arange(length_row.shape[0], dtype=jnp.int32)[None, :]
    ).astype(jnp.int32)
    position = places - jnp.sum(doc_pick * starts_at[None, :], -1)
    active = jnp.sum(doc_pick * head_row[None, :], -1)
    head_mask = (jnp.arange(heads, dtype=jnp.int32)[None, :] < active[:, None]).astype(F32)
    visible = (owner_doc[:, None] == owner_doc[None, :]) & (places[None, :] <= places[:, None])
    return (position, head_mask, visible)


def angles(position, head_dim):
    inverse = 10000.0 ** (-2.0 * jnp.arange(head_dim // 2, dtype=F32) / head_dim)
    phase = position.astype(F32)[:, None] * inverse[None, :]
    return (jnp.cos(phase)[:, None, :], jnp.sin(phase)[:, None, :])


def rotate(values, cosine, sine):
    half_dim = values.shape[-1] // 2
    first_half = values[..., :half_dim]
    second_half = values[..., half_dim:]
    return jnp.concatenate(
        [first_half * cosine - second_half * sine, second_half * cosine + first_half * sine], -1
    )


def unrotate(grads, cosine, sine):
    return rotate(grads, cosine, -sine)


def swap_cores(array):
    return lax.ppermute(array, "c", [(0, 1), (1, 0)])


def pairs(mask_0, mask_1):
    perm = []
    for p in range(4):
        perm.append((2 * p, 2 * (p ^ mask_0)))
        perm.append((2 * p + 1, 2 * (p ^ mask_1) + 1))
    return perm


def pick(array, index, dim):
    return lax.dynamic_index_in_dim(array, index, dim, keepdims=False)


def scatter_axis(grad, dim, axis):
    p = lax.axis_index(axis)
    core = lax.axis_index("c")
    first = jnp.where(core == 0, p ^ 1, p ^ 3)
    second = jnp.where(core == 0, p ^ 3, p ^ 1)
    sent = jnp.stack([pick(grad, first, dim), pick(grad, p ^ 2, dim)]).astype(BF16)
    got = lax.ppermute(sent, (axis, "c"), pairs(1, 3))
    sent = (got[1].astype(F32) + pick(grad, second, dim).astype(F32)).astype(BF16)
    got_2 = lax.ppermute(sent, (axis, "c"), pairs(3, 1))
    return got[0].astype(F32) + pick(grad, p, dim).astype(F32) + got_2.astype(F32)


def scatter_chips(grad, order):
    left = ["y", "x", "z"]
    for axis in order:
        dim = left.index(axis)
        left.pop(dim)
        grad = scatter_axis(grad, dim, axis)
    return grad


def by_chip(grad):
    return grad.reshape(4, 4, 4, -1, grad.shape[1])


def my_half(array, core):
    half = array.shape[1] // 2
    return lax.dynamic_slice_in_dim(array, core * half, half, 1)


def other_half(array, core):
    return my_half(array, 1 - core)


def body(
    tokens,
    norm_gain,
    qkv_weight,
    out_weight,
    ln_gain,
    ln_bias,
    up_weight,
    down_weight,
    buckets,
    router_prob,
    heads_active,
    doc_lengths,
    cotangent,
):
    core = lax.axis_index("c")
    count = tokens.shape[0]
    width = tokens.shape[1]
    hidden_units = up_weight.shape[1]
    block_width = hidden_units // NEST
    position, head_mask, visible = layout(doc_lengths[0], heads_active[0], count, HEADS)
    cosine, sine = angles(position, HD)
    scale = HD ** (-0.5)
    grad_out = cotangent.astype(F32)
    grad_branch_b = (grad_out * router_prob[:, None]).astype(BF16)
    grad_branch_2 = jnp.concatenate(
        [my_half(grad_branch_b, core), swap_cores(other_half(grad_branch_b, core))], 0
    )
    resid = tokens.astype(F32)
    rscale = lax.rsqrt(jnp.mean(resid * resid, -1, keepdims=True) + EPS)
    unit_in = resid * rscale
    normed_b = (unit_in * norm_gain).astype(BF16)
    normed_2 = jnp.concatenate([normed_b, swap_cores(normed_b)], 0)
    qkv = jnp.dot(normed_b, qkv_weight, preferred_element_type=F32)
    query_b = rotate(qkv[:, :width].reshape(count, HEADS, HD), cosine, sine).astype(BF16)
    keys_b = rotate(qkv[:, width : 2 * width].reshape(count, HEADS, HD), cosine, sine).astype(BF16)
    values_b = qkv[:, 2 * width :].reshape(count, HEADS, HD).astype(BF16)
    scores = jnp.einsum("qhd,khd->hqk", query_b, keys_b, preferred_element_type=F32) * scale
    scores = jnp.where(visible[None], scores, NEG)
    peak = jnp.max(scores, -1, keepdims=True)
    expd = jnp.exp(scores - peak)
    probs = expd / jnp.sum(expd, -1, keepdims=True)
    probs_b = probs.astype(BF16)
    heads_out = jnp.einsum("hqk,khd->qhd", probs_b, values_b, preferred_element_type=F32)
    mask_heads = head_mask[:, :, None]
    merged_b = (heads_out * mask_heads).reshape(count, width).astype(BF16)
    merged_2 = jnp.concatenate([merged_b, swap_cores(merged_b)], 0)
    middle = resid + jnp.dot(merged_b, out_weight, preferred_element_type=F32)
    center = jnp.mean(middle, -1, keepdims=True)
    shifted = middle - center
    rstd = lax.rsqrt(jnp.mean(shifted * shifted, -1, keepdims=True) + EPS)
    normed = shifted * rstd
    zed_b = (normed * ln_gain + ln_bias).astype(BF16)
    zed_2 = jnp.concatenate([zed_b, swap_cores(zed_b)], 0)
    bucket = buckets[:, 0]
    picks = (bucket[:, None] == jnp.arange(NEST, dtype=jnp.int32)[None, :]).astype(jnp.int32)
    level_counts = jnp.sum(picks, 0)
    width_mask = (
        jnp.arange(hidden_units, dtype=jnp.int32)[None, :] < (bucket[:, None] + 1) * block_width
    ).astype(F32)
    pre = jnp.dot(zed_b, up_weight, preferred_element_type=F32)
    act_b = (jnp.square(jax.nn.relu(pre)) * width_mask).astype(BF16)
    grad_act = contract(grad_branch_b, down_weight, 1, 1)
    grad_pre_b = (grad_act * 2.0 * jax.nn.relu(pre) * width_mask).astype(BF16)
    act_2 = jnp.concatenate([act_b, swap_cores(act_b)], 0)
    grad_pre_2 = jnp.concatenate(
        [my_half(grad_pre_b, core), swap_cores(other_half(grad_pre_b, core))], 0
    )
    down_part = by_chip(contract(act_2, grad_branch_2, 0, 0).astype(BF16))
    up_part = by_chip(contract(zed_2, grad_pre_2, 0, 0).astype(BF16))
    down_sum = scatter_chips(down_part, "yxz")
    up_sum = scatter_chips(up_part, "xzy")

    branch = jnp.dot(act_b, down_weight, preferred_element_type=F32).astype(BF16).astype(F32)
    mixed = (middle + router_prob[:, None] * branch).astype(BF16)
    grad_zed = contract(grad_pre_b, up_weight, 1, 1).astype(BF16).astype(F32)
    ln_gain_part = jnp.sum(grad_zed * normed, 0)
    ln_bias_part = jnp.sum(grad_zed, 0)
    grad_norm = grad_zed * ln_gain
    grad_mid = grad_out + rstd * (
        grad_norm
        - jnp.mean(grad_norm, -1, keepdims=True)
        - normed * jnp.mean(grad_norm * normed, -1, keepdims=True)
    )
    grad_attn_b = grad_mid.astype(BF16)
    grad_attn_2 = jnp.concatenate(
        [my_half(grad_attn_b, core), swap_cores(other_half(grad_attn_b, core))], 0
    )
    grad_merged = contract(grad_attn_b, out_weight, 1, 1).astype(BF16)
    grad_heads = grad_merged.reshape(count, HEADS, HD) * mask_heads.astype(BF16)
    grad_probs = jnp.einsum("qhd,khd->hqk", grad_heads, values_b, preferred_element_type=F32)
    grad_values = jnp.einsum("hqk,qhd->khd", probs_b, grad_heads, preferred_element_type=F32)
    grad_scores_b = (probs * (grad_probs - jnp.sum(probs * grad_probs, -1, keepdims=True))).astype(
        BF16
    )
    grad_query = unrotate(
        jnp.einsum("hqk,khd->qhd", grad_scores_b, keys_b, preferred_element_type=F32) * scale,
        cosine,
        sine,
    )
    grad_keys = unrotate(
        jnp.einsum("hqk,qhd->khd", grad_scores_b, query_b, preferred_element_type=F32) * scale,
        cosine,
        sine,
    )
    grad_qkv_b = jnp.concatenate(
        [
            grad_query.reshape(count, width),
            grad_keys.reshape(count, width),
            grad_values.reshape(count, width),
        ],
        1,
    ).astype(BF16)
    grad_qkv_2 = jnp.concatenate(
        [my_half(grad_qkv_b, core), swap_cores(other_half(grad_qkv_b, core))], 0
    )
    grad_normed = contract(grad_qkv_b, qkv_weight, 1, 1)
    gain_part = jnp.sum(grad_normed * unit_in, 0)
    grad_unit = grad_normed * norm_gain
    input_grad = grad_mid + rscale * (
        grad_unit - unit_in * jnp.mean(grad_unit * unit_in, -1, keepdims=True)
    )
    qkv_part = contract(normed_2, grad_qkv_2, 0, 0).astype(BF16)
    out_part = contract(merged_2, grad_attn_2, 0, 0).astype(BF16)
    gains = jnp.stack([gain_part, ln_gain_part, ln_bias_part]).reshape(3, 64, 16)
    digits = (level_counts[:, None] >> (2 * jnp.arange(5, dtype=jnp.int32))[None, :]) & 3
    line = jnp.concatenate(
        [
            gains.transpose(1, 0, 2).reshape(64, 48),
            jnp.broadcast_to(digits.reshape(1, 20).astype(F32), (64, 20)),
            jnp.zeros((64, 60), F32),
        ],
        1,
    )
    lines = jnp.pad(line[:, None, :], ((0, 0), (0, 15), (0, 0))).reshape(1024, 128)
    last_part = by_chip(jnp.concatenate([qkv_part, out_part, lines.astype(BF16)], 1))
    last_sum = scatter_chips(last_part, "zyx")

    qkv_cols = qkv_weight.shape[1] // 2
    both_cols = qkv_cols + out_weight.shape[1] // 2
    line_sum = last_sum[:1, both_cols:]
    both_sum = last_sum[:, :both_cols]

    def whole_rows(half_sum):
        halves = half_sum.reshape(2, -1, half_sum.shape[1])
        return pick(halves, core, 0), pick(halves, 1 - core, 0)

    def joined(own, other):
        return jnp.concatenate(
            [jnp.where(core == 0, own, other), jnp.where(core == 0, other, own)], 1
        )

    down_own, down_given = whole_rows(down_sum)
    up_own, up_given = whole_rows(up_sum)
    both_own, both_given = whole_rows(both_sum)
    down_grad = joined(down_own, swap_cores(down_given))
    up_grad = joined(up_own, swap_cores(up_given))
    taken = swap_cores(
        jnp.concatenate([both_given, jnp.pad(line_sum, ((0, 7), (0, 0)))], 1)
    )
    qkv_grad = joined(both_own[:, :qkv_cols], taken[:, :qkv_cols])
    out_grad = joined(both_own[:, qkv_cols:], taken[:, qkv_cols:both_cols])
    line_sum = line_sum[0] + taken[0, both_cols:]
    gain_sums = pick(line_sum[:48].reshape(3, 2, 8), core, 1)
    totals = jnp.sum(
        line_sum[48:68].astype(jnp.int32).reshape(4, 5)
        << (2 * jnp.arange(5, dtype=jnp.int32))[None, :],
        1,
    )
    return (
        mixed,
        input_grad,
        gain_sums[0],
        qkv_grad,
        out_grad,
        gain_sums[1],
        gain_sums[2],
        up_grad,
        down_grad,
        totals,
    )


def solution(mesh):
    finer = Mesh(mesh.devices.reshape(4, 4, 4, 2), AX)
    rows = P(AX, None)
    return jax.shard_map(
        body,
        mesh=finer,
        in_specs=(rows, P(), P(), P(), P(), P(), P(), P(), rows, P(AX), rows, rows, rows),
        out_specs=(rows, rows, P(AX), rows, rows, P(AX), P(AX), rows, rows, P()),
        check_vma=False,
    )
```

```python
import jax
import jax.numpy as jnp
from jax import lax
from jax.experimental import pallas as pl
from jax.experimental.pallas import tpu as pltpu
from jax.sharding import Mesh
from jax.sharding import PartitionSpec as P

HD = 64
NEST = 4
AX = ("y", "x", "z", "c")

NEG = -1e30
EPS = 1e-05
F32 = jnp.float32
BF16 = jnp.bfloat16
T = 256
D = 1024
FF = 4096
GW = 256
GROUPS = D // GW
HB = 1024
TB = 256
DIGITS = 5
MIB = 1024 * 1024


def nn(a, b):
    return lax.dot_general(a, b, (((1,), (0,)), ((), ())), preferred_element_type=F32)


def nt(a, b):
    return lax.dot_general(a, b, (((1,), (1,)), ((), ())), preferred_element_type=F32)


def tn(a, b):
    return lax.dot_general(a, b, (((0,), (0,)), ((), ())), preferred_element_type=F32)


def sds(shape, dtype):
    return jax.ShapeDtypeStruct(shape, dtype)


def fixed(*shape):
    return pl.BlockSpec(shape, lambda *_: (0,) * len(shape))


def smem():
    return pl.BlockSpec(memory_space=pltpu.SMEM)


def call(kernel, name, flops, moved, **kw):
    return pl.pallas_call(
        kernel,
        name=name,
        compiler_params=pltpu.CompilerParams(vmem_limit_bytes=56 * MIB),
        cost_estimate=pl.CostEstimate(flops=flops, bytes_accessed=moved, transcendentals=0),
        **kw,
    )


def first_halves():
    return lax.broadcasted_iota(jnp.int32, (T, 128), 1) % HD < HD // 2


def low_heads():
    return lax.broadcasted_iota(jnp.int32, (T, 128), 1) < HD


def turned(x, cosine, sine, first):
    parts = []
    for at in range(0, x.shape[1], 128):
        part = x[:, at : at + 128]
        other = jnp.where(first, pltpu.roll(part, 128 - HD // 2, 1), pltpu.roll(part, HD // 2, 1))
        parts.append(part * cosine + other * sine)
    return jnp.concatenate(parts, 1)


def doc_start(lengths, place):
    end_0 = lengths[0, 0]
    end_1 = end_0 + lengths[0, 1]
    return jnp.where(place >= end_1, end_1, jnp.where(place >= end_0, end_0, 0))


def of_doc(lengths, place, values):
    end_0 = lengths[0, 0]
    end_1 = end_0 + lengths[0, 1]
    return jnp.where(
        place >= end_1, values[0, 2], jnp.where(place >= end_0, values[0, 1], values[0, 0])
    )


def normalized(middle):
    shifted = middle - jnp.mean(middle, -1, keepdims=True)
    rstd = lax.rsqrt(jnp.mean(shifted * shifted, -1, keepdims=True) + EPS)
    return shifted * rstd, rstd


def front_kernel(
    lengths,
    heads,
    tokens,
    norm_gain,
    inverse,
    wq,
    wk,
    wv,
    wo,
    ln_gain,
    ln_bias,
    cot,
    router,
    q_out,
    k_out,
    v_out,
    turned_out,
    zed_out,
    middle_out,
    cos_out,
    sin_out,
    gb_out,
    normed,
    bias,
    active,
):
    g = pl.program_id(0)
    first = first_halves()
    low = low_heads()

    @pl.when(g == 0)
    def _():
        resid = tokens[...].astype(F32)
        rscale = lax.rsqrt(jnp.mean(resid * resid, -1, keepdims=True) + EPS)
        normed[...] = (resid * rscale * norm_gain[...]).astype(BF16)
        turned_out[1] = normed[...].T
        middle_out[...] = resid
        place = lax.broadcasted_iota(jnp.int32, (T, 128), 0)
        phase = (place - doc_start(lengths, place)).astype(F32) * inverse[...]
        cos_out[...] = jnp.cos(phase)
        sine = jnp.sin(phase)
        sin_out[...] = jnp.where(first, -sine, sine)
        row = lax.broadcasted_iota(jnp.int32, (T, T), 0)
        col = lax.broadcasted_iota(jnp.int32, (T, T), 1)
        bias[...] = jnp.where((col >= doc_start(lengths, row)) & (col <= row), 0.0, NEG)
        active[...] = of_doc(lengths, place, heads)
        gb_out[...] = (cot[...].astype(F32) * router[...]).astype(BF16)

    cosine = cos_out[...]
    sine = sin_out[...]
    x = normed[...]
    q = turned(nn(x, wq[...]), cosine, sine, first).astype(BF16)
    k = turned(nn(x, wk[...]), cosine, sine, first).astype(BF16)
    v = nn(x, wv[...]).astype(BF16)
    q_out[...] = q
    k_out[...] = k
    v_out[...] = v
    zero = jnp.zeros((T, 128), BF16)
    for pair in range(2):
        lanes = slice(128 * pair, 128 * pair + 128)
        qp, kp, vp = q[:, lanes], k[:, lanes], v[:, lanes]
        out = jnp.zeros((T, 128), F32)
        for side in range(2):
            keep = low if side == 0 else ~low
            s = nt(qp, jnp.where(keep, kp, zero)) * (HD**-0.5) + bias[...]
            e = jnp.exp(s - jnp.max(s, -1, keepdims=True))
            p = (e / jnp.sum(e, -1, keepdims=True)).astype(BF16)
            out = out + nn(p, jnp.where(keep, vp, zero))
        head = 4 * g + 2 * pair + jnp.where(low, 0, 1)
        merged = jnp.where(head < active[...], out, 0.0).astype(BF16)
        rows = pl.ds(pl.multiple_of(g * GW + 128 * pair, 128), 128)
        turned_out[2, rows, :] = merged.T
        middle_out[...] += nn(merged, wo[lanes, :])

    @pl.when(g == GROUPS - 1)
    def _():
        normed_mid, _ = normalized(middle_out[...])
        zed = (normed_mid * ln_gain[...] + ln_bias[...]).astype(BF16)
        zed_out[...] = zed
        turned_out[0] = zed.T


def front(lengths, heads, tokens, norm_gain, inverse, qkv_weight, out_weight, ln_gain, ln_bias, cot, router):
    def weight(shift):
        return pl.BlockSpec((D, GW), lambda g: (0, g + shift))

    group = pl.BlockSpec((T, GW), lambda g: (0, g))
    return call(
        front_kernel,
        "front",
        2 * T * D * 4 * D,
        12 * MIB,
        grid=(GROUPS,),
        in_specs=[
            smem(),
            smem(),
            fixed(T, D),
            fixed(1, D),
            fixed(1, 128),
            weight(0),
            weight(GROUPS),
            weight(2 * GROUPS),
            pl.BlockSpec((GW, D), lambda g: (g, 0)),
            fixed(1, D),
            fixed(1, D),
            fixed(T, D),
            fixed(T, 1),
        ],
        out_specs=[group] * 3
        + [fixed(3, D, T), fixed(T, D), fixed(T, D), fixed(T, 128), fixed(T, 128), fixed(T, D)],
        out_shape=[sds((T, D), BF16)] * 3
        + [
            sds((3, D, T), BF16),
            sds((T, D), BF16),
            sds((T, D), F32),
            sds((T, 128), F32),
            sds((T, 128), F32),
            sds((T, D), BF16),
        ],
        scratch_shapes=[
            pltpu.VMEM((T, D), BF16),
            pltpu.VMEM((T, T), F32),
            pltpu.VMEM((T, 128), jnp.int32),
        ],
    )(
        lengths,
        heads,
        tokens,
        norm_gain,
        inverse,
        qkv_weight,
        qkv_weight,
        qkv_weight,
        out_weight,
        ln_gain,
        ln_bias,
        cot,
        router,
    )


def ffn_hidden_kernel(zed, gb, bucket, up, down, out):
    on = bucket[...] >= pl.program_id(0) // (FF // NEST // HB)
    r = jnp.where(on, jnp.maximum(nn(zed[...], up[...]), 0.0), 0.0)
    out[0] = (r * r).astype(BF16)
    out[1] = (nt(gb[...], down[...]) * 2.0 * r).astype(BF16)


def ffn_hidden(zed, gb, bucket, up_weight, down_weight):
    return call(
        ffn_hidden_kernel,
        "ffn_hidden",
        4 * T * D * FF,
        22 * MIB,
        grid=(FF // HB,),
        in_specs=[
            fixed(T, D),
            fixed(T, D),
            fixed(T, 1),
            pl.BlockSpec((D, HB), lambda j: (0, j)),
            pl.BlockSpec((HB, D), lambda j: (j, 0)),
        ],
        out_specs=pl.BlockSpec((2, T, HB), lambda j: (0, 0, j)),
        out_shape=sds((2, T, FF), BF16),
    )(zed, gb, bucket, up_weight, down_weight)


def ffn_ends_kernel(
    hidden, up, down, middle, ln_gain, router, cot, mixed, parts, grad_mid, grad_attn, branch, gz
):
    j = pl.program_id(0)
    b = nn(hidden[0], down[...])
    z = nt(hidden[1], up[...])

    @pl.when(j == 0)
    def _():
        branch[...] = b
        gz[...] = z

    @pl.when(j > 0)
    def _():
        branch[...] += b
        gz[...] += z

    @pl.when(j == FF // HB - 1)
    def _():
        mid = middle[...]
        mixed[...] = (mid + router[...] * branch[...].astype(BF16).astype(F32)).astype(BF16)
        normed, rstd = normalized(mid)
        grad_zed = gz[...].astype(BF16).astype(F32)
        parts[0:1, :] = jnp.sum(grad_zed * normed, 0, keepdims=True)
        parts[1:2, :] = jnp.sum(grad_zed, 0, keepdims=True)
        grad_norm = grad_zed * ln_gain[...]
        grad = cot[...].astype(F32) + rstd * (
            grad_norm
            - jnp.mean(grad_norm, -1, keepdims=True)
            - normed * jnp.mean(grad_norm * normed, -1, keepdims=True)
        )
        grad_mid[...] = grad
        grad_attn[...] = grad.astype(BF16)


def ffn_ends(hidden, up_weight, down_weight, middle, ln_gain, router, cot):
    return call(
        ffn_ends_kernel,
        "ffn_ends",
        4 * T * D * FF,
        24 * MIB,
        grid=(FF // HB,),
        in_specs=[
            pl.BlockSpec((2, T, HB), lambda j: (0, 0, j)),
            pl.BlockSpec((D, HB), lambda j: (0, j)),
            pl.BlockSpec((HB, D), lambda j: (j, 0)),
            fixed(T, D),
            fixed(1, D),
            fixed(T, 1),
            fixed(T, D),
        ],
        out_specs=[fixed(T, D), fixed(8, D), fixed(T, D), fixed(T, D)],
        out_shape=[sds((T, D), BF16), sds((8, D), F32), sds((T, D), F32), sds((T, D), BF16)],
        scratch_shapes=[pltpu.VMEM((T, D), F32)] * 2,
    )(hidden, up_weight, down_weight, middle, ln_gain, router, cot)


def back_kernel(
    lengths, heads, grad_attn, wo, q_in, k_in, v_in, cos_in, sin_in, after, out, bias, active
):
    g = pl.program_id(0)
    first = first_halves()
    low = low_heads()

    @pl.when(g == 0)
    def _():
        query = lax.broadcasted_iota(jnp.int32, (T, T), 1)
        key = lax.broadcasted_iota(jnp.int32, (T, T), 0)
        bias[...] = jnp.where((key >= doc_start(lengths, query)) & (key <= query), 0.0, NEG)
        place = lax.broadcasted_iota(jnp.int32, (T, 128), 0)
        active[...] = of_doc(lengths, place, heads)

    cosine = cos_in[...]
    sine = -sin_in[...]
    grad_merged = nt(grad_attn[...], wo[...])
    zero = jnp.zeros((T, 128), BF16)
    scale = HD**-0.5
    for pair in range(2):
        lanes = slice(128 * pair, 128 * pair + 128)
        head = 4 * g + 2 * pair + jnp.where(low, 0, 1)
        gm = jnp.where(head < active[...], grad_merged[:, lanes], 0.0).astype(BF16)
        qp, kp, vp = q_in[:, lanes], k_in[:, lanes], v_in[:, lanes]
        k_turned = kp.T
        grad_values = jnp.zeros((T, 128), F32)
        grad_keys = jnp.zeros((T, 128), F32)
        grad_query = []
        for side in range(2):
            keep = low if side == 0 else ~low
            q_head = jnp.where(keep, qp, zero)
            gm_head = jnp.where(keep, gm, zero)
            s = nt(kp, q_head) * scale + bias[...]
            e = jnp.exp(s - jnp.max(s, 0, keepdims=True))
            p = e / jnp.sum(e, 0, keepdims=True)
            grad_p = nt(vp, gm_head)
            grad_values = grad_values + nn(p.astype(BF16), gm_head)
            grad_s = (p * (grad_p - jnp.sum(p * grad_p, 0, keepdims=True))).astype(BF16)
            grad_keys = grad_keys + nn(grad_s, q_head)
            grad_query.append(nn(k_turned[HD * side : HD * side + HD], grad_s))
        grad_q = jnp.concatenate(grad_query, 0).T * scale
        out[0, :, lanes] = turned(grad_q, cosine, sine, first).astype(BF16)
        out[1, :, lanes] = turned(grad_keys * scale, cosine, sine, first).astype(BF16)
        out[2, :, lanes] = grad_values.astype(BF16)


def back(lengths, heads, grad_attn, out_weight, q, k, v, cosine, sine, after):
    group = pl.BlockSpec((T, GW), lambda g: (0, g))
    return call(
        back_kernel,
        "attention_back",
        2 * T * D * D + 10 * 16 * T * T * 256,
        8 * MIB,
        grid=(GROUPS,),
        in_specs=[
            smem(),
            smem(),
            fixed(T, D),
            pl.BlockSpec((GW, D), lambda g: (g, 0)),
            group,
            group,
            group,
            fixed(T, 128),
            fixed(T, 128),
            pl.BlockSpec(memory_space=pl.ANY),
        ],
        out_specs=pl.BlockSpec((3, T, GW), lambda g: (0, 0, g)),
        out_shape=sds((3, T, D), BF16),
        scratch_shapes=[pltpu.VMEM((T, T), F32), pltpu.VMEM((T, 128), jnp.int32)],
    )(lengths, heads, grad_attn, out_weight, q, k, v, cosine, sine, after)


def tail_kernel(
    grad_qkv, wq, wk, wv, tokens, norm_gain, grad_mid, bucket, parts, input_grad, lines, acc
):
    j = pl.program_id(0)
    grad_normed = nt(grad_qkv[0], wq[...]) + nt(grad_qkv[1], wk[...]) + nt(grad_qkv[2], wv[...])
    acc[:, pl.ds(pl.multiple_of(j * TB, TB), TB)] = grad_normed

    @pl.when(j == D // TB - 1)
    def _():
        grad = acc[...]
        resid = tokens[...].astype(F32)
        rscale = lax.rsqrt(jnp.mean(resid * resid, -1, keepdims=True) + EPS)
        unit = resid * rscale
        grad_unit = grad * norm_gain[...]
        input_grad[...] = grad_mid[...] + rscale * (
            grad_unit - unit * jnp.mean(grad_unit * unit, -1, keepdims=True)
        )
        row = lax.broadcasted_iota(jnp.int32, (128, 1), 0)
        level = (row - 3) // DIGITS
        digit = (row - 3) % DIGITS
        count = jnp.zeros((128, 1), jnp.int32)
        for n in range(NEST):
            total = jnp.sum((bucket[...] == n).astype(jnp.int32), 0, keepdims=True)
            count = jnp.where(level == n, total, count)
        count = lax.shift_right_logical(count, 2 * digit) & 3
        count = jnp.where((row >= 3) & (row < 3 + DIGITS * NEST), count, 0).astype(F32)
        gain = jnp.sum(grad * unit, 0, keepdims=True)
        wide = jnp.where(row == 0, gain, jnp.where(row == 1, parts[0:1, :], parts[1:2, :]))
        lines[...] = jnp.where(row < 3, wide, count).T.astype(BF16)


def tail(grad_qkv, qkv_weight, tokens, norm_gain, grad_mid, bucket, parts):
    def weight(at):
        return pl.BlockSpec((TB, D), lambda j: (j, at))

    return call(
        tail_kernel,
        "tail",
        2 * T * D * 3 * D,
        10 * MIB,
        grid=(D // TB,),
        in_specs=[
            fixed(3, T, D),
            weight(0),
            weight(1),
            weight(2),
            fixed(T, D),
            fixed(1, D),
            fixed(T, D),
            fixed(T, 1),
            fixed(8, D),
        ],
        out_specs=[fixed(T, D), fixed(D, 128)],
        out_shape=[sds((T, D), F32), sds((D, 128), BF16)],
        scratch_shapes=[pltpu.VMEM((T, D), F32)],
    )(grad_qkv, qkv_weight, qkv_weight, qkv_weight, tokens, norm_gain, grad_mid, bucket, parts)


def store_part(part, sent, kept):
    i = pl.program_id(0)

    @pl.when(i < 2)
    def _():
        sent[...] = part.astype(BF16).reshape(sent.shape)

    @pl.when(i >= 2)
    def _():
        kept[...] = part.astype(BF16).reshape(kept.shape)


def halves_out(lead, rows, columns):
    block = (1, lead, rows, columns)
    return dict(
        out_specs=[
            pl.BlockSpec(block, lambda i, o: (jnp.minimum(i, 1), 0, 0, 0)),
            pl.BlockSpec(block, lambda i, o: (jnp.maximum(i - 2, 0), 0, 0, 0)),
        ],
        out_shape=[sds((2, lead, rows, columns), BF16)] * 2,
    )


def down_grad_kernel(order, act_1, act_2, gb_1, gb_2, sent, kept):
    store_part(tn(act_1[0], gb_1[...]) + tn(act_2[0], gb_2[...]), sent, kept)


def down_grad_parts(order, hidden, hidden_2, gb, gb_2):
    act = pl.BlockSpec((1, T, FF // 4), lambda i, o: (0, 0, o[i]))
    half = pl.BlockSpec((T, D // 2), lambda i, o: (0, o[4]))
    out = halves_out(1, FF // 4, D // 2)
    return call(
        down_grad_kernel,
        "down_grad",
        2 * T * D * FF,
        9 * MIB,
        grid_spec=pltpu.PrefetchScalarGridSpec(
            num_scalar_prefetch=1,
            grid=(4,),
            in_specs=[act, act, half, half],
            out_specs=out["out_specs"],
        ),
        out_shape=out["out_shape"],
    )(order, hidden, hidden_2, gb, gb_2)


def up_grad_kernel(order, zed_1, zed_2, gp_1, gp_2, sent, kept):
    part = nn(zed_1[...].reshape(-1, T), gp_1[0]) + nn(zed_2[...].reshape(-1, T), gp_2[0])
    store_part(part, sent, kept)


def up_grad_parts(order, stack, stack_2, hidden, hidden_2):
    stack, stack_2 = stack.reshape(3, 4, 4, 64, T), stack_2.reshape(3, 4, 4, 64, T)
    zed = pl.BlockSpec((1, 4, 1, 64, T), lambda i, o: (0, 0, o[i], 0, 0))
    half = pl.BlockSpec((1, T, FF // 2), lambda i, o: (1, 0, o[4]))
    out = halves_out(4, 64, FF // 2)
    return call(
        up_grad_kernel,
        "up_grad",
        2 * T * D * FF,
        9 * MIB,
        grid_spec=pltpu.PrefetchScalarGridSpec(
            num_scalar_prefetch=1,
            grid=(4,),
            in_specs=[zed, zed, half, half],
            out_specs=out["out_specs"],
        ),
        out_shape=out["out_shape"],
    )(order, stack, stack_2, hidden, hidden_2)


def last_grad_kernel(
    order, normed_1, normed_2, merged_1, merged_2, gqkv_1, gqkv_2, ga_1, ga_2, lines, sent, kept
):
    normed_1, normed_2 = normed_1[...].reshape(-1, T), normed_2[...].reshape(-1, T)
    merged_1, merged_2 = merged_1[...].reshape(-1, T), merged_2[...].reshape(-1, T)
    parts = [nn(normed_1, gqkv_1[n]) + nn(normed_2, gqkv_2[n]) for n in range(3)]
    parts.append(nn(merged_1, ga_1[...]) + nn(merged_2, ga_2[...]))
    parts.append(lines[...].reshape(-1, 128).astype(F32))
    store_part(jnp.concatenate(parts, 1), sent, kept)


def last_grad_parts(order, stack, stack_2, grad_qkv, grad_qkv_2, grad_attn, grad_attn_2, lines):
    stack, stack_2 = stack.reshape(3, 16, 4, 16, T), stack_2.reshape(3, 16, 4, 16, T)
    normed = pl.BlockSpec((1, 16, 1, 16, T), lambda i, o: (1, 0, o[i], 0, 0))
    merged = pl.BlockSpec((1, 16, 1, 16, T), lambda i, o: (2, 0, o[i], 0, 0))
    third = pl.BlockSpec((3, T, D // 2), lambda i, o: (0, 0, o[4]))
    half = pl.BlockSpec((T, D // 2), lambda i, o: (0, o[4]))
    line = pl.BlockSpec((16, 1, 16, 128), lambda i, o: (0, o[i], 0, 0))
    out = halves_out(16, 16, 2 * D + 128)
    return call(
        last_grad_kernel,
        "qkv_and_out_grad",
        2 * T * D * 4 * D,
        9 * MIB,
        grid_spec=pltpu.PrefetchScalarGridSpec(
            num_scalar_prefetch=1,
            grid=(4,),
            in_specs=[normed, normed, merged, merged, third, third, half, half, line],
            out_specs=out["out_specs"],
        ),
        out_shape=out["out_shape"],
    )(
        order,
        stack,
        stack_2,
        stack,
        stack_2,
        grad_qkv,
        grad_qkv_2,
        grad_attn,
        grad_attn_2,
        lines.reshape(16, 4, 16, 128),
    )


def swap_cores(array):
    return lax.ppermute(array, "c", [(0, 1), (1, 0)])


def pairs(mask_0, mask_1):
    perm = []
    for p in range(4):
        perm.append((2 * p, 2 * (p ^ mask_0)))
        perm.append((2 * p + 1, 2 * (p ^ mask_1) + 1))
    return perm


def pick(array, index, dim):
    return lax.dynamic_index_in_dim(array, index, dim, keepdims=False)


def block_order(axis):
    p = lax.axis_index(axis)
    core = lax.axis_index("c")
    return [p ^ (1 + 2 * core), p ^ 2, p, p ^ (3 - 2 * core)]


def summed(sent, kept, axis):
    got = lax.ppermute(sent, (axis, "c"), pairs(1, 3))
    more = (got[1].astype(F32) + kept[1].astype(F32)).astype(BF16)
    got_2 = lax.ppermute(more, (axis, "c"), pairs(3, 1))
    return got[0].astype(F32) + kept[0].astype(F32) + got_2.astype(F32)


def scatter_axis(grad, dim, axis):
    first, across, own, second = [pick(grad, at, dim) for at in block_order(axis)]
    return summed(jnp.stack([first, across]).astype(BF16), [own, second], axis)


def body(
    tokens,
    norm_gain,
    qkv_weight,
    out_weight,
    ln_gain,
    ln_bias,
    up_weight,
    down_weight,
    buckets,
    router_prob,
    heads_active,
    doc_lengths,
    cotangent,
):
    core = lax.axis_index("c")
    orders = {a: jnp.stack(block_order(a) + [core]).astype(jnp.int32) for a in ("y", "x", "z")}
    norm_gain, ln_gain, ln_bias = [v.reshape(1, D) for v in (norm_gain, ln_gain, ln_bias)]
    router = router_prob.reshape(T, 1)
    inverse = 10000.0 ** (-2.0 * jnp.arange(HD // 2, dtype=F32) / HD)
    inverse = jnp.tile(inverse, 4).reshape(1, 128)

    q, k, v, stack, zed, middle, cosine, sine, gb = front(
        doc_lengths,
        heads_active,
        tokens,
        norm_gain,
        inverse,
        qkv_weight,
        out_weight,
        ln_gain,
        ln_bias,
        cotangent,
        router,
    )
    stack_2, gb_2 = swap_cores(stack), swap_cores(gb)
    hidden = ffn_hidden(zed, gb, buckets, up_weight, down_weight)
    hidden_2 = swap_cores(hidden)
    mixed, parts, grad_mid, grad_attn = ffn_ends(
        hidden, up_weight, down_weight, middle, ln_gain, router, cotangent
    )
    grad_attn_2 = swap_cores(grad_attn)
    down_sent, down_kept = down_grad_parts(orders["y"], hidden, hidden_2, gb, gb_2)
    up_sent, up_kept = up_grad_parts(orders["x"], stack, stack_2, hidden, hidden_2)
    grad_qkv = back(
        doc_lengths, heads_active, grad_attn, out_weight, q, k, v, cosine, sine, up_sent
    )
    grad_qkv_2 = swap_cores(grad_qkv)
    input_grad, lines = tail(grad_qkv, qkv_weight, tokens, norm_gain, grad_mid, buckets, parts)
    last_sent, last_kept = last_grad_parts(
        orders["z"], stack, stack_2, grad_qkv, grad_qkv_2, grad_attn, grad_attn_2, lines
    )

    down_sum = summed(down_sent, down_kept, "y").reshape(4, 4, 64, D // 2)
    down_sum = scatter_axis(scatter_axis(down_sum, 0, "x"), 0, "z")
    up_sum = summed(up_sent, up_kept, "x").reshape(4, 4, 16, FF // 2)
    up_sum = scatter_axis(scatter_axis(up_sum, 1, "z"), 0, "y")
    last_sum = summed(last_sent, last_kept, "z").reshape(4, 4, 16, 2 * D + 128)
    last_sum = scatter_axis(scatter_axis(last_sum, 0, "y"), 0, "x")

    def own_and_given(half_sum):
        halves = half_sum.reshape(2, -1, half_sum.shape[1])
        return pick(halves, core, 0), pick(halves, 1 - core, 0)

    def joined(own, other):
        return jnp.concatenate(
            [jnp.where(core == 0, own, other), jnp.where(core == 0, other, own)], -1
        )

    down_own, down_given = own_and_given(down_sum)
    up_own, up_given = own_and_given(up_sum)
    last_own, last_given = own_and_given(last_sum)
    down_grad = joined(down_own, swap_cores(down_given))
    up_grad = joined(up_own, swap_cores(up_given))
    last_other = swap_cores(last_given)
    weights_own, weights_other = last_own[:, : 2 * D], last_other[:, : 2 * D]
    thirds = joined(
        weights_own[:, : 3 * D // 2].reshape(8, 3, D // 2),
        weights_other[:, : 3 * D // 2].reshape(8, 3, D // 2),
    )
    qkv_grad = thirds.reshape(8, 3 * D)
    out_grad = joined(weights_own[:, 3 * D // 2 :], weights_other[:, 3 * D // 2 :])
    line = last_own[:, 2 * D :] + last_other[:, 2 * D :]
    digits = line[0, 3 : 3 + DIGITS * NEST].astype(jnp.int32).reshape(NEST, DIGITS)
    totals = jnp.sum(digits << (2 * jnp.arange(DIGITS, dtype=jnp.int32))[None, :], 1)
    return (
        mixed,
        input_grad,
        line[:, 0],
        qkv_grad,
        out_grad,
        line[:, 1],
        line[:, 2],
        up_grad,
        down_grad,
        totals,
    )


def solution(mesh):
    finer = Mesh(mesh.devices.reshape(4, 4, 4, 2), AX)
    rows = P(AX, None)
    return jax.shard_map(
        body,
        mesh=finer,
        in_specs=(rows, P(), P(), P(), P(), P(), P(), P(), rows, P(AX), rows, rows, rows),
        out_specs=(rows, rows, P(AX), rows, rows, P(AX), P(AX), rows, rows, P()),
        check_vma=False,
    )
```

```python
import jax
import jax.numpy as jnp
import numpy as np
from jax import lax
from jax.experimental import pallas as pl
from jax.experimental.pallas import tpu as pltpu
from jax.sharding import Mesh
from jax.sharding import PartitionSpec as P

HD = 64
NEST = 4
AX = ("y", "x", "z", "c")

NEG = -1e30
EPS = 1e-05
F32 = jnp.float32
BF16 = jnp.bfloat16
T = 256
D = 1024
FF = 4096
GW = 256
GROUPS = D // GW
DIGITS = 5
MIB = 1024 * 1024


def nn(a, b):
    return lax.dot_general(a, b, (((1,), (0,)), ((), ())), preferred_element_type=F32)


def nt(a, b):
    return lax.dot_general(a, b, (((1,), (1,)), ((), ())), preferred_element_type=F32)


def tn(a, b):
    return lax.dot_general(a, b, (((0,), (0,)), ((), ())), preferred_element_type=F32)


def sds(shape, dtype):
    return jax.ShapeDtypeStruct(shape, dtype)


def smem():
    return pl.BlockSpec(memory_space=pltpu.SMEM)


def vmem():
    return pl.BlockSpec(memory_space=pltpu.VMEM)


def hbm():
    return pl.BlockSpec(memory_space=pl.ANY)


def call(kernel, name, flops, moved, **kw):
    return pl.pallas_call(
        kernel,
        name=name,
        compiler_params=pltpu.CompilerParams(vmem_limit_bytes=56 * MIB),
        cost_estimate=pl.CostEstimate(flops=flops, bytes_accessed=moved, transcendentals=0),
        **kw,
    )


def first_halves():
    return lax.broadcasted_iota(jnp.int32, (T, 128), 1) % HD < HD // 2


def low_heads():
    return lax.broadcasted_iota(jnp.int32, (T, 128), 1) < HD


def turned(x, cosine, sine, first):
    parts = []
    for at in range(0, x.shape[1], 128):
        part = x[:, at : at + 128]
        other = jnp.where(first, pltpu.roll(part, 128 - HD // 2, 1), pltpu.roll(part, HD // 2, 1))
        parts.append(part * cosine + other * sine)
    return jnp.concatenate(parts, 1)


def doc_start(lengths, place):
    end_0 = lengths[0, 0]
    end_1 = end_0 + lengths[0, 1]
    return jnp.where(place >= end_1, end_1, jnp.where(place >= end_0, end_0, 0))


def of_doc(lengths, place, values):
    end_0 = lengths[0, 0]
    end_1 = end_0 + lengths[0, 1]
    return jnp.where(
        place >= end_1, values[0, 2], jnp.where(place >= end_0, values[0, 1], values[0, 0])
    )


def normalized(middle):
    shifted = middle - jnp.mean(middle, -1, keepdims=True)
    rstd = lax.rsqrt(jnp.mean(shifted * shifted, -1, keepdims=True) + EPS)
    return shifted * rstd, rstd


def load(src, dst, sem):
    copy = pltpu.make_async_copy(src, dst, sem)
    copy.start()
    return copy


def columns(j, size):
    return pl.ds(pl.multiple_of(j * size, size), size)


def forward_kernel(
    lengths,
    heads,
    tokens,
    norm_gain,
    inverse,
    ln_gain,
    ln_bias,
    cot,
    router,
    bucket,
    wqkv_hbm,
    wo_hbm,
    up_hbm,
    down_hbm,
    cos_out,
    sin_out,
    qkv_out,
    turned_out,
    middle_out,
    gb_out,
    hidden_out,
    wqkv,
    wo,
    up,
    down,
    qkv,
    turned_in,
    middle,
    gb,
    hidden,
    normed,
    merged,
    zed,
    bias,
    active,
    level,
    in_sem,
    ffn_sem,
    out_sem,
    hidden_sem,
):
    loads = [load(wqkv_hbm.at[:, n * D : (n + 1) * D], wqkv.at[n], in_sem.at[n]) for n in range(3)]
    loads.append(load(wo_hbm, wo, in_sem.at[3]))

    def ffn_loads(j):
        return (
            pltpu.make_async_copy(up_hbm.at[:, columns(j, D)], up.at[j], ffn_sem.at[0, j]),
            pltpu.make_async_copy(down_hbm.at[columns(j, D), :], down.at[j], ffn_sem.at[1, j]),
        )

    for j in range(NEST):
        for copy in ffn_loads(j):
            copy.start()

    first = first_halves()
    low = low_heads()
    resid = tokens[...].astype(F32)
    rscale = lax.rsqrt(jnp.mean(resid * resid, -1, keepdims=True) + EPS)
    normed[...] = (resid * rscale * norm_gain[...]).astype(BF16)
    place = lax.broadcasted_iota(jnp.int32, (T, 128), 0)
    phase = (place - doc_start(lengths, place)).astype(F32) * inverse[...]
    cosine = jnp.cos(phase)
    sine = jnp.sin(phase)
    sine = jnp.where(first, -sine, sine)
    cos_out[...] = cosine
    sin_out[...] = sine
    row = lax.broadcasted_iota(jnp.int32, (T, T), 0)
    col = lax.broadcasted_iota(jnp.int32, (T, T), 1)
    bias[...] = jnp.where((col >= doc_start(lengths, row)) & (col <= row), 0.0, NEG)
    active[...] = of_doc(lengths, place, heads)
    level[...] = upright(bucket[...])
    gb[...] = (cot[...].astype(F32) * upright(router[...])).astype(BF16)
    stores = [load(gb, gb_out, out_sem.at[0])]
    turned_in[1] = normed[...].T
    for n in range(3):
        loads[n].wait()
        part = nn(normed[...], wqkv[n])
        qkv[n] = (turned(part, cosine, sine, first) if n < 2 else part).astype(BF16)
    stores.append(load(qkv, qkv_out, out_sem.at[1]))

    zero = jnp.zeros((T, 128), BF16)

    def heads_of(g, carry):
        for pair in range(2):
            lanes = pl.ds(pl.multiple_of(g * GW + 128 * pair, 128), 128)
            qp, kp, vp = qkv[0, :, lanes], qkv[1, :, lanes], qkv[2, :, lanes]
            out = jnp.zeros((T, 128), F32)
            for side in range(2):
                keep = low if side == 0 else ~low
                s = nt(qp, jnp.where(keep, kp, zero)) * (HD**-0.5) + bias[...]
                e = jnp.exp(s - jnp.max(s, -1, keepdims=True))
                p = (e / jnp.sum(e, -1, keepdims=True)).astype(BF16)
                out = out + nn(p, jnp.where(keep, vp, zero))
            head = 4 * g + 2 * pair + jnp.where(low, 0, 1)
            merged[:, lanes] = jnp.where(head < active[...], out, 0.0).astype(BF16)
        return carry

    lax.fori_loop(0, GROUPS, heads_of, 0)
    turned_in[2] = merged[...].T
    loads[3].wait()
    middle[...] = tokens[...].astype(F32) + nn(merged[...], wo[...])
    stores.append(load(middle, middle_out, out_sem.at[2]))
    normed_mid, _ = normalized(middle[...])
    zed[...] = (normed_mid * ln_gain[...] + ln_bias[...]).astype(BF16)
    turned_in[0] = zed[...].T
    stores.append(load(turned_in, turned_out, out_sem.at[3]))

    def hidden_store(j):
        at = columns(j, D)
        return pltpu.make_async_copy(
            hidden.at[:, :, at], hidden_out.at[:, :, at], hidden_sem.at[j]
        )

    def ffn(j, carry):
        copy_up, copy_down = ffn_loads(j)
        copy_up.wait()
        r = jnp.where(level[...] >= j, jnp.maximum(nn(zed[...], up[j]), 0.0), 0.0)
        hidden[0, :, columns(j, D)] = (r * r).astype(BF16)
        copy_down.wait()
        hidden[1, :, columns(j, D)] = (nt(gb[...], down[j]) * 2.0 * r).astype(BF16)
        hidden_store(j).start()
        return carry

    lax.fori_loop(0, NEST, ffn, 0)
    for copy in stores:
        copy.wait()
    for j in range(NEST):
        hidden_store(j).wait()


def forward(
    lengths, heads, tokens, norm_gain, inverse, ln_gain, ln_bias, cot, router, bucket, *weights
):
    shapes = [
        sds((3, T, D), BF16),
        sds((3, D, T), BF16),
        sds((T, D), F32),
        sds((T, D), BF16),
        sds((2, T, FF), BF16),
    ]
    return call(
        forward_kernel,
        "forward",
        2 * T * D * 4 * D + 4 * T * D * FF,
        34 * MIB,
        in_specs=[smem()] * 2 + [vmem()] * 8 + [hbm()] * 4,
        out_specs=[vmem()] * 2 + [hbm()] * 5,
        out_shape=[sds((T, 128), F32)] * 2 + shapes,
        scratch_shapes=[
            pltpu.VMEM((3, D, D), BF16),
            pltpu.VMEM((D, D), BF16),
            pltpu.VMEM((NEST, D, D), BF16),
            pltpu.VMEM((NEST, D, D), BF16),
        ]
        + [pltpu.VMEM(s.shape, s.dtype) for s in shapes]
        + [
            pltpu.VMEM((T, D), BF16),
            pltpu.VMEM((T, D), BF16),
            pltpu.VMEM((T, D), BF16),
            pltpu.VMEM((T, T), F32),
            pltpu.VMEM((T, 128), jnp.int32),
            pltpu.VMEM((T, 1), jnp.int32),
            pltpu.SemaphoreType.DMA((4,)),
            pltpu.SemaphoreType.DMA((2, NEST)),
            pltpu.SemaphoreType.DMA((4,)),
            pltpu.SemaphoreType.DMA((NEST,)),
        ],
    )(lengths, heads, tokens, norm_gain, inverse, ln_gain, ln_bias, cot, router, bucket, *weights)


def backward_kernel(
    lengths,
    heads,
    middle,
    ln_gain,
    cot,
    router,
    cos_in,
    sin_in,
    hidden_hbm,
    up_hbm,
    down_hbm,
    wo_hbm,
    qkv_hbm,
    mixed,
    parts,
    grad_mid,
    grad_attn_out,
    grad_qkv_out,
    hidden,
    up,
    down,
    wo,
    qkv,
    branch,
    gz,
    grad_attn,
    grad_qkv,
    bias,
    active,
    ffn_sem,
    in_sem,
    out_sem,
    group_sem,
):
    def ffn_loads(j):
        at = columns(j, D)
        return (
            pltpu.make_async_copy(hidden_hbm.at[:, :, at], hidden.at[j], ffn_sem.at[0, j]),
            pltpu.make_async_copy(down_hbm.at[at, :], down.at[j], ffn_sem.at[1, j]),
            pltpu.make_async_copy(up_hbm.at[:, at], up.at[j], ffn_sem.at[2, j]),
        )

    for j in range(NEST):
        for copy in ffn_loads(j):
            copy.start()
    loads = [load(wo_hbm, wo, in_sem.at[0]), load(qkv_hbm, qkv, in_sem.at[1])]

    first = first_halves()
    low = low_heads()
    query = lax.broadcasted_iota(jnp.int32, (T, T), 1)
    key = lax.broadcasted_iota(jnp.int32, (T, T), 0)
    bias[...] = jnp.where((key >= doc_start(lengths, query)) & (key <= query), 0.0, NEG)
    place = lax.broadcasted_iota(jnp.int32, (T, 128), 0)
    active[...] = of_doc(lengths, place, heads)
    branch[...] = jnp.zeros_like(branch)
    gz[...] = jnp.zeros_like(gz)

    def ffn(j, carry):
        copy_hidden, copy_down, copy_up = ffn_loads(j)
        copy_hidden.wait()
        copy_down.wait()
        branch[...] += nn(hidden[j, 0], down[j])
        copy_up.wait()
        gz[...] += nt(hidden[j, 1], up[j])
        return carry

    lax.fori_loop(0, NEST, ffn, 0)
    mid = middle[...]
    mixed[...] = (mid + upright(router[...]) * branch[...].astype(BF16).astype(F32)).astype(BF16)
    normed, rstd = normalized(mid)
    grad_zed = gz[...].astype(BF16).astype(F32)
    parts[0:1, :] = jnp.sum(grad_zed * normed, 0, keepdims=True)
    parts[1:2, :] = jnp.sum(grad_zed, 0, keepdims=True)
    grad_norm = grad_zed * ln_gain[...]
    grad = cot[...].astype(F32) + rstd * (
        grad_norm
        - jnp.mean(grad_norm, -1, keepdims=True)
        - normed * jnp.mean(grad_norm * normed, -1, keepdims=True)
    )
    grad_mid[...] = grad
    grad_attn[...] = grad.astype(BF16)
    store = load(grad_attn, grad_attn_out, out_sem.at[0])
    for copy in loads:
        copy.wait()

    cosine = cos_in[...]
    sine = -sin_in[...]
    zero = jnp.zeros((T, 128), BF16)
    scale = HD**-0.5

    def group_store(g):
        at = columns(g, GW)
        return pltpu.make_async_copy(
            grad_qkv.at[:, :, at], grad_qkv_out.at[:, :, at], group_sem.at[g]
        )

    def heads_of(g, carry):
        grad_merged = nt(grad_attn[...], wo[columns(g, GW), :])
        for pair in range(2):
            lanes = pl.ds(pl.multiple_of(g * GW + 128 * pair, 128), 128)
            head = 4 * g + 2 * pair + jnp.where(low, 0, 1)
            gm = grad_merged[:, 128 * pair : 128 * pair + 128]
            gm = jnp.where(head < active[...], gm, 0.0).astype(BF16)
            qp, kp, vp = qkv[0, :, lanes], qkv[1, :, lanes], qkv[2, :, lanes]
            k_turned = kp.T
            grad_values = jnp.zeros((T, 128), F32)
            grad_keys = jnp.zeros((T, 128), F32)
            grad_query = []
            for side in range(2):
                keep = low if side == 0 else ~low
                q_head = jnp.where(keep, qp, zero)
                gm_head = jnp.where(keep, gm, zero)
                s = nt(kp, q_head) * scale + bias[...]
                e = jnp.exp(s - jnp.max(s, 0, keepdims=True))
                p = e / jnp.sum(e, 0, keepdims=True)
                grad_p = nt(vp, gm_head)
                grad_values = grad_values + nn(p.astype(BF16), gm_head)
                grad_s = (p * (grad_p - jnp.sum(p * grad_p, 0, keepdims=True))).astype(BF16)
                grad_keys = grad_keys + nn(grad_s, q_head)
                grad_query.append(nn(k_turned[HD * side : HD * side + HD], grad_s))
            grad_q = jnp.concatenate(grad_query, 0).T * scale
            grad_qkv[0, :, lanes] = turned(grad_q, cosine, sine, first).astype(BF16)
            grad_qkv[1, :, lanes] = turned(grad_keys * scale, cosine, sine, first).astype(BF16)
            grad_qkv[2, :, lanes] = grad_values.astype(BF16)
        group_store(g).start()
        return carry

    lax.fori_loop(0, GROUPS, heads_of, 0)
    store.wait()
    for g in range(GROUPS):
        group_store(g).wait()


def backward(
    lengths, heads, middle, ln_gain, cot, router, cosine, sine, hidden, up, down, wo, qkv
):
    return call(
        backward_kernel,
        "backward",
        4 * T * D * FF + 2 * T * D * D + 10 * 16 * T * T * 256,
        32 * MIB,
        in_specs=[smem()] * 2 + [vmem()] * 6 + [hbm()] * 5,
        out_specs=[vmem()] * 3 + [hbm()] * 2,
        out_shape=[
            sds((T, D), BF16),
            sds((8, D), F32),
            sds((T, D), F32),
            sds((T, D), BF16),
            sds((3, T, D), BF16),
        ],
        scratch_shapes=[
            pltpu.VMEM((NEST, 2, T, D), BF16),
            pltpu.VMEM((NEST, D, D), BF16),
            pltpu.VMEM((NEST, D, D), BF16),
            pltpu.VMEM((D, D), BF16),
            pltpu.VMEM((3, T, D), BF16),
            pltpu.VMEM((T, D), F32),
            pltpu.VMEM((T, D), F32),
            pltpu.VMEM((T, D), BF16),
            pltpu.VMEM((3, T, D), BF16),
            pltpu.VMEM((T, T), F32),
            pltpu.VMEM((T, 128), jnp.int32),
            pltpu.SemaphoreType.DMA((3, NEST)),
            pltpu.SemaphoreType.DMA((2,)),
            pltpu.SemaphoreType.DMA((1,)),
            pltpu.SemaphoreType.DMA((GROUPS,)),
        ],
    )(lengths, heads, middle, ln_gain, cot, router, cosine, sine, hidden, up, down, wo, qkv)


def upright(row):
    return jnp.broadcast_to(row, (8, T)).T[:, :1]


def both(a, b):
    return jnp.concatenate([a, b], 0)


def ffn_grads_kernel(
    order,
    hidden_1,
    hidden_2,
    gb_1,
    gb_2,
    turned_1,
    turned_2,
    down_sent,
    down_kept,
    up_sent,
    up_kept,
    act,
    gb,
    zed,
    gp,
    down_out,
    up_out,
    gb_sem,
    act_sem,
    gp_sem,
    zed_sem,
    down_sem,
    up_sem,
):
    core = order[0, 4]
    gb_loads = [
        load(ref.at[:, columns(core, D // 2)], gb.at[n], gb_sem.at[n])
        for n, ref in enumerate((gb_1, gb_2))
    ]
    act_loads, zed_loads = [], []
    for i in range(4):
        for n, ref in enumerate((hidden_1, hidden_2)):
            src = ref.at[0, :, columns(order[0, i], D)]
            act_loads.append(load(src, act.at[i, n], act_sem.at[i, n]))
    gp_loads = [
        load(ref.at[1, :, columns(core, FF // 2)], gp.at[n], gp_sem.at[n])
        for n, ref in enumerate((hidden_1, hidden_2))
    ]
    for i in range(4):
        for n, ref in enumerate((turned_1, turned_2)):
            zed_loads.append(load(ref.at[0, :, order[1, i]], zed.at[i, n], zed_sem.at[i, n]))
    stores = []
    for copy in gb_loads:
        copy.wait()
    for i in range(4):
        act_loads[2 * i].wait()
        act_loads[2 * i + 1].wait()
        part = tn(both(act[i, 0], act[i, 1]), both(gb[0], gb[1]))
        down_out[i] = part.astype(BF16)
        place = down_sent.at[i, 0] if i < 2 else down_kept.at[i - 2, 0]
        stores.append(load(down_out.at[i], place, down_sem.at[i]))
    for copy in gp_loads:
        copy.wait()
    for i in range(4):
        zed_loads[2 * i].wait()
        zed_loads[2 * i + 1].wait()
        part = nn(zed[i, 0].reshape(T, T), gp[0]) + nn(zed[i, 1].reshape(T, T), gp[1])
        up_out[i] = part.astype(BF16).reshape(4, 64, FF // 2)
        place = up_sent.at[i] if i < 2 else up_kept.at[i - 2]
        stores.append(load(up_out.at[i], place, up_sem.at[i]))
    for copy in stores:
        copy.wait()


def ffn_grads(order, hidden, hidden_2, gb, gb_2, turned_in, turned_2):
    turned_in, turned_2 = [a.reshape(3, 4, 4, 64, T) for a in (turned_in, turned_2)]
    down = sds((2, 1, FF // 4, D // 2), BF16)
    up = sds((2, 4, 64, FF // 2), BF16)
    return call(
        ffn_grads_kernel,
        "ffn_grads",
        4 * T * D * FF,
        16 * MIB,
        in_specs=[smem()] + [hbm()] * 6,
        out_specs=[hbm()] * 4,
        out_shape=[down, down, up, up],
        scratch_shapes=[
            pltpu.VMEM((4, 2, T, D), BF16),
            pltpu.VMEM((2, T, D // 2), BF16),
            pltpu.VMEM((4, 2, 4, 64, T), BF16),
            pltpu.VMEM((2, T, FF // 2), BF16),
            pltpu.VMEM((4, FF // 4, D // 2), BF16),
            pltpu.VMEM((4, 4, 64, FF // 2), BF16),
            pltpu.SemaphoreType.DMA((2,)),
            pltpu.SemaphoreType.DMA((4, 2)),
            pltpu.SemaphoreType.DMA((2,)),
            pltpu.SemaphoreType.DMA((4, 2)),
            pltpu.SemaphoreType.DMA((4,)),
            pltpu.SemaphoreType.DMA((4,)),
        ],
    )(order, hidden, hidden_2, gb, gb_2, turned_in, turned_2)


LAST = 2 * D + 128


def last_grads_kernel(
    order,
    tokens,
    norm_gain,
    grad_mid,
    bucket,
    parts,
    wqkv_hbm,
    gqkv_1,
    gqkv_2,
    ga_1,
    ga_2,
    turned_1,
    turned_2,
    after,
    input_grad_out,
    sent,
    kept,
    wqkv,
    gqkv,
    gqkv_half,
    ga,
    left,
    input_grad,
    lines,
    out,
    w_sem,
    gqkv_sem,
    half_sem,
    ga_sem,
    left_sem,
    out_sem,
):
    core = order[2, 4]
    loads = []
    for n in range(3):
        loads.append(load(gqkv_1.at[n], gqkv.at[n], gqkv_sem.at[n]))
        loads.append(load(wqkv_hbm.at[:, n * D : (n + 1) * D], wqkv.at[n], w_sem.at[n]))
    half = columns(core, D // 2)
    late = []
    for m, (gq, g_attn) in enumerate(((gqkv_1, ga_1), (gqkv_2, ga_2))):
        late.append(load(gq.at[:, :, half], gqkv_half.at[m], half_sem.at[m]))
        late.append(load(g_attn.at[:, half], ga.at[m], ga_sem.at[m]))
    left_loads = []
    for i in range(4):
        for m, ref in enumerate((turned_1, turned_2)):
            src = ref.at[1:3, :, order[2, i]]
            left_loads.append(load(src, left.at[i, m], left_sem.at[i, m]))

    row = lax.broadcasted_iota(jnp.int32, (128, 1), 0)
    level = (row - 3) // DIGITS
    digit = (row - 3) % DIGITS
    count = jnp.zeros((128, 1), jnp.int32)
    for n in range(NEST):
        total = jnp.sum((bucket[...] == n).astype(jnp.int32), 1, keepdims=True)
        count = jnp.where(level == n, total, count)
    count = lax.shift_right_logical(count, 2 * digit) & 3
    count = jnp.where((row >= 3) & (row < 3 + DIGITS * NEST), count, 0).astype(F32)

    resid = tokens[...].astype(F32)
    rscale = lax.rsqrt(jnp.mean(resid * resid, -1, keepdims=True) + EPS)
    unit = resid * rscale
    grad = jnp.zeros((T, D), F32)
    for n in range(3):
        loads[2 * n].wait()
        loads[2 * n + 1].wait()
        grad = grad + nt(gqkv[n], wqkv[n])
    grad_unit = grad * norm_gain[...]
    input_grad[...] = grad_mid[...] + rscale * (
        grad_unit - unit * jnp.mean(grad_unit * unit, -1, keepdims=True)
    )
    stores = [load(input_grad, input_grad_out, out_sem.at[4])]
    gain = jnp.sum(grad * unit, 0, keepdims=True)
    wide = jnp.where(row == 0, gain, jnp.where(row == 1, parts[0:1, :], parts[1:2, :]))
    lines[...] = jnp.where(row < 3, wide, count).T.astype(BF16).reshape(16, 4, 16, 128)

    for copy in late:
        copy.wait()
    for i in range(4):
        left_loads[2 * i].wait()
        left_loads[2 * i + 1].wait()
        for n in range(4):
            if n < 3:
                right = [gqkv_half[m, n] for m in range(2)]
            else:
                right = [ga[m] for m in range(2)]
            side = 0 if n < 3 else 1
            part = sum(nn(left[i, m, side].reshape(T, T), right[m]) for m in range(2))
            at = slice(n * (D // 2), (n + 1) * (D // 2))
            out[i, :, :, at] = part.astype(BF16).reshape(16, 16, D // 2)
        out[i, :, :, 2 * D :] = lines[:, order[2, i]]
        place = sent.at[i] if i < 2 else kept.at[i - 2]
        stores.append(load(out.at[i], place, out_sem.at[i]))
    for copy in stores:
        copy.wait()


def last_grads(
    order,
    tokens,
    norm_gain,
    grad_mid,
    bucket,
    parts,
    wqkv,
    gqkv,
    gqkv_2,
    ga,
    ga_2,
    turned_in,
    turned_2,
    after,
):
    turned_in, turned_2 = [a.reshape(3, 16, 4, 16, T) for a in (turned_in, turned_2)]
    part = sds((2, 16, 16, LAST), BF16)
    return call(
        last_grads_kernel,
        "last_grads",
        2 * T * D * 7 * D,
        20 * MIB,
        in_specs=[smem()] + [vmem()] * 5 + [hbm()] * 8,
        out_specs=[hbm()] * 3,
        out_shape=[sds((T, D), F32), part, part],
        scratch_shapes=[
            pltpu.VMEM((3, D, D), BF16),
            pltpu.VMEM((3, T, D), BF16),
            pltpu.VMEM((2, 3, T, D // 2), BF16),
            pltpu.VMEM((2, T, D // 2), BF16),
            pltpu.VMEM((4, 2, 2, 16, 16, T), BF16),
            pltpu.VMEM((T, D), F32),
            pltpu.VMEM((16, 4, 16, 128), BF16),
            pltpu.VMEM((4, 16, 16, LAST), BF16),
            pltpu.SemaphoreType.DMA((3,)),
            pltpu.SemaphoreType.DMA((3,)),
            pltpu.SemaphoreType.DMA((2,)),
            pltpu.SemaphoreType.DMA((2,)),
            pltpu.SemaphoreType.DMA((4, 2)),
            pltpu.SemaphoreType.DMA((5,)),
        ],
    )(
        order,
        tokens,
        norm_gain,
        grad_mid,
        bucket,
        parts,
        wqkv,
        gqkv,
        gqkv_2,
        ga,
        ga_2,
        turned_in,
        turned_2,
        after,
    )


def swap_cores(array):
    return lax.ppermute(array, "c", [(0, 1), (1, 0)])


def pairs(mask_0, mask_1):
    perm = []
    for p in range(4):
        perm.append((2 * p, 2 * (p ^ mask_0)))
        perm.append((2 * p + 1, 2 * (p ^ mask_1) + 1))
    return perm


def pick(array, index, dim):
    return lax.dynamic_index_in_dim(array, index, dim, keepdims=False)


def block_order(axis):
    p = lax.axis_index(axis)
    core = lax.axis_index("c")
    return [p ^ (1 + 2 * core), p ^ 2, p, p ^ (3 - 2 * core)]


def summed(sent, kept, axis):
    got = lax.ppermute(sent, (axis, "c"), pairs(1, 3))
    more = (got[1].astype(F32) + kept[1].astype(F32)).astype(BF16)
    got_2 = lax.ppermute(more, (axis, "c"), pairs(3, 1))
    return got[0].astype(F32) + kept[0].astype(F32) + got_2.astype(F32)


def scatter_axis(grad, dim, axis):
    first, across, own, second = [pick(grad, at, dim) for at in block_order(axis)]
    return summed(jnp.stack([first, across]).astype(BF16), [own, second], axis)


def body(
    tokens,
    norm_gain,
    qkv_weight,
    out_weight,
    ln_gain,
    ln_bias,
    up_weight,
    down_weight,
    buckets,
    router_prob,
    heads_active,
    doc_lengths,
    cotangent,
):
    core = lax.axis_index("c")
    orders = jnp.stack([jnp.stack(block_order(axis) + [core]) for axis in ("y", "x", "z")])
    orders = orders.astype(jnp.int32)
    norm_gain, ln_gain, ln_bias = [v.reshape(1, D) for v in (norm_gain, ln_gain, ln_bias)]
    router = router_prob.reshape(1, T)
    levels = buckets.reshape(1, T)
    inverse = np.tile(10000.0 ** (-2.0 * np.arange(HD // 2) / HD), 4).reshape(1, 128)
    inverse = jnp.asarray(inverse, F32)

    cosine, sine, qkv, turned_in, middle, gb, hidden = forward(
        doc_lengths,
        heads_active,
        tokens,
        norm_gain,
        inverse,
        ln_gain,
        ln_bias,
        cotangent,
        router,
        levels,
        qkv_weight,
        out_weight,
        up_weight,
        down_weight,
    )
    hidden_2, turned_2, gb_2 = swap_cores(hidden), swap_cores(turned_in), swap_cores(gb)
    mixed, parts, grad_mid, grad_attn, grad_qkv = backward(
        doc_lengths,
        heads_active,
        middle,
        ln_gain,
        cotangent,
        router,
        cosine,
        sine,
        hidden,
        up_weight,
        down_weight,
        out_weight,
        qkv,
    )
    grad_attn_2, grad_qkv_2 = swap_cores(grad_attn), swap_cores(grad_qkv)
    down_sent, down_kept, up_sent, up_kept = ffn_grads(
        orders, hidden, hidden_2, gb, gb_2, turned_in, turned_2
    )
    input_grad, last_sent, last_kept = last_grads(
        orders,
        tokens,
        norm_gain,
        grad_mid,
        levels,
        parts,
        qkv_weight,
        grad_qkv,
        grad_qkv_2,
        grad_attn,
        grad_attn_2,
        turned_in,
        turned_2,
        up_sent,
    )

    down_sum = summed(down_sent, down_kept, "y").reshape(4, 4, 64, D // 2)
    down_sum = scatter_axis(scatter_axis(down_sum, 0, "x"), 0, "z")
    up_sum = summed(up_sent, up_kept, "x").reshape(4, 4, 16, FF // 2)
    up_sum = scatter_axis(scatter_axis(up_sum, 0, "y"), 0, "z")
    last_sum = summed(last_sent, last_kept, "z").reshape(4, 4, 16, 2 * D + 128)
    last_sum = scatter_axis(scatter_axis(last_sum, 0, "y"), 0, "x")

    def own_and_given(half_sum):
        halves = half_sum.reshape(2, -1, half_sum.shape[1])
        return pick(halves, core, 0), pick(halves, 1 - core, 0)

    def joined(own, other):
        return jnp.concatenate(
            [jnp.where(core == 0, own, other), jnp.where(core == 0, other, own)], -1
        )

    down_own, down_given = own_and_given(down_sum)
    up_own, up_given = own_and_given(up_sum)
    last_own, last_given = own_and_given(last_sum)
    down_grad = joined(down_own, swap_cores(down_given))
    up_grad = joined(up_own, swap_cores(up_given))
    last_other = swap_cores(last_given)
    weights_own, weights_other = last_own[:, : 2 * D], last_other[:, : 2 * D]
    thirds = joined(
        weights_own[:, : 3 * D // 2].reshape(8, 3, D // 2),
        weights_other[:, : 3 * D // 2].reshape(8, 3, D // 2),
    )
    qkv_grad = thirds.reshape(8, 3 * D)
    out_grad = joined(weights_own[:, 3 * D // 2 :], weights_other[:, 3 * D // 2 :])
    line = last_own[:, 2 * D :] + last_other[:, 2 * D :]
    digits = line[0, 3 : 3 + DIGITS * NEST].astype(jnp.int32).reshape(NEST, DIGITS)
    totals = jnp.sum(digits << (2 * jnp.arange(DIGITS, dtype=jnp.int32))[None, :], 1)
    return (
        mixed,
        input_grad,
        line[:, 0],
        qkv_grad,
        out_grad,
        line[:, 1],
        line[:, 2],
        up_grad,
        down_grad,
        totals,
    )


def solution(mesh):
    finer = Mesh(mesh.devices.reshape(4, 4, 4, 2), AX)
    rows = P(AX, None)
    return jax.shard_map(
        body,
        mesh=finer,
        in_specs=(rows, P(), P(), P(), P(), P(), P(), P(), rows, P(AX), rows, rows, rows),
        out_specs=(rows, rows, P(AX), rows, rows, P(AX), P(AX), rows, rows, P()),
        check_vma=False,
    )
```

```python
import functools

import jax
import jax.numpy as jnp
import numpy as np
from jax import lax
from jax.experimental import pallas as pl
from jax.experimental.pallas import tpu as pltpu
from jax.sharding import Mesh
from jax.sharding import PartitionSpec as P

HD = 64
NEST = 4
AX = ("y", "x", "z", "c")

NEG = -1e30
EPS = 1e-05
F32 = jnp.float32
BF16 = jnp.bfloat16
T = 256
D = 1024
FF = 4096
GW = 256
GROUPS = D // GW
FIRST = FF // 2 + 2 * D + 512
SECOND = FF + 512
THIRD = 3 * D + 512 + T
BITS = 9
MIB = 1024 * 1024


def nn(a, b):
    return lax.dot_general(a, b, (((1,), (0,)), ((), ())), preferred_element_type=F32)


def nt(a, b):
    return lax.dot_general(a, b, (((1,), (1,)), ((), ())), preferred_element_type=F32)


def tn(a, b):
    return lax.dot_general(a, b, (((0,), (0,)), ((), ())), preferred_element_type=F32)


def sds(shape, dtype):
    return jax.ShapeDtypeStruct(shape, dtype)


def smem():
    return pl.BlockSpec(memory_space=pltpu.SMEM)


def vmem():
    return pl.BlockSpec(memory_space=pltpu.VMEM)


def hbm():
    return pl.BlockSpec(memory_space=pl.ANY)


def call(kernel, name, flops, moved, **kw):
    return pl.pallas_call(
        kernel,
        name=name,
        compiler_params=pltpu.CompilerParams(vmem_limit_bytes=58 * MIB),
        cost_estimate=pl.CostEstimate(flops=flops, bytes_accessed=moved, transcendentals=0),
        **kw,
    )


def first_halves():
    return lax.broadcasted_iota(jnp.int32, (T, 128), 1) % HD < HD // 2


def low_heads():
    return lax.broadcasted_iota(jnp.int32, (T, 128), 1) < HD


def turned(x, cosine, sine, first):
    parts = []
    for at in range(0, x.shape[1], 128):
        part = x[:, at : at + 128]
        other = jnp.where(first, pltpu.roll(part, 128 - HD // 2, 1), pltpu.roll(part, HD // 2, 1))
        parts.append(part * cosine + other * sine)
    return jnp.concatenate(parts, 1)


def doc_start(lengths, place):
    end_0 = lengths[0, 0]
    end_1 = end_0 + lengths[0, 1]
    return jnp.where(place >= end_1, end_1, jnp.where(place >= end_0, end_0, 0))


def of_doc(lengths, place, values):
    end_0 = lengths[0, 0]
    end_1 = end_0 + lengths[0, 1]
    return jnp.where(
        place >= end_1, values[0, 2], jnp.where(place >= end_0, values[0, 1], values[0, 0])
    )


def normalized(middle):
    shifted = middle - jnp.mean(middle, -1, keepdims=True)
    rstd = lax.rsqrt(jnp.mean(shifted * shifted, -1, keepdims=True) + EPS)
    return shifted * rstd, rstd


def load(src, dst, sem):
    copy = pltpu.make_async_copy(src, dst, sem)
    copy.start()
    return copy


def columns(j, size):
    return pl.ds(pl.multiple_of(j * size, size), size)


def upright(row):
    return jnp.broadcast_to(row, (8, T)).T[:, :1]


def layer_kernel(
    lengths,
    heads,
    order,
    norm_gain,
    inverse,
    ln_gain,
    ln_bias,
    router,
    bucket,
    tokens_hbm,
    cot_hbm,
    wqkv_hbm,
    wo_hbm,
    up_hbm,
    down_hbm,
    first_mine,
    first_other,
    second_mine,
    second_other,
    third_mine,
    third_other,
    mixed_out,
    input_grad_out,
    tokens,
    cot,
    wqkv,
    wo,
    up,
    down,
    qkv,
    normed,
    merged,
    zed,
    gb,
    act,
    act_turned,
    gp,
    turned_f,
    left,
    middle,
    grad_mid,
    ga,
    gqkv,
    mixed,
    lines_f,
    lines,
    bias,
    active,
    level,
    in_sem,
    ffn_sem,
    act_sem,
    gp_sem,
    left_sem,
    group_sem,
    gb_sem,
    ga_sem,
    out_sem,
):
    core = order[0, 4]
    firsts, seconds, thirds = (
        (first_mine, first_other),
        (second_mine, second_other),
        (third_mine, third_other),
    )
    loads = [load(tokens_hbm, tokens, in_sem.at[0])]
    for n in range(3):
        loads.append(load(wqkv_hbm.at[:, n * D : (n + 1) * D], wqkv.at[n], in_sem.at[1 + n]))

    def ffn_loads(j):
        at = columns(j, D)
        return (
            pltpu.make_async_copy(up_hbm.at[:, at], up.at[:, at], ffn_sem.at[0, j]),
            pltpu.make_async_copy(down_hbm.at[at, :], down.at[at, :], ffn_sem.at[1, j]),
        )

    stores = []

    def store_left(n, value, axis, refs, at):
        turned_f[...] = value.astype(F32).T.reshape(turned_f.shape)
        for side, ref in enumerate(refs):
            half = core if side == 0 else 1 - core
            for i in range(4):
                if axis == 0:
                    rows = turned_f[i, :, :, half]
                elif axis == 1:
                    rows = turned_f[:, i, :, half]
                else:
                    rows = turned_f[:, :, i, half]
                left[side, n, pl.ds(128 * i, 128), :] = rows.reshape(128, T).astype(BF16)
            dst = ref.at[pl.ds(at, 512), :]
            stores.append(load(left.at[side, n], dst, left_sem.at[side, n]))

    def block_stores(src, j, refs, at, sem):
        rows = pl.ds(pl.multiple_of(at + T * j, T), T)
        return [
            pltpu.make_async_copy(src.at[:, columns(j, T)], ref.at[rows, :], sem.at[side, j])
            for side, ref in enumerate(refs)
        ]

    first = first_halves()
    low = low_heads()
    zero = jnp.zeros((T, 128), BF16)
    scale = HD**-0.5
    place = lax.broadcasted_iota(jnp.int32, (T, 128), 0)
    phase = (place - doc_start(lengths, place)).astype(F32) * inverse[...]
    cosine = jnp.cos(phase)
    sine = jnp.sin(phase)
    sine = jnp.where(first, -sine, sine)
    row = lax.broadcasted_iota(jnp.int32, (T, T), 0)
    col = lax.broadcasted_iota(jnp.int32, (T, T), 1)
    bias[...] = jnp.where((col >= doc_start(lengths, row)) & (col <= row), 0.0, NEG)
    active[...] = of_doc(lengths, place, heads)
    level[...] = upright(bucket[...])
    prob = upright(router[...])

    loads[0].wait()
    resid = tokens[...].astype(F32)
    rscale = lax.rsqrt(jnp.mean(resid * resid, -1, keepdims=True) + EPS)
    normed[...] = (resid * rscale * norm_gain[...]).astype(BF16)
    for n in range(3):
        loads[1 + n].wait()
        if n == 1:
            loads.append(load(cot_hbm, cot, in_sem.at[4]))
        if n == 2:
            loads.append(load(wo_hbm, wo, in_sem.at[5]))
            for copy in ffn_loads(0) + ffn_loads(1):
                copy.start()
        part = nn(normed[...], wqkv[n])
        qkv[n] = (turned(part, cosine, sine, first) if n < 2 else part).astype(BF16)

    def attend(g, carry):
        for pair in range(2):
            lanes = pl.ds(pl.multiple_of(g * GW + 128 * pair, 128), 128)
            qp, kp, vp = qkv[0, :, lanes], qkv[1, :, lanes], qkv[2, :, lanes]
            out = jnp.zeros((T, 128), F32)
            for side in range(2):
                keep = low if side == 0 else ~low
                s = nt(qp, jnp.where(keep, kp, zero)) * scale + bias[...]
                e = jnp.exp(s - jnp.max(s, -1, keepdims=True))
                p = (e / jnp.sum(e, -1, keepdims=True)).astype(BF16)
                out = out + nn(p, jnp.where(keep, vp, zero))
            head = 4 * g + 2 * pair + jnp.where(low, 0, 1)
            merged[:, lanes] = jnp.where(head < active[...], out, 0.0).astype(BF16)

        @pl.when((g > 0) & (g < NEST - 1))
        def _():
            for copy in ffn_loads(g + 1):
                copy.start()

        return carry

    lax.fori_loop(0, GROUPS, attend, 0)
    loads[5].wait()
    middle[...] = tokens[...].astype(F32) + nn(merged[...], wo[...])
    normed_mid, _ = normalized(middle[...])
    zed[...] = (normed_mid * ln_gain[...] + ln_bias[...]).astype(BF16)
    loads[4].wait()
    gb[...] = (cot[...].astype(F32) * prob).astype(BF16)
    for j in range(4):
        for copy in block_stores(gb, j, firsts, FF // 2, gb_sem):
            copy.start()

    def act_stores(j):
        rows = columns(j, 512)
        return [
            pltpu.make_async_copy(act_turned.at[side, rows, :], ref.at[rows, :], act_sem.at[side, j])
            for side, ref in enumerate(firsts)
        ]

    def hidden(j, carry):
        copy_up, copy_down = ffn_loads(j)
        at = columns(j, D)
        copy_up.wait()
        r = jnp.where(level[...] >= j, jnp.maximum(nn(zed[...], up[:, at]), 0.0), 0.0)
        a = (r * r).astype(BF16)
        act[:, at] = a
        by_core = a.T.reshape(16, 2, 32, T)
        low_rows, high_rows = by_core[:, 0].reshape(512, T), by_core[:, 1].reshape(512, T)
        act_turned[0, columns(j, 512), :] = jnp.where(core == 0, low_rows, high_rows)
        act_turned[1, columns(j, 512), :] = jnp.where(core == 0, high_rows, low_rows)
        for copy in act_stores(j):
            copy.start()
        copy_down.wait()
        gp[:, at] = (nt(gb[...], down[at, :]) * 2.0 * r).astype(BF16)
        for q in range(4):
            for copy in block_stores(gp, 4 * j + q, seconds, 0, gp_sem):
                copy.start()
        return carry

    lax.fori_loop(0, NEST, hidden, 0)
    store_left(0, zed[...], 1, seconds, FF)
    store_left(1, normed[...], 2, thirds, 3 * D)
    store_left(2, merged[...], 0, firsts, FF // 2 + 2 * D)

    branch = nn(act[...], down[...]).astype(BF16).astype(F32)
    mid = middle[...]
    mixed[...] = (mid + prob * branch).astype(BF16)
    stores.append(load(mixed, mixed_out, out_sem.at[1]))
    grad_zed = nt(gp[...], up[...]).astype(BF16).astype(F32)
    normed_mid, rstd = normalized(mid)
    ln_gain_part = jnp.sum(grad_zed * normed_mid, 0, keepdims=True)
    ln_bias_part = jnp.sum(grad_zed, 0, keepdims=True)
    grad_norm = grad_zed * ln_gain[...]
    grad = cot[...].astype(F32) + rstd * (
        grad_norm
        - jnp.mean(grad_norm, -1, keepdims=True)
        - normed_mid * jnp.mean(grad_norm * normed_mid, -1, keepdims=True)
    )
    grad_mid[...] = grad
    ga[...] = grad.astype(BF16)
    for j in range(4):
        for copy in block_stores(ga, j, firsts, FF // 2 + D, ga_sem):
            copy.start()

    bias[...] = jnp.where((row >= doc_start(lengths, col)) & (row <= col), 0.0, NEG)

    def group_stores(g):
        return [
            copy
            for n in range(3)
            for copy in block_stores(gqkv.at[n], g, thirds, n * D, group_sem.at[n])
        ]

    def attend_back(g, carry):
        grad_merged = nt(ga[...], wo[columns(g, GW), :])
        for pair in range(2):
            lanes = pl.ds(pl.multiple_of(g * GW + 128 * pair, 128), 128)
            head = 4 * g + 2 * pair + jnp.where(low, 0, 1)
            gm = grad_merged[:, 128 * pair : 128 * pair + 128]
            gm = jnp.where(head < active[...], gm, 0.0).astype(BF16)
            qp, kp, vp = qkv[0, :, lanes], qkv[1, :, lanes], qkv[2, :, lanes]
            k_turned = kp.T
            grad_values = jnp.zeros((T, 128), F32)
            grad_keys = jnp.zeros((T, 128), F32)
            grad_query = []
            for side in range(2):
                keep = low if side == 0 else ~low
                q_head = jnp.where(keep, qp, zero)
                gm_head = jnp.where(keep, gm, zero)
                s = nt(kp, q_head) * scale + bias[...]
                e = jnp.exp(s - jnp.max(s, 0, keepdims=True))
                p = e / jnp.sum(e, 0, keepdims=True)
                grad_p = nt(vp, gm_head)
                grad_values = grad_values + nn(p.astype(BF16), gm_head)
                grad_s = (p * (grad_p - jnp.sum(p * grad_p, 0, keepdims=True))).astype(BF16)
                grad_keys = grad_keys + nn(grad_s, q_head)
                grad_query.append(nn(k_turned[HD * side : HD * side + HD], grad_s))
            grad_q = jnp.concatenate(grad_query, 0).T * scale
            gqkv[0, :, lanes] = turned(grad_q, cosine, -sine, first).astype(BF16)
            gqkv[1, :, lanes] = turned(grad_keys * scale, cosine, -sine, first).astype(BF16)
            gqkv[2, :, lanes] = grad_values.astype(BF16)
        for copy in group_stores(g):
            copy.start()
        return carry

    lax.fori_loop(0, GROUPS, attend_back, 0)

    grad_normed = nt(gqkv[0], wqkv[0]) + nt(gqkv[1], wqkv[1]) + nt(gqkv[2], wqkv[2])
    resid = tokens[...].astype(F32)
    unit = resid * rscale
    gain_part = jnp.sum(grad_normed * unit, 0, keepdims=True)
    grad_unit = grad_normed * norm_gain[...]
    middle[...] = grad_mid[...] + rscale * (
        grad_unit - unit * jnp.mean(grad_unit * unit, -1, keepdims=True)
    )
    stores.append(load(middle, input_grad_out, out_sem.at[3]))

    item = lax.broadcasted_iota(jnp.int32, (128, 1), 0)
    count = jnp.zeros((128, 1), jnp.int32)
    for n in range(NEST):
        total = jnp.sum((bucket[...] == n).astype(jnp.int32), 1, keepdims=True)
        at = item - 3 - BITS * n
        bit = lax.shift_right_logical(total, jnp.clip(at, 0, BITS - 1)) & 1
        count = jnp.where((at >= 0) & (at < BITS), bit, count)
    wide = jnp.where(item == 0, gain_part, jnp.where(item == 1, ln_gain_part, ln_bias_part))
    lines_f[...] = jnp.where(item < 3, wide, count.astype(F32)).T.reshape(lines_f.shape)
    for side, ref in enumerate(thirds):
        half = core if side == 0 else 1 - core
        for i in range(4):
            part = lines_f[:, :, i, half].reshape(128, 128).astype(BF16)
            lines[side, pl.ds(128 * (i % 2), 128), pl.ds(128 * (i // 2), 128)] = part
        dst = ref.at[pl.ds(3 * D + 512, T), :]
        stores.append(load(lines.at[side], dst, out_sem.at[4 + side]))

    for j in range(NEST):
        for copy in act_stores(j):
            copy.wait()
        for copy in block_stores(gb, j, firsts, FF // 2, gb_sem):
            copy.wait()
        for copy in block_stores(ga, j, firsts, FF // 2 + D, ga_sem):
            copy.wait()
        for copy in group_stores(j):
            copy.wait()
    for j in range(FF // T):
        for copy in block_stores(gp, j, seconds, 0, gp_sem):
            copy.wait()
    for copy in stores:
        copy.wait()


def layer(lengths, heads, order, norm_gain, inverse, ln_gain, ln_bias, router, bucket, *arrays):
    firsts = sds((FIRST, T), BF16)
    seconds = sds((SECOND, T), BF16)
    thirds = sds((THIRD, T), BF16)
    row_b = sds((T, D), BF16)
    row_f = sds((T, D), F32)
    scratch = [
        row_b,
        row_b,
        sds((3, D, D), BF16),
        sds((D, D), BF16),
        sds((D, FF), BF16),
        sds((FF, D), BF16),
        sds((3, T, D), BF16),
        row_b,
        row_b,
        row_b,
        row_b,
        sds((T, FF), BF16),
        sds((2, FF // 2, T), BF16),
        sds((T, FF), BF16),
        sds((4, 4, 4, 2, 8, T), F32),
        sds((2, 3, 512, T), BF16),
        row_f,
        row_f,
        row_b,
        sds((3, T, D), BF16),
        row_b,
        sds((4, 4, 4, 2, 8, 128), F32),
        sds((2, T, T), BF16),
        sds((T, T), F32),
        sds((T, 128), jnp.int32),
        sds((T, 1), jnp.int32),
    ]
    semaphores = [(6,), (2, NEST), (2, NEST), (2, FF // T), (2, 3), (3, 2, GROUPS), (2, 4), (2, 4)]
    semaphores.append((6,))
    return call(
        layer_kernel,
        "layer",
        12 * T * D * (3 * D + FF),
        40 * MIB,
        in_specs=[smem()] * 3 + [vmem()] * 6 + [hbm()] * 6,
        out_specs=[hbm()] * 8,
        out_shape=[firsts, firsts, seconds, seconds, thirds, thirds, row_b, row_f],
        scratch_shapes=[pltpu.VMEM(s.shape, s.dtype) for s in scratch]
        + [pltpu.SemaphoreType.DMA(s) for s in semaphores],
    )(lengths, heads, order, norm_gain, inverse, ln_gain, ln_bias, router, bucket, *arrays)


def load_left(refs, at, rows, order, axis, left, sem):
    return [
        load(
            ref.at[pl.ds(pl.multiple_of(at + rows * order[axis, i], rows), rows), :],
            left.at[pl.ds(rows * i, rows), pl.ds(T * m, T)],
            sem.at[i, m],
        )
        for i in range(4)
        for m, ref in enumerate(refs)
    ]


def load_right(refs, at, right, sem):
    return [
        load(
            ref.at[pl.ds(at + T * q, T), :],
            right.at[pl.ds(T * m, T), pl.ds(T * q, T)],
            sem.at[m, q],
        )
        for m, ref in enumerate(refs)
        for q in range(D // T)
    ]


def wait(copies):
    for copy in copies:
        copy.wait()


def store_out(out, rows, at, sent, kept, sem):
    return [
        load(out.at[pl.ds(2 * side, 2), rows, at], ref.at[:, rows, at], sem.at[side])
        for side, ref in enumerate((sent, kept))
    ]


def down_grad_kernel(
    order, one, two, sent, kept, act, merged, gb, ga, out, act_sem, merged_sem, gb_sem, ga_sem, sem
):
    refs = (one, two)
    gb_loads = load_right(refs, FF // 2, gb, gb_sem)
    act_loads = load_left(refs, 0, 512, order, 0, act, act_sem)
    merged_loads = load_left(refs, FF // 2 + 2 * D, 128, order, 0, merged, merged_sem)
    ga_loads = load_right(refs, FF // 2 + D, ga, ga_sem)
    stores = []
    wait(gb_loads)
    wide = pl.ds(0, D)
    for i in range(4):
        wait(act_loads[2 * i : 2 * i + 2])
        out[i, :, wide] = nn(act[pl.ds(512 * i, 512), :], gb[...]).astype(BF16)
        if i % 2 == 1:
            ref = (sent, kept)[i // 2]
            src = out.at[pl.ds(i - 1, 2), :, wide]
            stores.append(load(src, ref.at[:, :, wide], sem.at[0, i // 2]))
    wait(merged_loads + ga_loads)
    part = nn(merged[...], ga[...])
    more = pl.ds(D, T)
    for i in range(4):
        rows = part[128 * i : 128 * i + 128].reshape(16, 8, D)
        quarters = [rows[:, :, T * q : T * q + T] for q in range(4)]
        out[i, :, more] = jnp.concatenate(quarters, 1).reshape(512, T).astype(BF16)
    stores += store_out(out, pl.ds(0, 512), more, sent, kept, sem.at[1])
    wait(stores)


def down_grads(order, one, two):
    part = sds((2, 512, D + T), BF16)
    return call(
        down_grad_kernel,
        "down_and_out_grad",
        2 * T * D * (FF + D),
        10 * MIB,
        in_specs=[smem()] + [hbm()] * 2,
        out_specs=[hbm()] * 2,
        out_shape=[part, part],
        scratch_shapes=[
            pltpu.VMEM((FF // 2, 2 * T), BF16),
            pltpu.VMEM((512, 2 * T), BF16),
            pltpu.VMEM((2 * T, D), BF16),
            pltpu.VMEM((2 * T, D), BF16),
            pltpu.VMEM((4, 512, D + T), BF16),
            pltpu.SemaphoreType.DMA((4, 2)),
            pltpu.SemaphoreType.DMA((4, 2)),
            pltpu.SemaphoreType.DMA((2, 4)),
            pltpu.SemaphoreType.DMA((2, 4)),
            pltpu.SemaphoreType.DMA((2, 2)),
        ],
    )(order, one, two)


def wide_kernel(axis, parts, order, one, two, after, sent, kept, left, right, lines, out, *sems):
    left_sem, right_sem, line_sem, sem = sems
    refs = (one, two)
    loads = load_left(refs, parts * D, 128, order, axis, left, left_sem)
    rights = [load_right(refs, n * D, right.at[n], right_sem.at[n]) for n in range(parts)]
    line_loads = []
    if axis == 2:
        for i in range(4):
            block = order[axis, i]
            rows = pl.ds(pl.multiple_of(parts * D + 512 + 128 * (block % 2), 128), 128)
            at = pl.ds(pl.multiple_of(128 * (block // 2), 128), 128)
            for m, ref in enumerate(refs):
                line_loads.append(load(ref.at[rows, at], lines.at[i, m], line_sem.at[i, m]))
    stores = []
    wait(loads)
    every = pl.ds(0, 128)
    for n in range(parts):
        wait(rights[n])
        at = pl.ds(n * D, D)
        out[:, :, at] = nn(left[...], right[n]).astype(BF16).reshape(4, 128, D)
        stores += store_out(out, every, at, sent, kept, sem.at[n])
    if axis == 2:
        wait(line_loads)
        at = pl.ds(parts * D, 128)
        out[:, :, at] = (lines[:, 0].astype(F32) + lines[:, 1].astype(F32)).astype(BF16)
        stores += store_out(out, every, at, sent, kept, sem.at[parts])
    wait(stores)


def wide_grads(name, axis, parts, order, one, two, after):
    width = parts * D + (128 if axis == 2 else 0)
    part = sds((2, 128, width), BF16)
    return call(
        functools.partial(wide_kernel, axis, parts),
        name,
        2 * T * D * D * parts,
        9 * MIB,
        in_specs=[smem()] + [hbm()] * 3,
        out_specs=[hbm()] * 2,
        out_shape=[part, part],
        scratch_shapes=[
            pltpu.VMEM((512, 2 * T), BF16),
            pltpu.VMEM((parts, 2 * T, D), BF16),
            pltpu.VMEM((4, 2, 128, 128), BF16),
            pltpu.VMEM((4, 128, width), BF16),
            pltpu.SemaphoreType.DMA((4, 2)),
            pltpu.SemaphoreType.DMA((parts, 2, 4)),
            pltpu.SemaphoreType.DMA((4, 2)),
            pltpu.SemaphoreType.DMA((parts + 1, 2)),
        ],
    )(order, one, two, after)


def swap_cores(array):
    return lax.ppermute(array, "c", [(0, 1), (1, 0)])


def pairs(mask_0, mask_1):
    perm = []
    for p in range(4):
        perm.append((2 * p, 2 * (p ^ mask_0)))
        perm.append((2 * p + 1, 2 * (p ^ mask_1) + 1))
    return perm


def pick(array, index, dim):
    return lax.dynamic_index_in_dim(array, index, dim, keepdims=False)


def block_order(axis):
    p = lax.axis_index(axis)
    core = lax.axis_index("c")
    return [p ^ (1 + 2 * core), p ^ 2, p, p ^ (3 - 2 * core)]


def ordered(token, *arrays):
    return lax.optimization_barrier((*arrays, token))[:-1]


def chain(sent, kept, axes, shape, done):
    left = [axis for axis in ("y", "x", "z") if axis != axes[0]]
    for axis in axes:
        got = lax.ppermute(sent, (axis, "c"), pairs(1, 3))
        token = yield sent
        got, kept = ordered(token, got, kept)
        more = (got[1].astype(F32) + kept[1].astype(F32)).astype(BF16)
        got_2 = lax.ppermute(more, (axis, "c"), pairs(3, 1))
        token = yield more
        got, kept, got_2 = ordered(token, got, kept, got_2)
        terms = [a.reshape(shape).astype(F32) for a in (got[0], kept[0], got_2)]
        if not left:
            done.append(sum(terms))
            return
        following = axes[axes.index(axis) + 1]
        dim = left.index(following)
        left.pop(dim)
        shape = shape[:dim] + shape[dim + 1 :]
        first, across, own, second = [
            sum(pick(term, at, dim) for term in terms) for at in block_order(following)
        ]
        sent = jnp.stack([first, across]).astype(BF16)
        kept = jnp.stack([own, second])


def take_turns(token, *chains):
    for steps in chains:
        next(steps)
    running = list(chains)
    while running:
        for steps in list(running):
            try:
                token = steps.send(token)
            except StopIteration:
                running.remove(steps)


def body(
    tokens,
    norm_gain,
    qkv_weight,
    out_weight,
    ln_gain,
    ln_bias,
    up_weight,
    down_weight,
    buckets,
    router_prob,
    heads_active,
    doc_lengths,
    cotangent,
):
    core = lax.axis_index("c")
    orders = jnp.stack([jnp.stack(block_order(axis) + [core]) for axis in ("y", "x", "z")])
    orders = orders.astype(jnp.int32)
    norm_gain, ln_gain, ln_bias = [v.reshape(1, D) for v in (norm_gain, ln_gain, ln_bias)]
    router = router_prob.reshape(1, T)
    levels = buckets.reshape(1, T)
    inverse = np.tile(10000.0 ** (-2.0 * np.arange(HD // 2) / HD), 4).reshape(1, 128)
    inverse = jnp.asarray(inverse, F32)

    first, first_other, second, second_other, third, third_other, mixed, input_grad = layer(
        doc_lengths,
        heads_active,
        orders,
        norm_gain,
        inverse,
        ln_gain,
        ln_bias,
        router,
        levels,
        tokens,
        cotangent,
        qkv_weight,
        out_weight,
        up_weight,
        down_weight,
    )
    first_2 = swap_cores(first_other)
    (second_other,) = ordered(first_2, second_other)
    second_2 = swap_cores(second_other)
    (third_other,) = ordered(second_2, third_other)
    third_2 = swap_cores(third_other)
    down_sent, down_kept = down_grads(orders, first, first_2)
    up_sent, up_kept = wide_grads("up_grad", 1, 4, orders, second, second_2, down_sent)
    qkv_sent, qkv_kept = wide_grads("qkv_grad", 2, 3, orders, third, third_2, up_sent)

    down, up, qkv = [], [], []
    take_turns(
        qkv_sent,
        chain(down_sent, down_kept, "yxz", (4, 4, 32, D + T), down),
        chain(up_sent, up_kept, "xyz", (4, 4, 8, FF), up),
        chain(qkv_sent, qkv_kept, "zyx", (4, 4, 8, 3 * D + 128), qkv),
    )
    (down,), (up_grad,), (qkv,) = down, up, qkv
    down_grad = down[:, :D]
    out_grad = down[:, D:].reshape(4, 8, T).transpose(1, 0, 2).reshape(8, D)
    qkv_grad, line = qkv[:, : 3 * D], qkv[:, 3 * D :]
    bits = line[0, 3 : 3 + BITS * NEST].astype(jnp.int32).reshape(NEST, BITS)
    totals = jnp.sum(bits << jnp.arange(BITS, dtype=jnp.int32)[None, :], 1)
    return (
        mixed,
        input_grad,
        line[:, 0],
        qkv_grad,
        out_grad,
        line[:, 1],
        line[:, 2],
        up_grad,
        down_grad,
        totals,
    )


def solution(mesh):
    finer = Mesh(mesh.devices.reshape(4, 4, 4, 2), AX)
    rows = P(AX, None)
    return jax.shard_map(
        body,
        mesh=finer,
        in_specs=(rows, P(), P(), P(), P(), P(), P(), P(), rows, P(AX), rows, rows, rows),
        out_specs=(rows, rows, P(AX), rows, rows, P(AX), P(AX), rows, rows, P()),
        check_vma=False,
    )
```

```python
import jax
import jax.numpy as jnp
import numpy as np
from jax import lax
from jax.experimental import pallas as pl
from jax.experimental.pallas import tpu as pltpu
from jax.sharding import Mesh
from jax.sharding import PartitionSpec as P

HD = 64
NEST = 4
AX = ("y", "x", "z", "c")

NEG = -1e30
EPS = 1e-05
F32 = jnp.float32
BF16 = jnp.bfloat16
T = 256
D = 1024
FF = 4096
GW = 256
GROUPS = D // GW
ACT, GB, GA, MERGED, FIRST = 0, 512, 768, 1024, 1152
GP, ZED, NORMED, SECOND = 0, 1024, 1152, 1280
GQKV, LINES, THIRD = 0, 768, 896
BITS = 9
MIB = 1024 * 1024


def nn(a, b):
    return lax.dot_general(a, b, (((1,), (0,)), ((), ())), preferred_element_type=F32)


def nt(a, b):
    return lax.dot_general(a, b, (((1,), (1,)), ((), ())), preferred_element_type=F32)


def tn(a, b):
    return lax.dot_general(a, b, (((0,), (0,)), ((), ())), preferred_element_type=F32)


def sds(shape, dtype):
    return jax.ShapeDtypeStruct(shape, dtype)


def smem():
    return pl.BlockSpec(memory_space=pltpu.SMEM)


def vmem():
    return pl.BlockSpec(memory_space=pltpu.VMEM)


def hbm():
    return pl.BlockSpec(memory_space=pltpu.HBM)


def call(kernel, name, flops, moved, room, anywhere=False, **kw):
    def in_hbm(spec):
        return spec.memory_space == pltpu.HBM

    kw["out_shape"] = [
        pltpu.HBM(s.shape, s.dtype) if in_hbm(spec) else s
        for s, spec in zip(kw["out_shape"], kw["out_specs"])
    ]
    run = pl.pallas_call(
        kernel,
        name=name,
        compiler_params=pltpu.CompilerParams(vmem_limit_bytes=room * MIB),
        cost_estimate=pl.CostEstimate(flops=flops, bytes_accessed=moved, transcendentals=0),
        **kw,
    )

    def placed(*args):
        return run(
            *(
                pltpu.with_memory_space_constraint(arg, pltpu.HBM)
                if in_hbm(spec) and not anywhere
                else arg
                for arg, spec in zip(args, kw["in_specs"])
            )
        )

    return placed


def first_halves():
    return lax.broadcasted_iota(jnp.int32, (T, 128), 1) % HD < HD // 2


def low_heads():
    return lax.broadcasted_iota(jnp.int32, (T, 128), 1) < HD


def turned(x, cosine, sine, first):
    parts = []
    for at in range(0, x.shape[1], 128):
        part = x[:, at : at + 128]
        other = jnp.where(first, pltpu.roll(part, 128 - HD // 2, 1), pltpu.roll(part, HD // 2, 1))
        parts.append(part * cosine + other * sine)
    return jnp.concatenate(parts, 1)


def doc_start(lengths, place):
    end_0 = lengths[0, 0]
    end_1 = end_0 + lengths[0, 1]
    return jnp.where(place >= end_1, end_1, jnp.where(place >= end_0, end_0, 0))


def of_doc(lengths, place, values):
    end_0 = lengths[0, 0]
    end_1 = end_0 + lengths[0, 1]
    return jnp.where(
        place >= end_1, values[0, 2], jnp.where(place >= end_0, values[0, 1], values[0, 0])
    )


def normalized(middle):
    shifted = middle - jnp.mean(middle, -1, keepdims=True)
    rstd = lax.rsqrt(jnp.mean(shifted * shifted, -1, keepdims=True) + EPS)
    return shifted * rstd, rstd


def load(src, dst, sem):
    copy = pltpu.make_async_copy(src, dst, sem)
    copy.start()
    return copy


def columns(j, size):
    if isinstance(j, int):
        return pl.ds(j * size, size)
    return pl.ds(pl.multiple_of(j * size, size), size)


def upright(row):
    return jnp.broadcast_to(row, (8, T)).T[:, :1]


def places():
    return lax.broadcasted_iota(jnp.int32, (T, 128), 0)


def rotary(lengths, inverse):
    phase = (places() - doc_start(lengths, places())).astype(F32) * inverse[...]
    sine = jnp.sin(phase)
    return jnp.cos(phase), jnp.where(first_halves(), -sine, sine)


def store_both(src, refs, at, sem):
    return [pltpu.make_async_copy(src, ref.at[at], sem.at[side]) for side, ref in enumerate(refs)]


def start(copies):
    for copy in copies:
        copy.start()


def wait(copies):
    for copy in copies:
        copy.wait()


def front_kernel(
    lengths,
    heads,
    order,
    norm_gain,
    inverse,
    ln_gain,
    ln_bias,
    router,
    bucket,
    tokens_hbm,
    cot_hbm,
    wqkv_hbm,
    wo_hbm,
    up_hbm,
    down_hbm,
    parts,
    first_mine,
    first_other,
    second_mine,
    second_other,
    qkv_out,
    grad_mid_out,
    mixed_out,
    tokens,
    cot,
    wqkv,
    wo,
    up,
    down,
    qkv,
    normed,
    merged,
    zed,
    gb,
    act,
    act_turned,
    gp,
    turned_f,
    left,
    middle,
    grad_mid,
    ga,
    mixed,
    bias,
    active,
    level,
    in_sem,
    ffn_sem,
    act_sem,
    gp_sem,
    left_sem,
    gb_sem,
    ga_sem,
    out_sem,
):
    core = order[0, 4]
    firsts, seconds = (first_mine, first_other), (second_mine, second_other)
    loads = [load(tokens_hbm, tokens, in_sem.at[0])]
    for n in range(3):
        loads.append(load(wqkv_hbm.at[:, n * D : (n + 1) * D], wqkv.at[n], in_sem.at[1 + n]))

    def ffn_loads(j):
        at = columns(j, D)
        return (
            pltpu.make_async_copy(up_hbm.at[:, at], up.at[:, at], ffn_sem.at[0, j]),
            pltpu.make_async_copy(down_hbm.at[at, :], down.at[at, :], ffn_sem.at[1, j]),
        )

    stores = []

    def store_left(n, value, axis, refs, at):
        turned_f[...] = value.astype(F32).T.reshape(turned_f.shape)
        for side, ref in enumerate(refs):
            half = core if side == 0 else 1 - core
            for i in range(4):
                if axis == 0:
                    rows = turned_f[i, :, :, half]
                elif axis == 1:
                    rows = turned_f[:, i, :, half]
                else:
                    rows = turned_f[:, :, i, half]
                left[side, n, :, pl.ds(T * i, T)] = rows.reshape(128, T).astype(BF16)
            dst = ref.at[pl.ds(at, 128), :]
            stores.append(load(left.at[side, n], dst, left_sem.at[side, n]))

    first = first_halves()
    low = low_heads()
    zero = jnp.zeros((T, 128), BF16)
    scale = HD**-0.5
    cosine, sine = rotary(lengths, inverse)
    row = lax.broadcasted_iota(jnp.int32, (T, T), 0)
    col = lax.broadcasted_iota(jnp.int32, (T, T), 1)
    bias[...] = jnp.where((col >= doc_start(lengths, row)) & (col <= row), 0.0, NEG)
    active[...] = of_doc(lengths, places(), heads)
    level[...] = upright(bucket[...])
    prob = upright(router[...])

    loads[0].wait()
    resid = tokens[...].astype(F32)
    rscale = lax.rsqrt(jnp.mean(resid * resid, -1, keepdims=True) + EPS)
    normed[...] = (resid * rscale * norm_gain[...]).astype(BF16)
    for n in range(3):
        loads[1 + n].wait()
        if n == 1:
            loads.append(load(cot_hbm, cot, in_sem.at[4]))
        if n == 2:
            loads.append(load(wo_hbm, wo, in_sem.at[5]))
            for copy in ffn_loads(0) + ffn_loads(1):
                copy.start()
        part = nn(normed[...], wqkv[n])
        qkv[n] = (turned(part, cosine, sine, first) if n < 2 else part).astype(BF16)
    stores.append(load(qkv, qkv_out, out_sem.at[0]))

    def attend(g, carry):
        for pair in range(2):
            lanes = pl.ds(pl.multiple_of(g * GW + 128 * pair, 128), 128)
            qp, kp, vp = qkv[0, :, lanes], qkv[1, :, lanes], qkv[2, :, lanes]
            out = jnp.zeros((T, 128), F32)
            for side in range(2):
                keep = low if side == 0 else ~low
                s = nt(qp, jnp.where(keep, kp, zero)) * scale + bias[...]
                e = jnp.exp(s - jnp.max(s, -1, keepdims=True))
                p = (e / jnp.sum(e, -1, keepdims=True)).astype(BF16)
                out = out + nn(p, jnp.where(keep, vp, zero))
            head = 4 * g + 2 * pair + jnp.where(low, 0, 1)
            merged[:, lanes] = jnp.where(head < active[...], out, 0.0).astype(BF16)

        @pl.when((g > 0) & (g < NEST - 1))
        def _():
            for copy in ffn_loads(g + 1):
                copy.start()

        return carry

    lax.fori_loop(0, GROUPS, attend, 0)
    loads[5].wait()
    middle[...] = tokens[...].astype(F32) + nn(merged[...], wo[...])
    normed_mid, _ = normalized(middle[...])
    zed[...] = (normed_mid * ln_gain[...] + ln_bias[...]).astype(BF16)
    loads[4].wait()
    gb[...] = (cot[...].astype(F32) * prob).astype(BF16)
    both_gb = store_both(gb, firsts, (pl.ds(GB, T), slice(None)), gb_sem)
    for copy in both_gb:
        copy.start()

    def act_stores(j):
        at = (pl.ds(ACT, 512), columns(j, T))
        return [
            pltpu.make_async_copy(act_turned.at[side, :, at[1]], ref.at[at], act_sem.at[side, j])
            for side, ref in enumerate(firsts)
        ]

    def gp_stores(j):
        rows = pl.ds(pl.multiple_of(GP + T * j, T), T)
        return store_both(gp.at[:, columns(j, D)], seconds, (rows, slice(None)), gp_sem.at[j])

    def hidden(j, carry):
        copy_up, copy_down = ffn_loads(j)
        at = columns(j, D)
        copy_up.wait()
        r = jnp.where(level[...] >= j, jnp.maximum(nn(zed[...], up[:, at]), 0.0), 0.0)
        a = (r * r).astype(BF16)
        act[:, at] = a
        by_core = a.T.reshape(16, 2, 32, T)
        low_rows, high_rows = by_core[:, 0].reshape(512, T), by_core[:, 1].reshape(512, T)
        act_turned[0, :, columns(j, T)] = jnp.where(core == 0, low_rows, high_rows)
        act_turned[1, :, columns(j, T)] = jnp.where(core == 0, high_rows, low_rows)
        for copy in act_stores(j):
            copy.start()
        copy_down.wait()
        gp[:, at] = (nt(gb[...], down[at, :]) * 2.0 * r).astype(BF16)
        for copy in gp_stores(j):
            copy.start()
        return carry

    lax.fori_loop(0, NEST, hidden, 0)
    store_left(0, zed[...], 1, seconds, ZED)
    store_left(1, normed[...], 2, seconds, NORMED)
    store_left(2, merged[...], 0, firsts, MERGED)

    branch = nn(act[...], down[...]).astype(BF16).astype(F32)
    mid = middle[...]
    mixed[...] = (mid + prob * branch).astype(BF16)
    stores.append(load(mixed, mixed_out, out_sem.at[1]))
    grad_zed = nt(gp[...], up[...]).astype(BF16).astype(F32)
    normed_mid, rstd = normalized(mid)
    parts[0:1, :] = jnp.sum(grad_zed * normed_mid, 0, keepdims=True)
    parts[1:2, :] = jnp.sum(grad_zed, 0, keepdims=True)
    grad_norm = grad_zed * ln_gain[...]
    grad = cot[...].astype(F32) + rstd * (
        grad_norm
        - jnp.mean(grad_norm, -1, keepdims=True)
        - normed_mid * jnp.mean(grad_norm * normed_mid, -1, keepdims=True)
    )
    ga[...] = grad.astype(BF16)
    both_ga = store_both(ga, firsts, (pl.ds(GA, T), slice(None)), ga_sem)
    for copy in both_ga:
        copy.start()
    grad_mid[...] = grad
    stores.append(load(grad_mid, grad_mid_out, out_sem.at[2]))
    for j in range(NEST):
        wait(act_stores(j) + gp_stores(j))
    wait(both_gb + both_ga + stores)


def front(lengths, heads, order, norm_gain, inverse, ln_gain, ln_bias, router, bucket, *arrays):
    firsts = sds((FIRST, D), BF16)
    seconds = sds((SECOND, D), BF16)
    row_b = sds((T, D), BF16)
    row_f = sds((T, D), F32)
    scratch = [
        row_b,
        row_b,
        sds((3, D, D), BF16),
        sds((D, D), BF16),
        sds((D, FF), BF16),
        sds((FF, D), BF16),
        sds((3, T, D), BF16),
        row_b,
        row_b,
        row_b,
        row_b,
        sds((T, FF), BF16),
        sds((2, 512, D), BF16),
        sds((T, FF), BF16),
        sds((4, 4, 4, 2, 8, T), F32),
        sds((2, 3, 128, D), BF16),
        row_f,
        row_f,
        row_b,
        row_b,
        sds((T, T), F32),
        sds((T, 128), jnp.int32),
        sds((T, 1), jnp.int32),
    ]
    semaphores = [(6,), (2, NEST), (2, NEST), (NEST, 2), (2, 3), (2,), (2,), (3,)]
    return call(
        front_kernel,
        "front",
        2 * T * D * (4 * D + 4 * FF),
        40 * MIB,
        58,
        in_specs=[smem()] * 3 + [vmem()] * 6 + [hbm()] * 6,
        out_specs=[vmem()] + [hbm()] * 7,
        out_shape=[sds((8, D), F32), firsts, firsts, seconds, seconds, sds((3, T, D), BF16)]
        + [row_f, row_b],
        scratch_shapes=[pltpu.VMEM(s.shape, s.dtype) for s in scratch]
        + [pltpu.SemaphoreType.DMA(s) for s in semaphores],
    )(lengths, heads, order, norm_gain, inverse, ln_gain, ln_bias, router, bucket, *arrays)


def back_kernel(
    lengths,
    heads,
    order,
    norm_gain,
    inverse,
    bucket,
    parts,
    first_mine,
    qkv_hbm,
    grad_mid_hbm,
    tokens_hbm,
    wqkv_hbm,
    wo_hbm,
    third_mine,
    third_other,
    input_grad_out,
    ga,
    qkv,
    grad_mid,
    tokens,
    wqkv,
    wo,
    gqkv,
    lines_f,
    lines,
    bias,
    active,
    in_sem,
    w_sem,
    group_sem,
    out_sem,
):
    core = order[0, 4]
    thirds = (third_mine, third_other)
    loads = [
        load(first_mine.at[pl.ds(GA, T), :], ga, in_sem.at[0]),
        load(wo_hbm.at[pl.ds(0, GW), :], wo.at[pl.ds(0, GW), :], in_sem.at[1]),
        load(qkv_hbm.at[:, :, pl.ds(0, GW)], qkv.at[:, :, pl.ds(0, GW)], in_sem.at[2]),
    ]
    others = pl.ds(GW, D - GW)
    more = [
        pltpu.make_async_copy(wo_hbm.at[others, :], wo.at[others, :], in_sem.at[5]),
        pltpu.make_async_copy(qkv_hbm.at[:, :, others], qkv.at[:, :, others], in_sem.at[6]),
    ]
    late = [
        pltpu.make_async_copy(tokens_hbm, tokens, in_sem.at[3]),
        pltpu.make_async_copy(grad_mid_hbm, grad_mid, in_sem.at[4]),
    ]
    for n in range(3):
        src = wqkv_hbm.at[:, n * D : (n + 1) * D]
        late.append(pltpu.make_async_copy(src, wqkv.at[n], w_sem.at[n]))

    first = first_halves()
    low = low_heads()
    zero = jnp.zeros((T, 128), BF16)
    scale = HD**-0.5
    cosine, sine = rotary(lengths, inverse)
    sine = -sine
    query = lax.broadcasted_iota(jnp.int32, (T, T), 1)
    key = lax.broadcasted_iota(jnp.int32, (T, T), 0)
    bias[...] = jnp.where((key >= doc_start(lengths, query)) & (key <= query), 0.0, NEG)
    active[...] = of_doc(lengths, places(), heads)
    wait(loads)
    for copy in more:
        copy.start()

    def group_stores(g):
        at = columns(g, GW)
        return [
            copy
            for n in range(3)
            for copy in store_both(
                gqkv.at[n, :, at], thirds, (pl.ds(GQKV + T * n, T), at), group_sem.at[n, g]
            )
        ]

    def attend_back(g, carry):
        @pl.when(g == 1)
        def _():
            wait(more)
            start(late)

        grad_merged = nt(ga[...], wo[columns(g, GW), :])
        for pair in range(2):
            lanes = pl.ds(pl.multiple_of(g * GW + 128 * pair, 128), 128)
            head = 4 * g + 2 * pair + jnp.where(low, 0, 1)
            gm = grad_merged[:, 128 * pair : 128 * pair + 128]
            gm = jnp.where(head < active[...], gm, 0.0).astype(BF16)
            qp, kp, vp = qkv[0, :, lanes], qkv[1, :, lanes], qkv[2, :, lanes]
            k_turned = kp.T
            grad_values = jnp.zeros((T, 128), F32)
            grad_keys = jnp.zeros((T, 128), F32)
            grad_query = []
            for side in range(2):
                keep = low if side == 0 else ~low
                q_head = jnp.where(keep, qp, zero)
                gm_head = jnp.where(keep, gm, zero)
                s = nt(kp, q_head) * scale + bias[...]
                e = jnp.exp(s - jnp.max(s, 0, keepdims=True))
                p = e / jnp.sum(e, 0, keepdims=True)
                grad_p = nt(vp, gm_head)
                grad_values = grad_values + nn(p.astype(BF16), gm_head)
                grad_s = (p * (grad_p - jnp.sum(p * grad_p, 0, keepdims=True))).astype(BF16)
                grad_keys = grad_keys + nn(grad_s, q_head)
                grad_query.append(nn(k_turned[HD * side : HD * side + HD], grad_s))
            grad_q = jnp.concatenate(grad_query, 0).T * scale
            gqkv[0, :, lanes] = turned(grad_q, cosine, sine, first).astype(BF16)
            gqkv[1, :, lanes] = turned(grad_keys * scale, cosine, sine, first).astype(BF16)
            gqkv[2, :, lanes] = grad_values.astype(BF16)
        for copy in group_stores(g):
            copy.start()
        return carry

    lax.fori_loop(0, GROUPS, attend_back, 0)

    wait(late)
    grad_normed = nt(gqkv[0], wqkv[0]) + nt(gqkv[1], wqkv[1]) + nt(gqkv[2], wqkv[2])
    resid = tokens[...].astype(F32)
    rscale = lax.rsqrt(jnp.mean(resid * resid, -1, keepdims=True) + EPS)
    unit = resid * rscale
    gain_part = jnp.sum(grad_normed * unit, 0, keepdims=True)
    grad_unit = grad_normed * norm_gain[...]
    grad_mid[...] += rscale * (
        grad_unit - unit * jnp.mean(grad_unit * unit, -1, keepdims=True)
    )
    stores = [load(grad_mid, input_grad_out, out_sem.at[0])]

    item = lax.broadcasted_iota(jnp.int32, (128, 1), 0)
    count = jnp.zeros((128, 1), jnp.int32)
    for n in range(NEST):
        total = jnp.sum((bucket[...] == n).astype(jnp.int32), 1, keepdims=True)
        at = item - 3 - BITS * n
        bit = lax.shift_right_logical(total, jnp.clip(at, 0, BITS - 1)) & 1
        count = jnp.where((at >= 0) & (at < BITS), bit, count)
    wide = jnp.where(item == 0, gain_part, jnp.where(item == 1, parts[0:1, :], parts[1:2, :]))
    lines_f[...] = jnp.where(item < 3, wide, count.astype(F32)).T.reshape(lines_f.shape)
    for side, ref in enumerate(thirds):
        half = core if side == 0 else 1 - core
        for i in range(4):
            part = lines_f[:, i, :, half].reshape(128, 128).astype(BF16)
            lines[side, :, pl.ds(128 * i, 128)] = part
        dst = ref.at[pl.ds(LINES, 128), pl.ds(0, 512)]
        stores.append(load(lines.at[side], dst, out_sem.at[1 + side]))
    for g in range(GROUPS):
        wait(group_stores(g))
    wait(stores)


def back(lengths, heads, order, norm_gain, inverse, bucket, parts, *arrays):
    thirds = sds((THIRD, D), BF16)
    scratch = [
        sds((T, D), BF16),
        sds((3, T, D), BF16),
        sds((T, D), F32),
        sds((T, D), BF16),
        sds((3, D, D), BF16),
        sds((D, D), BF16),
        sds((3, T, D), BF16),
        sds((4, 4, 4, 2, 8, 128), F32),
        sds((2, 128, 512), BF16),
        sds((T, T), F32),
        sds((T, 128), jnp.int32),
    ]
    return call(
        back_kernel,
        "back",
        2 * T * D * 4 * D + 10 * 16 * T * T * 256,
        18 * MIB,
        32,
        in_specs=[smem()] * 3 + [vmem()] * 4 + [hbm()] * 6,
        out_specs=[hbm()] * 3,
        out_shape=[thirds, thirds, sds((T, D), F32)],
        scratch_shapes=[pltpu.VMEM(s.shape, s.dtype) for s in scratch]
        + [pltpu.SemaphoreType.DMA(s) for s in [(7,), (3,), (3, GROUPS, 2), (3,)]],
    )(lengths, heads, order, norm_gain, inverse, bucket, parts, *arrays)


def load_left(refs, at, rows, order, axis, left, sem):
    return [
        pltpu.make_async_copy(
            ref.at[pl.ds(at, rows), columns(order[axis, i], T)],
            left.at[pl.ds(rows * i, rows), pl.ds(T * m, T)],
            sem.at[i, m],
        )
        for i in range(4)
        for m, ref in enumerate(refs)
    ]


def load_right(refs, at, right, sem):
    return [
        pltpu.make_async_copy(ref.at[pl.ds(at, T), :], right.at[pl.ds(T * m, T), :], sem.at[m])
        for m, ref in enumerate(refs)
    ]


def store_out(out, at, sent, kept, sem):
    return [
        load(out.at[pl.ds(2 * side, 2), :, at], ref.at[:, :, at], sem.at[side])
        for side, ref in enumerate((sent, kept))
    ]


def down_grad_kernel(
    order, one, two, sent, kept, act, merged, gb, ga, out, act_sem, merged_sem, gb_sem, ga_sem, sem
):
    refs = (one, two)
    gb_loads = load_right(refs, GB, gb, gb_sem)
    act_loads = load_left(refs, ACT, 512, order, 0, act, act_sem)
    ga_loads = load_right(refs, GA, ga, ga_sem)
    merged_loads = load_left(refs, MERGED, 128, order, 0, merged, merged_sem)
    stages = [gb_loads + act_loads[:2], act_loads[2:4], act_loads[4:6], act_loads[6:]]
    stages.append(ga_loads + merged_loads)
    stores = []
    start(stages[0] + stages[1])
    wide = pl.ds(0, D)
    for i in range(4):
        wait(stages[i])
        start(stages[i + 2] if i < 3 else [])
        out[i, :, wide] = nn(act[pl.ds(512 * i, 512), :], gb[...]).astype(BF16)
        dst = (sent, kept)[i // 2].at[i % 2, :, wide]
        stores.append(load(out.at[i, :, wide], dst, sem.at[0, i]))
    wait(stages[4])
    part = nn(merged[...], ga[...])
    more = pl.ds(D, T)
    for i in range(4):
        rows = part[128 * i : 128 * i + 128].reshape(16, 8, D)
        quarters = [rows[:, :, T * q : T * q + T] for q in range(4)]
        out[i, :, more] = jnp.concatenate(quarters, 1).reshape(512, T).astype(BF16)
    stores += store_out(out, more, sent, kept, sem.at[1])
    wait(stores)


def down_grads(order, one, two):
    part = sds((2, 512, D + T), BF16)
    return call(
        down_grad_kernel,
        "down_and_out_grad",
        2 * T * D * (FF + D),
        10 * MIB,
        24,
        True,
        in_specs=[smem()] + [hbm()] * 2,
        out_specs=[hbm()] * 2,
        out_shape=[part, part],
        scratch_shapes=[
            pltpu.VMEM((FF // 2, 2 * T), BF16),
            pltpu.VMEM((512, 2 * T), BF16),
            pltpu.VMEM((2 * T, D), BF16),
            pltpu.VMEM((2 * T, D), BF16),
            pltpu.VMEM((4, 512, D + T), BF16),
            pltpu.SemaphoreType.DMA((4, 2)),
            pltpu.SemaphoreType.DMA((4, 2)),
            pltpu.SemaphoreType.DMA((2,)),
            pltpu.SemaphoreType.DMA((2,)),
            pltpu.SemaphoreType.DMA((2, 4)),
        ],
    )(order, one, two)


def up_and_qkv_kernel(
    order,
    one,
    two,
    three,
    four,
    after,
    up_sent,
    up_kept,
    qkv_sent,
    qkv_kept,
    zed,
    normed,
    gp,
    gqkv,
    lines,
    up_out,
    qkv_out,
    zed_sem,
    normed_sem,
    gp_sem,
    gqkv_sem,
    line_sem,
    up_sem,
    qkv_sem,
):
    refs = (one, two)
    late = (three, four)
    zed_loads = load_left(refs, ZED, 128, order, 1, zed, zed_sem)
    gp_loads = [load_right(refs, GP + T * n, gp.at[n], gp_sem.at[n]) for n in range(4)]
    line_loads = [
        pltpu.make_async_copy(
            ref.at[pl.ds(LINES, 128), columns(order[1, i], 128)],
            lines.at[i, m],
            line_sem.at[i, m],
        )
        for i in range(4)
        for m, ref in enumerate(late)
    ]
    normed_loads = load_left(refs, NORMED, 128, order, 2, normed, normed_sem)
    gqkv_loads = [load_right(late, GQKV + T * n, gqkv.at[n], gqkv_sem.at[n]) for n in range(3)]
    stages = [zed_loads + gp_loads[0], *gp_loads[1:], normed_loads + gqkv_loads[0]]
    stages += [gqkv_loads[1], gqkv_loads[2] + line_loads, []]
    stores = []
    start(stages[0] + stages[1])
    for n in range(4):
        wait(stages[n])
        start(stages[n + 2])
        at = pl.ds(n * D, D)
        up_out[:, :, at] = nn(zed[...], gp[n]).astype(BF16).reshape(4, 128, D)
        stores += store_out(up_out, at, up_sent, up_kept, up_sem.at[n])
    for n in range(3):
        wait(stages[4 + n])
        start(stages[6] if n == 0 else [])
        at = pl.ds(n * D, D)
        qkv_out[:, :, at] = nn(normed[...], gqkv[n]).astype(BF16).reshape(4, 128, D)
        stores += store_out(qkv_out, at, qkv_sent, qkv_kept, qkv_sem.at[n])
    at = pl.ds(FF, 128)
    up_out[:, :, at] = (lines[:, 0].astype(F32) + lines[:, 1].astype(F32)).astype(BF16)
    stores += store_out(up_out, at, up_sent, up_kept, up_sem.at[4])
    wait(stores)


def up_and_qkv_grads(order, one, two, three, four, after):
    up = sds((2, 128, FF + 128), BF16)
    qkv = sds((2, 128, 3 * D), BF16)
    return call(
        up_and_qkv_kernel,
        "up_and_qkv_grad",
        2 * T * D * (FF + 3 * D),
        16 * MIB,
        28,
        True,
        in_specs=[smem()] + [hbm()] * 5,
        out_specs=[hbm()] * 4,
        out_shape=[up, up, qkv, qkv],
        scratch_shapes=[
            pltpu.VMEM((512, 2 * T), BF16),
            pltpu.VMEM((512, 2 * T), BF16),
            pltpu.VMEM((4, 2 * T, D), BF16),
            pltpu.VMEM((3, 2 * T, D), BF16),
            pltpu.VMEM((4, 2, 128, 128), BF16),
            pltpu.VMEM((4, 128, FF + 128), BF16),
            pltpu.VMEM((4, 128, 3 * D), BF16),
            pltpu.SemaphoreType.DMA((4, 2)),
            pltpu.SemaphoreType.DMA((4, 2)),
            pltpu.SemaphoreType.DMA((4, 2)),
            pltpu.SemaphoreType.DMA((3, 2)),
            pltpu.SemaphoreType.DMA((4, 2)),
            pltpu.SemaphoreType.DMA((5, 2)),
            pltpu.SemaphoreType.DMA((3, 2)),
        ],
    )(order, one, two, three, four, after)


def swap_cores(array):
    return lax.ppermute(array, "c", [(0, 1), (1, 0)])


def pairs(mask_0, mask_1):
    perm = []
    for p in range(4):
        perm.append((2 * p, 2 * (p ^ mask_0)))
        perm.append((2 * p + 1, 2 * (p ^ mask_1) + 1))
    return perm


def block_order(axis):
    p = lax.axis_index(axis)
    core = lax.axis_index("c")
    return [p ^ (1 + 2 * core), p ^ 2, p, p ^ (3 - 2 * core)]


def ordered(token, *arrays):
    return lax.optimization_barrier((*arrays, token))[:-1]


def chain(sent, kept, axes, shape, finish):
    left = [axis for axis in ("y", "x", "z") if axis != axes[0]]
    for axis in axes:
        got = lax.ppermute(sent, (axis, "c"), pairs(1, 3))
        token = yield sent
        got, kept = ordered(token, got, kept)
        more = (got[1].astype(F32) + kept[1].astype(F32)).astype(BF16)
        got_2 = lax.ppermute(more, (axis, "c"), pairs(3, 1))
        token = yield more
        got, kept, got_2 = ordered(token, got, kept, got_2)
        terms = [got.reshape(2, *shape), kept.reshape(2, *shape), got_2.reshape(1, *shape)]
        if not left:
            finish(*terms)
            return
        following = axes[axes.index(axis) + 1]
        dim = left.index(following)
        left.pop(dim)
        shape = shape[:dim] + shape[dim + 1 :]

        def block(at):
            total = 0.0
            for term in terms:
                start = [0] * term.ndim
                start[1 + dim] = at
                sizes = (1,) + term.shape[1 : 1 + dim] + (1,) + term.shape[2 + dim :]
                total = total + lax.dynamic_slice(term, start, sizes).astype(F32)
            return total.reshape(shape)

        first, across, own, second = [block(at) for at in block_order(following)]
        sent = jnp.stack([first, across]).astype(BF16)
        kept = jnp.stack([own, second])


def total(terms, *at):
    return sum(term[(0, *at)].astype(F32) for term in terms)


def take_turns(token, turns, **chains):
    for steps in chains.values():
        next(steps)
    for turn in turns:
        token = next_step(chains[turn], token)


def next_step(steps, token):
    try:
        return steps.send(token)
    except StopIteration:
        return token


def body(
    tokens,
    norm_gain,
    qkv_weight,
    out_weight,
    ln_gain,
    ln_bias,
    up_weight,
    down_weight,
    buckets,
    router_prob,
    heads_active,
    doc_lengths,
    cotangent,
):
    core = lax.axis_index("c")
    orders = jnp.stack([jnp.stack(block_order(axis) + [core]) for axis in ("y", "x", "z")])
    orders = orders.astype(jnp.int32)
    norm_gain, ln_gain, ln_bias = [v.reshape(1, D) for v in (norm_gain, ln_gain, ln_bias)]
    router = router_prob.reshape(1, T)
    levels = buckets.reshape(1, T)
    inverse = np.tile(10000.0 ** (-2.0 * np.arange(HD // 2) / HD), 4).reshape(1, 128)
    inverse = jnp.asarray(inverse, F32)

    parts, first, first_other, second, second_other, qkv, grad_mid, mixed = front(
        doc_lengths,
        heads_active,
        orders,
        norm_gain,
        inverse,
        ln_gain,
        ln_bias,
        router,
        levels,
        tokens,
        cotangent,
        qkv_weight,
        out_weight,
        up_weight,
        down_weight,
    )
    first_2, second_2 = swap_cores(first_other), swap_cores(second_other)
    third, third_other, input_grad = back(
        doc_lengths,
        heads_active,
        orders,
        norm_gain,
        inverse,
        levels,
        parts,
        first,
        qkv,
        grad_mid,
        tokens,
        qkv_weight,
        out_weight,
    )
    third_2 = swap_cores(third_other)
    first_2, _ = lax.optimization_barrier((first_2, third))
    down_sent, down_kept = down_grads(orders, first, first_2)
    up_sent, up_kept, qkv_sent, qkv_kept = up_and_qkv_grads(
        orders, second, second_2, third, third_2, down_sent
    )

    every = slice(None)
    grads = {}

    def down_done(*terms):
        grads["down"] = total(terms, every, slice(0, D))
        out = total(terms, every, slice(D, D + T))
        grads["out"] = out.reshape(4, 8, T).transpose(1, 0, 2).reshape(8, D)

    def up_done(*terms):
        grads["up"] = total(terms, every, slice(0, FF))
        line = total(terms, every, slice(FF, FF + 128))
        grads["gains"] = [line[:, n] for n in range(3)]
        bits = line[0, 3 : 3 + BITS * NEST].astype(jnp.int32).reshape(NEST, BITS)
        grads["counts"] = jnp.sum(bits << jnp.arange(BITS, dtype=jnp.int32)[None, :], 1)

    def qkv_done(*terms):
        grads["qkv"] = total(terms)

    take_turns(
        qkv_sent,
        "dquqduqdqudqudqudu",
        d=chain(down_sent, down_kept, "yxz", (4, 4, 32, D + T), down_done),
        u=chain(up_sent, up_kept, "xyz", (4, 4, 8, FF + 128), up_done),
        q=chain(qkv_sent, qkv_kept, "zyx", (4, 4, 8, 3 * D), qkv_done),
    )
    gain_grad, ln_gain_grad, ln_bias_grad = grads["gains"]
    return (
        mixed,
        input_grad,
        gain_grad,
        grads["qkv"],
        grads["out"],
        ln_gain_grad,
        ln_bias_grad,
        grads["up"],
        grads["down"],
        grads["counts"],
    )


def solution(mesh):
    finer = Mesh(mesh.devices.reshape(4, 4, 4, 2), AX)
    rows = P(AX, None)
    return jax.shard_map(
        body,
        mesh=finer,
        in_specs=(rows, P(), P(), P(), P(), P(), P(), P(), rows, P(AX), rows, rows, rows),
        out_specs=(rows, rows, P(AX), rows, rows, P(AX), P(AX), rows, rows, P()),
        check_vma=False,
    )
```

```python
import jax
import jax.numpy as jnp
import numpy as np
from jax import lax
from jax.experimental import pallas as pl
from jax.experimental.pallas import tpu as pltpu
from jax.sharding import Mesh
from jax.sharding import PartitionSpec as P

HD = 64
NEST = 4
AX = ("y", "x", "z", "c")

NEG = -1e30
EPS = 1e-05
F32 = jnp.float32
BF16 = jnp.bfloat16
T = 256
D = 1024
FF = 4096
GW = 256
GROUPS = D // GW
HEADS = GW // HD
ACT, MERGED, FIRST_OWN, GB, GA, FIRST = 0, 512, 640, 640, 896, 1152
ZED, NORMED, SECOND_OWN, GP, SECOND = 0, 128, 256, 256, 1280
LINES, THIRD_OWN, GQKV, THIRD = 0, 128, 128, 896
BITS = 9
MIB = 1024 * 1024


def nn(a, b):
    return lax.dot_general(a, b, (((1,), (0,)), ((), ())), preferred_element_type=F32)


def nt(a, b):
    return lax.dot_general(a, b, (((1,), (1,)), ((), ())), preferred_element_type=F32)


def tn(a, b):
    return lax.dot_general(a, b, (((0,), (0,)), ((), ())), preferred_element_type=F32)


def sds(shape, dtype):
    return jax.ShapeDtypeStruct(shape, dtype)


def smem():
    return pl.BlockSpec(memory_space=pltpu.SMEM)


def vmem():
    return pl.BlockSpec(memory_space=pltpu.VMEM)


def hbm():
    return pl.BlockSpec(memory_space=pltpu.HBM)


def call(kernel, name, flops, moved, room, anywhere=(), **kw):
    def in_hbm(spec):
        return spec.memory_space == pltpu.HBM

    kw["out_shape"] = [
        pltpu.HBM(s.shape, s.dtype) if in_hbm(spec) else s
        for s, spec in zip(kw["out_shape"], kw["out_specs"])
    ]
    run = pl.pallas_call(
        kernel,
        name=name,
        compiler_params=pltpu.CompilerParams(vmem_limit_bytes=room * MIB),
        cost_estimate=pl.CostEstimate(flops=flops, bytes_accessed=moved, transcendentals=0),
        **kw,
    )

    def placed(*args):
        return run(
            *(
                pltpu.with_memory_space_constraint(arg, pltpu.HBM)
                if in_hbm(spec) and n not in anywhere
                else arg
                for n, (arg, spec) in enumerate(zip(args, kw["in_specs"]))
            )
        )

    return placed


def first_halves():
    return lax.broadcasted_iota(jnp.int32, (T, 128), 1) % HD < HD // 2


def head_of(g):
    return HEADS * g + lax.broadcasted_iota(jnp.int32, (T, GW), 1) // HD


def by_head(x):
    lane = lax.broadcasted_iota(jnp.int32, (T, GW), 1)
    zero = jnp.zeros((T, GW), x.dtype)
    own = [(lane >= HD * h) & (lane < HD * h + HD) for h in range(HEADS)]
    return jnp.concatenate([jnp.where(keep, x, zero) for keep in own], 0)


def turned(x, cosine, sine, first):
    parts = []
    for at in range(0, x.shape[1], 128):
        part = x[:, at : at + 128]
        other = jnp.where(first, pltpu.roll(part, 128 - HD // 2, 1), pltpu.roll(part, HD // 2, 1))
        parts.append(part * cosine + other * sine)
    return jnp.concatenate(parts, 1)


def doc_ends(lengths):
    return lengths[0, 0], lengths[0, 0] + lengths[0, 1]


def doc_start(lengths, place):
    end_0, end_1 = doc_ends(lengths)
    return jnp.where(place >= end_1, end_1, jnp.where(place >= end_0, end_0, 0))


def of_doc(lengths, place, values):
    end_0, end_1 = doc_ends(lengths)
    late = jnp.where(place >= end_1, values[0, 2], values[0, 1])
    return jnp.where(place >= end_0, late, values[0, 0])


def normalized(middle):
    shifted = middle - jnp.mean(middle, -1, keepdims=True)
    rstd = lax.rsqrt(jnp.mean(shifted * shifted, -1, keepdims=True) + EPS)
    return shifted * rstd, rstd


def block_order(axis):
    p = lax.axis_index(axis)
    core = lax.axis_index("c")
    return [p ^ (1 + 2 * core), p ^ 2, p, p ^ (3 - 2 * core)]


def load(src, dst, sem):
    copy = pltpu.make_async_copy(src, dst, sem)
    copy.start()
    return copy


def columns(j, size):
    if isinstance(j, int):
        return pl.ds(j * size, size)
    return pl.ds(pl.multiple_of(j * size, size), size)


def upright(row):
    return jnp.broadcast_to(row, (8, T)).T[:, :1]


def places():
    return lax.broadcasted_iota(jnp.int32, (T, 128), 0)


def rotary(lengths, inverse):
    phase = (places() - doc_start(lengths, places())).astype(F32) * inverse[...]
    sine = jnp.sin(phase)
    return jnp.cos(phase), jnp.where(first_halves(), -sine, sine)


def start(copies):
    for copy in copies:
        copy.start()


def wait(copies):
    for copy in copies:
        copy.wait()


def front_kernel(
    lengths,
    heads,
    norm_gain,
    inverse,
    ln_gain,
    ln_bias,
    router,
    bucket,
    tokens_hbm,
    cot_hbm,
    wqkv_hbm,
    wo_hbm,
    up_hbm,
    down_hbm,
    parts_out,
    first_mine,
    first_other,
    second_mine,
    second_other,
    qkv_out,
    mixed_out,
    parts,
    tokens,
    cot,
    wqkv,
    wo,
    up,
    down,
    qkv,
    normed,
    merged,
    zed,
    gb,
    act,
    act_turned,
    gp,
    turned_f,
    left,
    middle,
    ga,
    mixed,
    bias,
    active,
    level,
    in_sem,
    ffn_sem,
    act_sem,
    gp_sem,
    left_sem,
    out_sem,
):
    core = lax.axis_index("c")
    firsts, seconds = (first_mine, first_other), (second_mine, second_other)
    loads = [load(tokens_hbm, tokens, in_sem.at[0])]
    for n in range(3):
        src = wqkv_hbm.at[:, n * D : (n + 1) * D]
        loads.append(pltpu.make_async_copy(src, wqkv.at[n], in_sem.at[1 + n]))
    loads[1].start()

    def ffn_loads(j):
        at = columns(j, D)
        return (
            pltpu.make_async_copy(up_hbm.at[:, at], up.at[:, at], ffn_sem.at[0, j]),
            pltpu.make_async_copy(down_hbm.at[at, :], down.at[at, :], ffn_sem.at[1, j]),
        )

    stores = []

    def store_left(n, value, axis, refs, at):
        turned_f[...] = value.astype(F32).T.reshape(turned_f.shape)
        for side, ref in enumerate(refs):
            half = core if side == 0 else 1 - core
            for i in range(4):
                if axis == 0:
                    rows = turned_f[i, :, :, half]
                elif axis == 1:
                    rows = turned_f[:, i, :, half]
                else:
                    rows = turned_f[:, :, i, half]
                left[side, n, :, pl.ds(T * i, T)] = rows.reshape(128, T).astype(BF16)
            dst = ref.at[pl.ds(at, 128), :]
            stores.append(load(left.at[side, n], dst, left_sem.at[side, n]))

    first = first_halves()
    scale = jnp.asarray(HD**-0.5, BF16)
    cosine, sine = rotary(lengths, inverse)
    row = lax.broadcasted_iota(jnp.int32, (T, T), 0)
    col = lax.broadcasted_iota(jnp.int32, (T, T), 1)
    bias[...] = jnp.where((col >= doc_start(lengths, row)) & (col <= row), 0.0, NEG)
    active[...] = of_doc(lengths, lax.broadcasted_iota(jnp.int32, (T, GW), 0), heads)
    level[...] = upright(bucket[...])
    prob = upright(router[...])

    loads[0].wait()
    start(loads[2:4])
    resid = tokens[...].astype(F32)
    rscale = lax.rsqrt(jnp.mean(resid * resid, -1, keepdims=True) + EPS)
    normed[...] = (resid * rscale * norm_gain[...]).astype(BF16)
    for n in range(3):
        loads[1 + n].wait()
        if n == 1:
            loads.append(load(cot_hbm, cot, in_sem.at[4]))
        if n == 2:
            loads.append(load(wo_hbm, wo, in_sem.at[5]))
            for copy in ffn_loads(0) + ffn_loads(1):
                copy.start()
        part = nn(normed[...], wqkv[n])
        qkv[n] = (turned(part, cosine, sine, first) if n < 2 else part).astype(BF16)
    stores.append(load(qkv, qkv_out, out_sem.at[0]))

    def attend(g, carry):
        at = columns(g, GW)
        keys, values = by_head(qkv[1, :, at]), by_head(qkv[2, :, at])
        s = nt(qkv[0, :, at] * scale, keys)
        parts = []
        for h in range(HEADS):
            one = s[:, T * h : T * h + T] + bias[...]
            e = jnp.exp(one - jnp.max(one, -1, keepdims=True))
            parts.append((e / jnp.sum(e, -1, keepdims=True)).astype(BF16))
        out = nn(jnp.concatenate(parts, 1), values)
        merged[:, at] = jnp.where(head_of(g) < active[...], out, 0.0).astype(BF16)

        @pl.when((g > 0) & (g < NEST - 1))
        def _():
            for copy in ffn_loads(g + 1):
                copy.start()

        return carry

    lax.fori_loop(0, GROUPS, attend, 0)
    loads[5].wait()
    middle[...] = tokens[...].astype(F32) + nn(merged[...], wo[...])
    normed_mid, _ = normalized(middle[...])
    zed[...] = (normed_mid * ln_gain[...] + ln_bias[...]).astype(BF16)
    loads[4].wait()
    gb[...] = (cot[...].astype(F32) * prob).astype(BF16)
    stores.append(load(gb, first_other.at[pl.ds(GB, T), :], out_sem.at[2]))

    def act_stores(j):
        at = (pl.ds(ACT, 512), columns(j, T))
        return [
            pltpu.make_async_copy(act_turned.at[side, :, at[1]], ref.at[at], act_sem.at[side, j])
            for side, ref in enumerate(firsts)
        ]

    def gp_store(j):
        rows = pl.ds(pl.multiple_of(GP + T * j, T), T)
        return pltpu.make_async_copy(gp.at[:, columns(j, D)], second_other.at[rows, :], gp_sem.at[j])

    def hidden(j, carry):
        copy_up, copy_down = ffn_loads(j)
        at = columns(j, D)
        copy_up.wait()
        r = jnp.where(level[...] >= j, jnp.maximum(nn(zed[...], up[:, at]), 0.0), 0.0)
        a = (r * r).astype(BF16)
        act[:, at] = a
        by_core = a.T.reshape(16, 2, 32, T)
        low_rows, high_rows = by_core[:, 0].reshape(512, T), by_core[:, 1].reshape(512, T)
        act_turned[0, :, columns(j, T)] = jnp.where(core == 0, low_rows, high_rows)
        act_turned[1, :, columns(j, T)] = jnp.where(core == 0, high_rows, low_rows)
        for copy in act_stores(j):
            copy.start()
        copy_down.wait()
        gp[:, at] = (nt(gb[...], down[at, :]) * 2.0 * r).astype(BF16)
        gp_store(j).start()
        return carry

    lax.fori_loop(0, NEST, hidden, 0)
    store_left(0, zed[...], 1, seconds, ZED)
    store_left(1, normed[...], 2, seconds, NORMED)
    store_left(2, merged[...], 0, firsts, MERGED)

    branch = nn(act[...], down[...]).astype(BF16).astype(F32)
    mid = middle[...]
    mixed[...] = (mid + prob * branch).astype(BF16)
    stores.append(load(mixed, mixed_out, out_sem.at[1]))
    grad_zed = nt(gp[...], up[...]).astype(BF16).astype(F32)
    normed_mid, rstd = normalized(mid)
    parts[0:1, :] = jnp.sum(grad_zed * normed_mid, 0, keepdims=True)
    parts[1:2, :] = jnp.sum(grad_zed, 0, keepdims=True)
    grad_norm = grad_zed * ln_gain[...]
    grad = cot[...].astype(F32) + rstd * (
        grad_norm
        - jnp.mean(grad_norm, -1, keepdims=True)
        - normed_mid * jnp.mean(grad_norm * normed_mid, -1, keepdims=True)
    )
    ga[...] = grad.astype(BF16)
    stores.append(load(parts, parts_out, out_sem.at[3]))
    stores.append(load(ga, first_other.at[pl.ds(GA, T), :], out_sem.at[4]))
    for j in range(NEST):
        wait(act_stores(j) + [gp_store(j)])
    wait(stores)


def front(lengths, heads, norm_gain, inverse, ln_gain, ln_bias, router, bucket, *arrays):
    row_b = sds((T, D), BF16)
    scratch = [
        sds((8, D), F32),
        row_b,
        row_b,
        sds((3, D, D), BF16),
        sds((D, D), BF16),
        sds((D, FF), BF16),
        sds((FF, D), BF16),
        sds((3, T, D), BF16),
        row_b,
        row_b,
        row_b,
        row_b,
        sds((T, FF), BF16),
        sds((2, 512, D), BF16),
        sds((T, FF), BF16),
        sds((4, 4, 4, 2, 8, T), F32),
        sds((2, 3, 128, D), BF16),
        sds((T, D), F32),
        row_b,
        row_b,
        sds((T, T), F32),
        sds((T, GW), jnp.int32),
        sds((T, 1), jnp.int32),
    ]
    semaphores = [(6,), (2, NEST), (2, NEST), (NEST,), (2, 3), (5,)]
    return call(
        front_kernel,
        "front",
        2 * T * D * (4 * D + 4 * FF),
        40 * MIB,
        58,
        in_specs=[smem()] * 2 + [vmem()] * 6 + [hbm()] * 6,
        out_specs=[hbm()] * 7,
        out_shape=[
            sds((8, D), F32),
            sds((FIRST_OWN, D), BF16),
            sds((FIRST, D), BF16),
            sds((SECOND_OWN, D), BF16),
            sds((SECOND, D), BF16),
            sds((3, T, D), BF16),
            row_b,
        ],
        scratch_shapes=[pltpu.VMEM(s.shape, s.dtype) for s in scratch]
        + [pltpu.SemaphoreType.DMA(s) for s in semaphores],
    )(lengths, heads, norm_gain, inverse, ln_gain, ln_bias, router, bucket, *arrays)


def back_kernel(
    lengths,
    heads,
    norm_gain,
    inverse,
    bucket,
    parts_hbm,
    first_other,
    qkv_hbm,
    tokens_hbm,
    wqkv_hbm,
    wo_hbm,
    third_mine,
    third_other,
    input_grad_out,
    parts,
    ga,
    qkv,
    input_grad,
    tokens,
    wqkv,
    wo,
    gqkv,
    lines_f,
    lines,
    bias,
    active,
    in_sem,
    w_sem,
    group_sem,
    out_sem,
):
    core = lax.axis_index("c")
    thirds = (third_mine, third_other)
    loads = [
        load(first_other.at[pl.ds(GA, T), :], ga, in_sem.at[0]),
        load(wo_hbm.at[pl.ds(0, GW), :], wo.at[pl.ds(0, GW), :], in_sem.at[1]),
        load(qkv_hbm.at[:, :, pl.ds(0, GW)], qkv.at[:, :, pl.ds(0, GW)], in_sem.at[2]),
    ]
    others = pl.ds(GW, D - GW)
    more = [
        pltpu.make_async_copy(wo_hbm.at[others, :], wo.at[others, :], in_sem.at[5]),
        pltpu.make_async_copy(qkv_hbm.at[:, :, others], qkv.at[:, :, others], in_sem.at[6]),
    ]
    late = [
        pltpu.make_async_copy(tokens_hbm, tokens, in_sem.at[3]),
        pltpu.make_async_copy(parts_hbm, parts, in_sem.at[7]),
    ]
    for n in range(3):
        src = wqkv_hbm.at[:, n * D : (n + 1) * D]
        late.append(pltpu.make_async_copy(src, wqkv.at[n], w_sem.at[n]))

    first = first_halves()
    scale = jnp.asarray(HD**-0.5, BF16)
    cosine, sine = rotary(lengths, inverse)
    sine = -sine
    query = lax.broadcasted_iota(jnp.int32, (T, T), 1)
    key = lax.broadcasted_iota(jnp.int32, (T, T), 0)
    bias[...] = jnp.where((key >= doc_start(lengths, query)) & (key <= query), 0.0, NEG)
    active[...] = of_doc(lengths, lax.broadcasted_iota(jnp.int32, (T, GW), 0), heads)
    wait(loads)
    for copy in more:
        copy.start()

    def group_stores(g):
        at = columns(g, GW)
        return [
            pltpu.make_async_copy(
                gqkv.at[n, :, at], third_other.at[pl.ds(GQKV + T * n, T), at], group_sem.at[n, g]
            )
            for n in range(3)
        ]

    def attend_back(g, carry):
        @pl.when(g == 1)
        def _():
            wait(more)
            start(late)

        at = columns(g, GW)
        gm = nt(ga[...], wo[at, :])
        gm = jnp.where(head_of(g) < active[...], gm, 0.0).astype(BF16)
        gms, queries = by_head(gm), by_head(qkv[0, :, at] * scale)
        k = qkv[1, :, at]
        s = nt(k, queries)
        grad_p = nt(qkv[2, :, at], gms)
        parts_p, parts_s = [], []
        for h in range(HEADS):
            one = s[:, T * h : T * h + T] + bias[...]
            e = jnp.exp(one - jnp.max(one, 0, keepdims=True))
            p = e / jnp.sum(e, 0, keepdims=True)
            grad = grad_p[:, T * h : T * h + T]
            parts_p.append(p.astype(BF16))
            grad = p * (grad - jnp.sum(p * grad, 0, keepdims=True))
            parts_s.append(grad.astype(BF16))
        grad_s = jnp.concatenate(parts_s, 1)
        grad_v = nn(jnp.concatenate(parts_p, 1), gms)
        grad_k = nn(grad_s, queries)
        wide = nn((k * scale).T, grad_s)
        grad_q = [wide[HD * h : HD * h + HD, T * h : T * h + T] for h in range(HEADS)]
        grad_q = jnp.concatenate(grad_q, 0).T
        gqkv[0, :, at] = turned(grad_q, cosine, sine, first).astype(BF16)
        gqkv[1, :, at] = turned(grad_k, cosine, sine, first).astype(BF16)
        gqkv[2, :, at] = grad_v.astype(BF16)
        for copy in group_stores(g):
            copy.start()
        return carry

    lax.fori_loop(0, GROUPS, attend_back, 0)

    wait(late)
    grad_normed = nt(gqkv[0], wqkv[0]) + nt(gqkv[1], wqkv[1]) + nt(gqkv[2], wqkv[2])
    resid = tokens[...].astype(F32)
    rscale = lax.rsqrt(jnp.mean(resid * resid, -1, keepdims=True) + EPS)
    unit = resid * rscale
    gain_part = jnp.sum(grad_normed * unit, 0, keepdims=True)
    grad_unit = grad_normed * norm_gain[...]
    input_grad[...] = ga[...].astype(F32) + rscale * (
        grad_unit - unit * jnp.mean(grad_unit * unit, -1, keepdims=True)
    )
    stores = [load(input_grad, input_grad_out, out_sem.at[0])]

    item = lax.broadcasted_iota(jnp.int32, (128, 1), 0)
    count = jnp.zeros((128, 1), jnp.int32)
    for n in range(NEST):
        total = jnp.sum((bucket[...] == n).astype(jnp.int32), 1, keepdims=True)
        at = item - 3 - BITS * n
        bit = lax.shift_right_logical(total, jnp.clip(at, 0, BITS - 1)) & 1
        count = jnp.where((at >= 0) & (at < BITS), bit, count)
    wide = jnp.where(item == 0, gain_part, jnp.where(item == 1, parts[0:1, :], parts[1:2, :]))
    lines_f[...] = jnp.where(item < 3, wide, count.astype(F32)).T.reshape(lines_f.shape)
    for side, ref in enumerate(thirds):
        half = core if side == 0 else 1 - core
        for i in range(4):
            part = lines_f[:, i, :, half].reshape(128, 128).astype(BF16)
            lines[side, :, pl.ds(128 * i, 128)] = part
        dst = ref.at[pl.ds(LINES, 128), pl.ds(0, 512)]
        stores.append(load(lines.at[side], dst, out_sem.at[1 + side]))
    for g in range(GROUPS):
        wait(group_stores(g))
    wait(stores)


def back(lengths, heads, norm_gain, inverse, bucket, parts, *arrays):
    scratch = [
        sds((8, D), F32),
        sds((T, D), BF16),
        sds((3, T, D), BF16),
        sds((T, D), F32),
        sds((T, D), BF16),
        sds((3, D, D), BF16),
        sds((D, D), BF16),
        sds((3, T, D), BF16),
        sds((4, 4, 4, 2, 8, 128), F32),
        sds((2, 128, 512), BF16),
        sds((T, T), F32),
        sds((T, GW), jnp.int32),
    ]
    return call(
        back_kernel,
        "back",
        2 * T * D * 4 * D + 10 * 16 * T * T * 256,
        18 * MIB,
        32,
        in_specs=[smem()] * 2 + [vmem()] * 3 + [hbm()] * 6,
        out_specs=[hbm()] * 3,
        out_shape=[sds((THIRD_OWN, D), BF16), sds((THIRD, D), BF16), sds((T, D), F32)],
        scratch_shapes=[pltpu.VMEM(s.shape, s.dtype) for s in scratch]
        + [pltpu.SemaphoreType.DMA(s) for s in [(8,), (3,), (3, GROUPS), (3,)]],
    )(lengths, heads, norm_gain, inverse, bucket, parts, *arrays)


def load_left(refs, at, rows, axis, left, sem):
    return [
        pltpu.make_async_copy(
            ref.at[pl.ds(at, rows), columns(block, T)],
            left.at[pl.ds(rows * i, rows), pl.ds(T * m, T)],
            sem.at[i, m],
        )
        for i, block in enumerate(block_order(axis))
        for m, ref in enumerate(refs)
    ]


def load_right(refs, at, right, sem):
    return [
        pltpu.make_async_copy(ref.at[pl.ds(at, T), :], right.at[pl.ds(T * m, T), :], sem.at[m])
        for m, ref in enumerate(refs)
    ]


def store_out(out, at, sent, kept, sem):
    return [
        load(out.at[pl.ds(2 * side, 2), :, at], ref.at[:, :, at], sem.at[side])
        for side, ref in enumerate((sent, kept))
    ]


def down_grad_kernel(
    own, one, two, sent, kept, act, merged, gb, ga, out, act_sem, merged_sem, gb_sem, ga_sem, sem
):
    refs, split = (one, two), (own, two)
    gb_loads = load_right(refs, GB, gb, gb_sem)
    act_loads = load_left(split, ACT, 512, "y", act, act_sem)
    ga_loads = load_right(refs, GA, ga, ga_sem)
    merged_loads = load_left(split, MERGED, 128, "y", merged, merged_sem)
    stages = [gb_loads + act_loads[:2], act_loads[2:4], act_loads[4:6], act_loads[6:]]
    stages.append(ga_loads + merged_loads)
    stores = []
    start(stages[0] + stages[1])
    wide = pl.ds(0, D)
    for i in range(4):
        wait(stages[i])
        start(stages[i + 2] if i < 3 else [])
        out[i, :, wide] = nn(act[pl.ds(512 * i, 512), :], gb[...]).astype(BF16)
        dst = (sent, kept)[i // 2].at[i % 2, :, wide]
        stores.append(load(out.at[i, :, wide], dst, sem.at[0, i]))
    wait(stages[4])
    part = nn(merged[...], ga[...])
    more = pl.ds(D, T)
    for i in range(4):
        rows = part[128 * i : 128 * i + 128].reshape(16, 8, D)
        quarters = [rows[:, :, T * q : T * q + T] for q in range(4)]
        out[i, :, more] = jnp.concatenate(quarters, 1).reshape(512, T).astype(BF16)
    stores += store_out(out, more, sent, kept, sem.at[1])
    wait(stores)


def down_grads(own, one, two):
    part = sds((2, 512, D + T), BF16)
    return call(
        down_grad_kernel,
        "down_and_out_grad",
        2 * T * D * (FF + D),
        10 * MIB,
        24,
        (2,),
        in_specs=[hbm()] * 3,
        out_specs=[hbm()] * 2,
        out_shape=[part, part],
        scratch_shapes=[
            pltpu.VMEM((FF // 2, 2 * T), BF16),
            pltpu.VMEM((512, 2 * T), BF16),
            pltpu.VMEM((2 * T, D), BF16),
            pltpu.VMEM((2 * T, D), BF16),
            pltpu.VMEM((4, 512, D + T), BF16),
            pltpu.SemaphoreType.DMA((4, 2)),
            pltpu.SemaphoreType.DMA((4, 2)),
            pltpu.SemaphoreType.DMA((2,)),
            pltpu.SemaphoreType.DMA((2,)),
            pltpu.SemaphoreType.DMA((2, 4)),
        ],
    )(own, one, two)


def up_and_qkv_kernel(
    own,
    one,
    two,
    late_own,
    three,
    four,
    after,
    up_sent,
    up_kept,
    qkv_sent,
    qkv_kept,
    zed,
    normed,
    gp,
    gqkv,
    lines,
    up_out,
    qkv_out,
    zed_sem,
    normed_sem,
    gp_sem,
    gqkv_sem,
    line_sem,
    up_sem,
    qkv_sem,
):
    refs, split = (one, two), (own, two)
    late = (three, four)
    zed_loads = load_left(split, ZED, 128, "x", zed, zed_sem)
    gp_loads = [load_right(refs, GP + T * n, gp.at[n], gp_sem.at[n]) for n in range(4)]
    line_loads = [
        pltpu.make_async_copy(
            ref.at[pl.ds(LINES, 128), columns(block, 128)],
            lines.at[i, m],
            line_sem.at[i, m],
        )
        for i, block in enumerate(block_order("x"))
        for m, ref in enumerate((late_own, four))
    ]
    normed_loads = load_left(split, NORMED, 128, "z", normed, normed_sem)
    gqkv_loads = [load_right(late, GQKV + T * n, gqkv.at[n], gqkv_sem.at[n]) for n in range(3)]
    stages = [zed_loads + gp_loads[0], *gp_loads[1:], normed_loads + gqkv_loads[0]]
    stages += [gqkv_loads[1], gqkv_loads[2] + line_loads, []]
    stores = []
    start(stages[0] + stages[1])
    for n in range(4):
        wait(stages[n])
        start(stages[n + 2])
        at = pl.ds(n * D, D)
        up_out[:, :, at] = nn(zed[...], gp[n]).astype(BF16).reshape(4, 128, D)
        stores += store_out(up_out, at, up_sent, up_kept, up_sem.at[n])
    for n in range(3):
        wait(stages[4 + n])
        start(stages[6] if n == 0 else [])
        at = pl.ds(n * D, D)
        qkv_out[:, :, at] = nn(normed[...], gqkv[n]).astype(BF16).reshape(4, 128, D)
        stores += store_out(qkv_out, at, qkv_sent, qkv_kept, qkv_sem.at[n])
    at = pl.ds(FF, 128)
    up_out[:, :, at] = (lines[:, 0].astype(F32) + lines[:, 1].astype(F32)).astype(BF16)
    stores += store_out(up_out, at, up_sent, up_kept, up_sem.at[4])
    wait(stores)


def up_and_qkv_grads(own, one, two, late_own, three, four, after):
    up = sds((2, 128, FF + 128), BF16)
    qkv = sds((2, 128, 3 * D), BF16)
    return call(
        up_and_qkv_kernel,
        "up_and_qkv_grad",
        2 * T * D * (FF + 3 * D),
        16 * MIB,
        28,
        (2, 5),
        in_specs=[hbm()] * 7,
        out_specs=[hbm()] * 4,
        out_shape=[up, up, qkv, qkv],
        scratch_shapes=[
            pltpu.VMEM((512, 2 * T), BF16),
            pltpu.VMEM((512, 2 * T), BF16),
            pltpu.VMEM((4, 2 * T, D), BF16),
            pltpu.VMEM((3, 2 * T, D), BF16),
            pltpu.VMEM((4, 2, 128, 128), BF16),
            pltpu.VMEM((4, 128, FF + 128), BF16),
            pltpu.VMEM((4, 128, 3 * D), BF16),
            pltpu.SemaphoreType.DMA((4, 2)),
            pltpu.SemaphoreType.DMA((4, 2)),
            pltpu.SemaphoreType.DMA((4, 2)),
            pltpu.SemaphoreType.DMA((3, 2)),
            pltpu.SemaphoreType.DMA((4, 2)),
            pltpu.SemaphoreType.DMA((5, 2)),
            pltpu.SemaphoreType.DMA((3, 2)),
        ],
    )(own, one, two, late_own, three, four, after)


def swap_cores(array):
    return lax.ppermute(array, "c", [(0, 1), (1, 0)])


def pairs(mask_0, mask_1):
    perm = []
    for p in range(4):
        perm.append((2 * p, 2 * (p ^ mask_0)))
        perm.append((2 * p + 1, 2 * (p ^ mask_1) + 1))
    return perm


def ordered(token, *arrays):
    return lax.optimization_barrier((*arrays, token))[:-1]


def chain(sent, kept, axes, shape, finish):
    left = [axis for axis in ("y", "x", "z") if axis != axes[0]]
    for axis in axes:
        got = lax.ppermute(sent, (axis, "c"), pairs(1, 3))
        token = yield sent
        got, kept = ordered(token, got, kept)
        more = (got[1].astype(F32) + kept[1].astype(F32)).astype(BF16)
        got_2 = lax.ppermute(more, (axis, "c"), pairs(3, 1))
        token = yield more
        got, kept, got_2 = ordered(token, got, kept, got_2)
        terms = [got.reshape(2, *shape), kept.reshape(2, *shape), got_2.reshape(1, *shape)]
        if not left:
            return finish(*terms)
        following = axes[axes.index(axis) + 1]
        dim = left.index(following)
        left.pop(dim)
        shape = shape[:dim] + shape[dim + 1 :]

        def block(at):
            total = 0.0
            for term in terms:
                start = [0] * term.ndim
                start[1 + dim] = at
                sizes = (1,) + term.shape[1 : 1 + dim] + (1,) + term.shape[2 + dim :]
                total = total + lax.dynamic_slice(term, start, sizes).astype(F32)
            return total.reshape(shape)

        first, across, own, second = [block(at) for at in block_order(following)]
        sent = jnp.stack([first, across]).astype(BF16)
        kept = jnp.stack([own, second])


def total(terms, *at):
    return sum(term[(0, *at)].astype(F32) for term in terms)


def take_turns(token, turns, **chains):
    for steps in chains.values():
        next(steps)
    for turn in turns:
        token = next_step(chains[turn], token)


def next_step(steps, token):
    try:
        return steps.send(token)
    except StopIteration as end:
        return end.value


def body(
    tokens,
    norm_gain,
    qkv_weight,
    out_weight,
    ln_gain,
    ln_bias,
    up_weight,
    down_weight,
    buckets,
    router_prob,
    heads_active,
    doc_lengths,
    cotangent,
):
    norm_gain, ln_gain, ln_bias = [v.reshape(1, D) for v in (norm_gain, ln_gain, ln_bias)]
    router = router_prob.reshape(1, T)
    levels = buckets.reshape(1, T)
    inverse = np.tile(10000.0 ** (-2.0 * np.arange(HD // 2) / HD), 4).reshape(1, 128)
    inverse = jnp.asarray(inverse, F32)

    parts, first, first_other, second, second_other, qkv, mixed = front(
        doc_lengths,
        heads_active,
        norm_gain,
        inverse,
        ln_gain,
        ln_bias,
        router,
        levels,
        tokens,
        cotangent,
        qkv_weight,
        out_weight,
        up_weight,
        down_weight,
    )
    first_2, second_2 = swap_cores(first_other), swap_cores(second_other)
    third, third_other, input_grad = back(
        doc_lengths,
        heads_active,
        norm_gain,
        inverse,
        levels,
        parts,
        first_other,
        qkv,
        tokens,
        qkv_weight,
        out_weight,
    )
    third_2 = swap_cores(third_other)
    first_2, _ = lax.optimization_barrier((first_2, third))
    down_sent, down_kept = down_grads(first, first_other, first_2)
    up_sent, up_kept, qkv_sent, qkv_kept = up_and_qkv_grads(
        second, second_other, second_2, third, third_other, third_2, down_sent
    )

    every = slice(None)
    grads = {}

    def down_done(*terms):
        grads["down"] = total(terms, every, slice(0, D))
        out = total(terms, every, slice(D, D + T))
        grads["out"] = out.reshape(4, 8, T).transpose(1, 0, 2).reshape(8, D)
        grads["down"], grads["out"] = lax.optimization_barrier((grads["down"], grads["out"]))
        return grads["out"]

    def up_done(*terms):
        grads["up"] = total(terms, every, slice(0, FF))
        line = total(terms, every, slice(FF, FF + 128))
        grads["gains"] = [line[:, n] for n in range(3)]
        bits = line[0, 3 : 3 + BITS * NEST].astype(jnp.int32).reshape(NEST, BITS)
        grads["counts"] = jnp.sum(bits << jnp.arange(BITS, dtype=jnp.int32)[None, :], 1)
        done = (grads["up"], grads["counts"], *grads["gains"])
        grads["up"], grads["counts"], *grads["gains"] = lax.optimization_barrier(done)
        return grads["up"]

    def qkv_done(*terms):
        grads["qkv"] = total(terms)
        return grads["qkv"]

    take_turns(
        qkv_sent,
        "dquqduqduqdudquduq",
        d=chain(down_sent, down_kept, "yxz", (4, 4, 32, D + T), down_done),
        u=chain(up_sent, up_kept, "xyz", (4, 4, 8, FF + 128), up_done),
        q=chain(qkv_sent, qkv_kept, "zyx", (4, 4, 8, 3 * D), qkv_done),
    )
    gain_grad, ln_gain_grad, ln_bias_grad = grads["gains"]
    return (
        mixed,
        input_grad,
        gain_grad,
        grads["qkv"],
        grads["out"],
        ln_gain_grad,
        ln_bias_grad,
        grads["up"],
        grads["down"],
        grads["counts"],
    )


def solution(mesh):
    finer = Mesh(mesh.devices.reshape(4, 4, 4, 2), AX)
    rows = P(AX, None)
    return jax.shard_map(
        body,
        mesh=finer,
        in_specs=(rows, P(), P(), P(), P(), P(), P(), P(), rows, P(AX), rows, rows, rows),
        out_specs=(rows, rows, P(AX), rows, rows, P(AX), P(AX), rows, rows, P()),
        check_vma=False,
    )
```

```python
import jax
import jax.numpy as jnp
import numpy as np
from jax import lax
from jax.experimental import pallas as pl
from jax.experimental.pallas import tpu as pltpu
from jax.sharding import Mesh
from jax.sharding import PartitionSpec as P

HD = 64
NEST = 4
AX = ("y", "x", "z", "c")

NEG = -1e30
EPS = 1e-05
F32 = jnp.float32
BF16 = jnp.bfloat16
T = 256
D = 1024
FF = 4096
GW = 256
GROUPS = D // GW
HEADS = GW // HD
ACT, MERGED, FIRST_OWN, GB, GA, FIRST = 0, 512, 640, 640, 896, 1152
ZED, NORMED, SECOND_OWN, GP, SECOND = 0, 128, 256, 256, 1280
LINES, THIRD_OWN, GQKV, THIRD = 0, 128, 128, 896
TURNS = "dquqduqduqduqdudqu"
BITS = 9
MIB = 1024 * 1024


def nn(a, b):
    return lax.dot_general(a, b, (((1,), (0,)), ((), ())), preferred_element_type=F32)


def nt(a, b):
    return lax.dot_general(a, b, (((1,), (1,)), ((), ())), preferred_element_type=F32)


def tn(a, b):
    return lax.dot_general(a, b, (((0,), (0,)), ((), ())), preferred_element_type=F32)


def sds(shape, dtype):
    return jax.ShapeDtypeStruct(shape, dtype)


def smem():
    return pl.BlockSpec(memory_space=pltpu.SMEM)


def vmem():
    return pl.BlockSpec(memory_space=pltpu.VMEM)


def hbm():
    return pl.BlockSpec(memory_space=pltpu.HBM)


def call(kernel, name, flops, moved, room, anywhere=(), **kw):
    def in_hbm(spec):
        return spec.memory_space == pltpu.HBM

    kw["out_shape"] = [
        pltpu.HBM(s.shape, s.dtype) if in_hbm(spec) else s
        for s, spec in zip(kw["out_shape"], kw["out_specs"])
    ]
    run = pl.pallas_call(
        kernel,
        name=name,
        compiler_params=pltpu.CompilerParams(vmem_limit_bytes=room * MIB),
        cost_estimate=pl.CostEstimate(flops=flops, bytes_accessed=moved, transcendentals=0),
        **kw,
    )

    def placed(*args):
        return run(
            *(
                pltpu.with_memory_space_constraint(arg, pltpu.HBM)
                if in_hbm(spec) and n not in anywhere
                else arg
                for n, (arg, spec) in enumerate(zip(args, kw["in_specs"]))
            )
        )

    return placed


def first_halves():
    return lax.broadcasted_iota(jnp.int32, (T, 128), 1) % HD < HD // 2


def head_of(g):
    return HEADS * g + lax.broadcasted_iota(jnp.int32, (T, GW), 1) // HD


def by_head(x):
    lane = lax.broadcasted_iota(jnp.int32, (T, GW), 1)
    zero = jnp.zeros((T, GW), x.dtype)
    own = [(lane >= HD * h) & (lane < HD * h + HD) for h in range(HEADS)]
    return jnp.concatenate([jnp.where(keep, x, zero) for keep in own], 0)


def turned(x, cosine, sine, first):
    parts = []
    for at in range(0, x.shape[1], 128):
        part = x[:, at : at + 128]
        other = jnp.where(first, pltpu.roll(part, 128 - HD // 2, 1), pltpu.roll(part, HD // 2, 1))
        parts.append(part * cosine + other * sine)
    return jnp.concatenate(parts, 1)


def doc_ends(lengths):
    return lengths[0, 0], lengths[0, 0] + lengths[0, 1]


def doc_start(lengths, place):
    end_0, end_1 = doc_ends(lengths)
    return jnp.where(place >= end_1, end_1, jnp.where(place >= end_0, end_0, 0))


def of_doc(lengths, place, values):
    end_0, end_1 = doc_ends(lengths)
    late = jnp.where(place >= end_1, values[0, 2], values[0, 1])
    return jnp.where(place >= end_0, late, values[0, 0])


def normalized(middle):
    shifted = middle - jnp.mean(middle, -1, keepdims=True)
    rstd = lax.rsqrt(jnp.mean(shifted * shifted, -1, keepdims=True) + EPS)
    return shifted * rstd, rstd


def block_order(axis):
    p = lax.axis_index(axis)
    core = lax.axis_index("c")
    return [p ^ (1 + 2 * core), p ^ 2, p, p ^ (3 - 2 * core)]


def load(src, dst, sem):
    copy = pltpu.make_async_copy(src, dst, sem)
    copy.start()
    return copy


def columns(j, size):
    if isinstance(j, int):
        return pl.ds(j * size, size)
    return pl.ds(pl.multiple_of(j * size, size), size)


def upright(row):
    return jnp.broadcast_to(row, (8, T)).T[:, :1]


def places():
    return lax.broadcasted_iota(jnp.int32, (T, 128), 0)


def rotary(lengths, inverse):
    phase = (places() - doc_start(lengths, places())).astype(F32) * inverse[...]
    sine = jnp.sin(phase)
    return jnp.cos(phase), jnp.where(first_halves(), -sine, sine)


def start(copies):
    for copy in copies:
        copy.start()


def wait(copies):
    for copy in copies:
        copy.wait()


def front_kernel(
    lengths,
    heads,
    norm_gain,
    inverse,
    ln_gain,
    ln_bias,
    router,
    bucket,
    tokens_hbm,
    cot_hbm,
    wqkv_hbm,
    wo_hbm,
    up_hbm,
    down_hbm,
    parts_out,
    first_mine,
    first_other,
    second_mine,
    second_other,
    qkv_out,
    act_out,
    middle_out,
    parts,
    tokens,
    cot,
    wqkv,
    wo,
    up,
    down,
    qkv,
    normed,
    merged,
    zed,
    gb,
    act,
    act_turned,
    gp,
    turned_f,
    left,
    middle,
    ga,
    bias,
    active,
    level,
    in_sem,
    ffn_sem,
    act_sem,
    gp_sem,
    left_sem,
    out_sem,
):
    core = lax.axis_index("c")
    firsts, seconds = (first_mine, first_other), (second_mine, second_other)
    loads = [load(tokens_hbm, tokens, in_sem.at[0])]
    for n in range(3):
        src = wqkv_hbm.at[:, n * D : (n + 1) * D]
        loads.append(pltpu.make_async_copy(src, wqkv.at[n], in_sem.at[1 + n]))
    loads[1].start()

    def ffn_loads(j):
        at = columns(j, D)
        return (
            pltpu.make_async_copy(up_hbm.at[:, at], up.at[:, at], ffn_sem.at[0, j]),
            pltpu.make_async_copy(down_hbm.at[at, :], down.at[at, :], ffn_sem.at[1, j]),
        )

    stores = []

    def store_left(n, value, axis, refs, at):
        turned_f[...] = value.astype(F32).T.reshape(turned_f.shape)
        for side, ref in enumerate(refs):
            half = core if side == 0 else 1 - core
            for i in range(4):
                if axis == 0:
                    rows = turned_f[i, :, :, half]
                elif axis == 1:
                    rows = turned_f[:, i, :, half]
                else:
                    rows = turned_f[:, :, i, half]
                left[side, n, :, pl.ds(T * i, T)] = rows.reshape(128, T).astype(BF16)
            dst = ref.at[pl.ds(at, 128), :]
            stores.append(load(left.at[side, n], dst, left_sem.at[side, n]))

    first = first_halves()
    scale = jnp.asarray(HD**-0.5, BF16)
    cosine, sine = rotary(lengths, inverse)
    row = lax.broadcasted_iota(jnp.int32, (T, T), 0)
    col = lax.broadcasted_iota(jnp.int32, (T, T), 1)
    bias[...] = jnp.where((col >= doc_start(lengths, row)) & (col <= row), 0.0, NEG)
    active[...] = of_doc(lengths, lax.broadcasted_iota(jnp.int32, (T, GW), 0), heads)
    level[...] = upright(bucket[...])
    prob = upright(router[...])

    loads[0].wait()
    start(loads[2:4])
    resid = tokens[...].astype(F32)
    rscale = lax.rsqrt(jnp.mean(resid * resid, -1, keepdims=True) + EPS)
    normed[...] = (resid * rscale * norm_gain[...]).astype(BF16)
    for n in range(3):
        loads[1 + n].wait()
        if n == 1:
            loads.append(load(cot_hbm, cot, in_sem.at[4]))
        if n == 2:
            loads.append(load(wo_hbm, wo, in_sem.at[5]))
            for copy in ffn_loads(0) + ffn_loads(1):
                copy.start()
        part = nn(normed[...], wqkv[n])
        qkv[n] = (turned(part, cosine, sine, first) if n < 2 else part).astype(BF16)
    stores.append(load(qkv, qkv_out, out_sem.at[0]))

    def attend(g, carry):
        at = columns(g, GW)
        keys, values = by_head(qkv[1, :, at]), by_head(qkv[2, :, at])
        s = nt(qkv[0, :, at] * scale, keys)
        parts = []
        for h in range(HEADS):
            one = s[:, T * h : T * h + T] + bias[...]
            e = jnp.exp(one - jnp.max(one, -1, keepdims=True))
            parts.append((e / jnp.sum(e, -1, keepdims=True)).astype(BF16))
        out = nn(jnp.concatenate(parts, 1), values)
        merged[:, at] = jnp.where(head_of(g) < active[...], out, 0.0).astype(BF16)

        @pl.when((g > 0) & (g < NEST - 1))
        def _():
            for copy in ffn_loads(g + 1):
                copy.start()

        return carry

    lax.fori_loop(0, GROUPS, attend, 0)
    loads[5].wait()
    middle[...] = tokens[...].astype(F32) + nn(merged[...], wo[...])
    stores.append(load(middle, middle_out, out_sem.at[1]))
    normed_mid, _ = normalized(middle[...])
    zed[...] = (normed_mid * ln_gain[...] + ln_bias[...]).astype(BF16)
    loads[4].wait()
    gb[...] = (cot[...].astype(F32) * prob).astype(BF16)
    stores.append(load(gb, first_other.at[pl.ds(GB, T), :], out_sem.at[2]))

    def act_stores(j):
        at = (pl.ds(ACT, 512), columns(j, T))
        return [
            pltpu.make_async_copy(act_turned.at[side, :, at[1]], ref.at[at], act_sem.at[side, j])
            for side, ref in enumerate(firsts)
        ]

    def act_store(j):
        at = columns(j, D)
        return pltpu.make_async_copy(act.at[:, at], act_out.at[:, at], act_sem.at[2, j])

    def gp_store(j):
        rows = pl.ds(pl.multiple_of(GP + T * j, T), T)
        return pltpu.make_async_copy(gp.at[:, columns(j, D)], second_other.at[rows, :], gp_sem.at[j])

    def hidden(j, carry):
        copy_up, copy_down = ffn_loads(j)
        at = columns(j, D)
        copy_up.wait()
        r = jnp.where(level[...] >= j, jnp.maximum(nn(zed[...], up[:, at]), 0.0), 0.0)
        a = (r * r).astype(BF16)
        act[:, at] = a
        by_core = a.T.reshape(16, 2, 32, T)
        low_rows, high_rows = by_core[:, 0].reshape(512, T), by_core[:, 1].reshape(512, T)
        act_store(j).start()
        act_turned[0, :, columns(j, T)] = jnp.where(core == 0, low_rows, high_rows)
        act_turned[1, :, columns(j, T)] = jnp.where(core == 0, high_rows, low_rows)
        for copy in act_stores(j):
            copy.start()
        copy_down.wait()
        gp[:, at] = (nt(gb[...], down[at, :]) * 2.0 * r).astype(BF16)
        gp_store(j).start()
        return carry

    lax.fori_loop(0, NEST, hidden, 0)
    store_left(0, zed[...], 1, seconds, ZED)
    store_left(1, normed[...], 2, seconds, NORMED)
    store_left(2, merged[...], 0, firsts, MERGED)

    grad_zed = nt(gp[...], up[...]).astype(BF16).astype(F32)
    normed_mid, rstd = normalized(middle[...])
    parts[0:1, :] = jnp.sum(grad_zed * normed_mid, 0, keepdims=True)
    parts[1:2, :] = jnp.sum(grad_zed, 0, keepdims=True)
    grad_norm = grad_zed * ln_gain[...]
    grad = cot[...].astype(F32) + rstd * (
        grad_norm
        - jnp.mean(grad_norm, -1, keepdims=True)
        - normed_mid * jnp.mean(grad_norm * normed_mid, -1, keepdims=True)
    )
    ga[...] = grad.astype(BF16)
    stores.append(load(parts, parts_out, out_sem.at[3]))
    stores.append(load(ga, first_other.at[pl.ds(GA, T), :], out_sem.at[4]))
    for j in range(NEST):
        wait(act_stores(j) + [act_store(j), gp_store(j)])
    wait(stores)


def front(lengths, heads, norm_gain, inverse, ln_gain, ln_bias, router, bucket, *arrays):
    row_b = sds((T, D), BF16)
    scratch = [
        sds((8, D), F32),
        row_b,
        row_b,
        sds((3, D, D), BF16),
        sds((D, D), BF16),
        sds((D, FF), BF16),
        sds((FF, D), BF16),
        sds((3, T, D), BF16),
        row_b,
        row_b,
        row_b,
        row_b,
        sds((T, FF), BF16),
        sds((2, 512, D), BF16),
        sds((T, FF), BF16),
        sds((4, 4, 4, 2, 8, T), F32),
        sds((2, 3, 128, D), BF16),
        sds((T, D), F32),
        row_b,
        sds((T, T), F32),
        sds((T, GW), jnp.int32),
        sds((T, 1), jnp.int32),
    ]
    semaphores = [(6,), (2, NEST), (3, NEST), (NEST,), (2, 3), (5,)]
    return call(
        front_kernel,
        "front",
        2 * T * D * (4 * D + 3 * FF),
        40 * MIB,
        58,
        in_specs=[smem()] * 2 + [vmem()] * 6 + [hbm()] * 6,
        out_specs=[hbm()] * 8,
        out_shape=[
            sds((8, D), F32),
            sds((FIRST_OWN, D), BF16),
            sds((FIRST, D), BF16),
            sds((SECOND_OWN, D), BF16),
            sds((SECOND, D), BF16),
            sds((3, T, D), BF16),
            sds((T, FF), BF16),
            sds((T, D), F32),
        ],
        scratch_shapes=[pltpu.VMEM(s.shape, s.dtype) for s in scratch]
        + [pltpu.SemaphoreType.DMA(s) for s in semaphores],
    )(lengths, heads, norm_gain, inverse, ln_gain, ln_bias, router, bucket, *arrays)


def back_kernel(
    lengths,
    heads,
    norm_gain,
    inverse,
    bucket,
    parts_hbm,
    first_other,
    qkv_hbm,
    tokens_hbm,
    wqkv_hbm,
    wo_hbm,
    third_mine,
    third_other,
    input_grad_out,
    parts,
    ga,
    qkv,
    input_grad,
    tokens,
    wqkv,
    wo,
    gqkv,
    lines_f,
    lines,
    bias,
    active,
    in_sem,
    w_sem,
    group_sem,
    out_sem,
):
    core = lax.axis_index("c")
    thirds = (third_mine, third_other)
    loads = [
        load(first_other.at[pl.ds(GA, T), :], ga, in_sem.at[0]),
        load(wo_hbm.at[pl.ds(0, GW), :], wo.at[pl.ds(0, GW), :], in_sem.at[1]),
        load(qkv_hbm.at[:, :, pl.ds(0, GW)], qkv.at[:, :, pl.ds(0, GW)], in_sem.at[2]),
    ]
    others = pl.ds(GW, D - GW)
    more = [
        pltpu.make_async_copy(wo_hbm.at[others, :], wo.at[others, :], in_sem.at[5]),
        pltpu.make_async_copy(qkv_hbm.at[:, :, others], qkv.at[:, :, others], in_sem.at[6]),
    ]
    late = [
        pltpu.make_async_copy(tokens_hbm, tokens, in_sem.at[3]),
        pltpu.make_async_copy(parts_hbm, parts, in_sem.at[7]),
    ]
    for n in range(3):
        src = wqkv_hbm.at[:, n * D : (n + 1) * D]
        late.append(pltpu.make_async_copy(src, wqkv.at[n], w_sem.at[n]))

    first = first_halves()
    scale = jnp.asarray(HD**-0.5, BF16)
    cosine, sine = rotary(lengths, inverse)
    sine = -sine
    query = lax.broadcasted_iota(jnp.int32, (T, T), 1)
    key = lax.broadcasted_iota(jnp.int32, (T, T), 0)
    bias[...] = jnp.where((key >= doc_start(lengths, query)) & (key <= query), 0.0, NEG)
    active[...] = of_doc(lengths, lax.broadcasted_iota(jnp.int32, (T, GW), 0), heads)
    wait(loads)
    for copy in more:
        copy.start()

    def group_stores(g):
        at = columns(g, GW)
        return [
            pltpu.make_async_copy(
                gqkv.at[n, :, at], third_other.at[pl.ds(GQKV + T * n, T), at], group_sem.at[n, g]
            )
            for n in range(3)
        ]

    def attend_back(g, carry):
        @pl.when(g == 1)
        def _():
            wait(more)
            start(late)

        at = columns(g, GW)
        gm = nt(ga[...], wo[at, :])
        gm = jnp.where(head_of(g) < active[...], gm, 0.0).astype(BF16)
        gms, queries = by_head(gm), by_head(qkv[0, :, at] * scale)
        k = qkv[1, :, at]
        s = nt(k, queries)
        grad_p = nt(qkv[2, :, at], gms)
        parts_p, parts_s = [], []
        for h in range(HEADS):
            one = s[:, T * h : T * h + T] + bias[...]
            e = jnp.exp(one - jnp.max(one, 0, keepdims=True))
            p = e / jnp.sum(e, 0, keepdims=True)
            grad = grad_p[:, T * h : T * h + T]
            parts_p.append(p.astype(BF16))
            grad = p * (grad - jnp.sum(p * grad, 0, keepdims=True))
            parts_s.append(grad.astype(BF16))
        grad_s = jnp.concatenate(parts_s, 1)
        grad_v = nn(jnp.concatenate(parts_p, 1), gms)
        grad_k = nn(grad_s, queries)
        wide = nn((k * scale).T, grad_s)
        grad_q = [wide[HD * h : HD * h + HD, T * h : T * h + T] for h in range(HEADS)]
        grad_q = jnp.concatenate(grad_q, 0).T
        gqkv[0, :, at] = turned(grad_q, cosine, sine, first).astype(BF16)
        gqkv[1, :, at] = turned(grad_k, cosine, sine, first).astype(BF16)
        gqkv[2, :, at] = grad_v.astype(BF16)
        for copy in group_stores(g):
            copy.start()
        return carry

    lax.fori_loop(0, GROUPS, attend_back, 0)

    wait(late)
    grad_normed = nt(gqkv[0], wqkv[0]) + nt(gqkv[1], wqkv[1]) + nt(gqkv[2], wqkv[2])
    resid = tokens[...].astype(F32)
    rscale = lax.rsqrt(jnp.mean(resid * resid, -1, keepdims=True) + EPS)
    unit = resid * rscale
    gain_part = jnp.sum(grad_normed * unit, 0, keepdims=True)
    grad_unit = grad_normed * norm_gain[...]
    input_grad[...] = ga[...].astype(F32) + rscale * (
        grad_unit - unit * jnp.mean(grad_unit * unit, -1, keepdims=True)
    )
    stores = [load(input_grad, input_grad_out, out_sem.at[0])]

    item = lax.broadcasted_iota(jnp.int32, (128, 1), 0)
    count = jnp.zeros((128, 1), jnp.int32)
    for n in range(NEST):
        total = jnp.sum((bucket[...] == n).astype(jnp.int32), 1, keepdims=True)
        at = item - 3 - BITS * n
        bit = lax.shift_right_logical(total, jnp.clip(at, 0, BITS - 1)) & 1
        count = jnp.where((at >= 0) & (at < BITS), bit, count)
    wide = jnp.where(item == 0, gain_part, jnp.where(item == 1, parts[0:1, :], parts[1:2, :]))
    lines_f[...] = jnp.where(item < 3, wide, count.astype(F32)).T.reshape(lines_f.shape)
    for side, ref in enumerate(thirds):
        half = core if side == 0 else 1 - core
        for i in range(4):
            part = lines_f[:, :, i, half].reshape(128, 128).astype(BF16)
            lines[side, :, pl.ds(128 * i, 128)] = part
        dst = ref.at[pl.ds(LINES, 128), pl.ds(0, 512)]
        stores.append(load(lines.at[side], dst, out_sem.at[1 + side]))
    for g in range(GROUPS):
        wait(group_stores(g))
    wait(stores)


def back(lengths, heads, norm_gain, inverse, bucket, parts, *arrays):
    scratch = [
        sds((8, D), F32),
        sds((T, D), BF16),
        sds((3, T, D), BF16),
        sds((T, D), F32),
        sds((T, D), BF16),
        sds((3, D, D), BF16),
        sds((D, D), BF16),
        sds((3, T, D), BF16),
        sds((4, 4, 4, 2, 8, 128), F32),
        sds((2, 128, 512), BF16),
        sds((T, T), F32),
        sds((T, GW), jnp.int32),
    ]
    return call(
        back_kernel,
        "back",
        2 * T * D * 4 * D + 10 * 16 * T * T * 256,
        18 * MIB,
        32,
        in_specs=[smem()] * 2 + [vmem()] * 3 + [hbm()] * 6,
        out_specs=[hbm()] * 3,
        out_shape=[sds((THIRD_OWN, D), BF16), sds((THIRD, D), BF16), sds((T, D), F32)],
        scratch_shapes=[pltpu.VMEM(s.shape, s.dtype) for s in scratch]
        + [pltpu.SemaphoreType.DMA(s) for s in [(8,), (3,), (3, GROUPS), (3,)]],
    )(lengths, heads, norm_gain, inverse, bucket, parts, *arrays)


def mixed_kernel(
    router, middle_hbm, act_hbm, down_hbm, after, mixed_out, middle, act, down, mixed, sem, ffn_sem
):
    loads = [load(middle_hbm, middle, sem.at[0])]
    stages = []
    for j in range(NEST):
        at = pl.ds(j * D, D)
        stages.append(
            [
                pltpu.make_async_copy(act_hbm.at[:, at], act.at[:, at], ffn_sem.at[0, j]),
                pltpu.make_async_copy(down_hbm.at[at, :], down.at[at, :], ffn_sem.at[1, j]),
            ]
        )
        start(stages[j])
    for stage in stages:
        wait(stage)
    branch = nn(act[...], down[...]).astype(BF16).astype(F32)
    wait(loads)
    mixed[...] = (middle[...] + upright(router[...]) * branch).astype(BF16)
    load(mixed, mixed_out, sem.at[1]).wait()


def mixed_output(router, middle, act, down, after):
    (mixed,) = call(
        mixed_kernel,
        "mixed_output",
        2 * T * D * FF,
        12 * MIB,
        24,
        in_specs=[vmem()] + [hbm()] * 4,
        out_specs=[hbm()],
        out_shape=[sds((T, D), BF16)],
        scratch_shapes=[
            pltpu.VMEM((T, D), F32),
            pltpu.VMEM((T, FF), BF16),
            pltpu.VMEM((FF, D), BF16),
            pltpu.VMEM((T, D), BF16),
            pltpu.SemaphoreType.DMA((2,)),
            pltpu.SemaphoreType.DMA((2, NEST)),
        ],
    )(router, middle, act, down, after)
    return mixed


def load_left(refs, at, rows, axis, left, sem):
    return [
        pltpu.make_async_copy(
            ref.at[pl.ds(at, rows), columns(block, T)],
            left.at[pl.ds(rows * i, rows), pl.ds(T * m, T)],
            sem.at[i, m],
        )
        for i, block in enumerate(block_order(axis))
        for m, ref in enumerate(refs)
    ]


def load_right(refs, at, right, sem):
    return [
        pltpu.make_async_copy(ref.at[pl.ds(at, T), :], right.at[pl.ds(T * m, T), :], sem.at[m])
        for m, ref in enumerate(refs)
    ]


def store_out(out, at, sent, kept, sem):
    return [
        load(out.at[pl.ds(2 * side, 2), :, at], ref.at[:, :, at], sem.at[side])
        for side, ref in enumerate((sent, kept))
    ]


def down_grad_kernel(
    own, one, two, sent, kept, act, merged, gb, ga, out, act_sem, merged_sem, gb_sem, ga_sem, sem
):
    refs, split = (one, two), (own, two)
    gb_loads = load_right(refs, GB, gb, gb_sem)
    act_loads = load_left(split, ACT, 512, "y", act, act_sem)
    ga_loads = load_right(refs, GA, ga, ga_sem)
    merged_loads = load_left(split, MERGED, 128, "y", merged, merged_sem)
    stages = [gb_loads + act_loads[:2], act_loads[2:4], act_loads[4:6], act_loads[6:]]
    stages.append(ga_loads + merged_loads)
    stores = []
    start(stages[0] + stages[1])
    wide = pl.ds(0, D)
    for i in range(4):
        wait(stages[i])
        start(stages[i + 2] if i < 3 else [])
        out[i, :, wide] = nn(act[pl.ds(512 * i, 512), :], gb[...]).astype(BF16)
        dst = (sent, kept)[i // 2].at[i % 2, :, wide]
        stores.append(load(out.at[i, :, wide], dst, sem.at[0, i]))
    wait(stages[4])
    part = nn(merged[...], ga[...])
    more = pl.ds(D, T)
    for i in range(4):
        rows = part[128 * i : 128 * i + 128].reshape(16, 8, D)
        quarters = [rows[:, :, T * q : T * q + T] for q in range(4)]
        out[i, :, more] = jnp.concatenate(quarters, 1).reshape(512, T).astype(BF16)
    stores += store_out(out, more, sent, kept, sem.at[1])
    wait(stores)


def down_grads(own, one, two):
    part = sds((2, 512, D + T), BF16)
    return call(
        down_grad_kernel,
        "down_and_out_grad",
        2 * T * D * (FF + D),
        10 * MIB,
        24,
        (2,),
        in_specs=[hbm()] * 3,
        out_specs=[hbm()] * 2,
        out_shape=[part, part],
        scratch_shapes=[
            pltpu.VMEM((FF // 2, 2 * T), BF16),
            pltpu.VMEM((512, 2 * T), BF16),
            pltpu.VMEM((2 * T, D), BF16),
            pltpu.VMEM((2 * T, D), BF16),
            pltpu.VMEM((4, 512, D + T), BF16),
            pltpu.SemaphoreType.DMA((4, 2)),
            pltpu.SemaphoreType.DMA((4, 2)),
            pltpu.SemaphoreType.DMA((2,)),
            pltpu.SemaphoreType.DMA((2,)),
            pltpu.SemaphoreType.DMA((2, 4)),
        ],
    )(own, one, two)


def up_and_qkv_kernel(
    own,
    one,
    two,
    late_own,
    three,
    four,
    after,
    up_sent,
    up_kept,
    qkv_sent,
    qkv_kept,
    zed,
    normed,
    gp,
    gqkv,
    lines,
    up_out,
    qkv_out,
    zed_sem,
    normed_sem,
    gp_sem,
    gqkv_sem,
    line_sem,
    up_sem,
    qkv_sem,
):
    refs, split = (one, two), (own, two)
    late = (three, four)
    zed_loads = load_left(split, ZED, 128, "x", zed, zed_sem)
    gp_loads = [load_right(refs, GP + T * n, gp.at[n], gp_sem.at[n]) for n in range(4)]
    line_loads = [
        pltpu.make_async_copy(
            ref.at[pl.ds(LINES, 128), columns(block, 128)],
            lines.at[i, m],
            line_sem.at[i, m],
        )
        for i, block in enumerate(block_order("z"))
        for m, ref in enumerate((late_own, four))
    ]
    normed_loads = load_left(split, NORMED, 128, "z", normed, normed_sem)
    gqkv_loads = [load_right(late, GQKV + T * n, gqkv.at[n], gqkv_sem.at[n]) for n in range(3)]
    stages = [zed_loads + gp_loads[0], *gp_loads[1:], normed_loads + gqkv_loads[0]]
    stages += [gqkv_loads[1], gqkv_loads[2] + line_loads, []]
    stores = []
    start(stages[0] + stages[1])
    for n in range(4):
        wait(stages[n])
        start(stages[n + 2])
        at = pl.ds(n * D, D)
        up_out[:, :, at] = nn(zed[...], gp[n]).astype(BF16).reshape(4, 128, D)
        stores += store_out(up_out, at, up_sent, up_kept, up_sem.at[n])
    for n in range(3):
        wait(stages[4 + n])
        start(stages[6] if n == 0 else [])
        at = pl.ds(n * D, D)
        qkv_out[:, :, at] = nn(normed[...], gqkv[n]).astype(BF16).reshape(4, 128, D)
        stores += store_out(qkv_out, at, qkv_sent, qkv_kept, qkv_sem.at[n])
    at = pl.ds(3 * D, 128)
    qkv_out[:, :, at] = (lines[:, 0].astype(F32) + lines[:, 1].astype(F32)).astype(BF16)
    stores += store_out(qkv_out, at, qkv_sent, qkv_kept, qkv_sem.at[3])
    wait(stores)


def up_and_qkv_grads(own, one, two, late_own, three, four, after):
    up = sds((2, 128, FF), BF16)
    qkv = sds((2, 128, 3 * D + 128), BF16)
    return call(
        up_and_qkv_kernel,
        "up_and_qkv_grad",
        2 * T * D * (FF + 3 * D),
        16 * MIB,
        28,
        (2, 5),
        in_specs=[hbm()] * 7,
        out_specs=[hbm()] * 4,
        out_shape=[up, up, qkv, qkv],
        scratch_shapes=[
            pltpu.VMEM((512, 2 * T), BF16),
            pltpu.VMEM((512, 2 * T), BF16),
            pltpu.VMEM((4, 2 * T, D), BF16),
            pltpu.VMEM((3, 2 * T, D), BF16),
            pltpu.VMEM((4, 2, 128, 128), BF16),
            pltpu.VMEM((4, 128, FF), BF16),
            pltpu.VMEM((4, 128, 3 * D + 128), BF16),
            pltpu.SemaphoreType.DMA((4, 2)),
            pltpu.SemaphoreType.DMA((4, 2)),
            pltpu.SemaphoreType.DMA((4, 2)),
            pltpu.SemaphoreType.DMA((3, 2)),
            pltpu.SemaphoreType.DMA((4, 2)),
            pltpu.SemaphoreType.DMA((4, 2)),
            pltpu.SemaphoreType.DMA((4, 2)),
        ],
    )(own, one, two, late_own, three, four, after)


def swap_cores(array):
    return lax.ppermute(array, "c", [(0, 1), (1, 0)])


def pairs(mask_0, mask_1):
    perm = []
    for p in range(4):
        perm.append((2 * p, 2 * (p ^ mask_0)))
        perm.append((2 * p + 1, 2 * (p ^ mask_1) + 1))
    return perm


def ordered(token, *arrays):
    return lax.optimization_barrier((*arrays, token))[:-1]


def chain(sent, kept, axes, shape, finish):
    left = [axis for axis in ("y", "x", "z") if axis != axes[0]]
    for axis in axes:
        got = lax.ppermute(sent, (axis, "c"), pairs(1, 3))
        token = yield sent
        got, kept = ordered(token, got, kept)
        more = (got[1].astype(F32) + kept[1].astype(F32)).astype(BF16)
        got_2 = lax.ppermute(more, (axis, "c"), pairs(3, 1))
        token = yield more
        got, kept, got_2 = ordered(token, got, kept, got_2)
        terms = [got.reshape(2, *shape), kept.reshape(2, *shape), got_2.reshape(1, *shape)]
        if not left:
            return finish(*terms)
        following = axes[axes.index(axis) + 1]
        dim = left.index(following)
        left.pop(dim)
        shape = shape[:dim] + shape[dim + 1 :]

        def block(at):
            total = 0.0
            for term in terms:
                start = [0] * term.ndim
                start[1 + dim] = at
                sizes = (1,) + term.shape[1 : 1 + dim] + (1,) + term.shape[2 + dim :]
                total = total + lax.dynamic_slice(term, start, sizes).astype(F32)
            return total.reshape(shape)

        first, across, own, second = [block(at) for at in block_order(following)]
        sent = jnp.stack([first, across]).astype(BF16)
        kept = jnp.stack([own, second])


def total(terms, *at):
    return sum(term[(0, *at)].astype(F32) for term in terms)


def take_turns(token, turns, **chains):
    for steps in chains.values():
        next(steps)
    for turn in turns:
        token = next_step(chains[turn], token)


def next_step(steps, token):
    try:
        return steps.send(token)
    except StopIteration as end:
        return end.value


def body(
    tokens,
    norm_gain,
    qkv_weight,
    out_weight,
    ln_gain,
    ln_bias,
    up_weight,
    down_weight,
    buckets,
    router_prob,
    heads_active,
    doc_lengths,
    cotangent,
):
    norm_gain, ln_gain, ln_bias = [v.reshape(1, D) for v in (norm_gain, ln_gain, ln_bias)]
    router = router_prob.reshape(1, T)
    levels = buckets.reshape(1, T)
    inverse = np.tile(10000.0 ** (-2.0 * np.arange(HD // 2) / HD), 4).reshape(1, 128)
    inverse = jnp.asarray(inverse, F32)

    parts, first, first_other, second, second_other, qkv, act, middle = front(
        doc_lengths,
        heads_active,
        norm_gain,
        inverse,
        ln_gain,
        ln_bias,
        router,
        levels,
        tokens,
        cotangent,
        qkv_weight,
        out_weight,
        up_weight,
        down_weight,
    )
    first_2, second_2 = swap_cores(first_other), swap_cores(second_other)
    third, third_other, input_grad = back(
        doc_lengths,
        heads_active,
        norm_gain,
        inverse,
        levels,
        parts,
        first_other,
        qkv,
        tokens,
        qkv_weight,
        out_weight,
    )
    third_2 = swap_cores(third_other)
    first_2, _ = lax.optimization_barrier((first_2, third))
    down_sent, down_kept = down_grads(first, first_other, first_2)
    up_sent, up_kept, qkv_sent, qkv_kept = up_and_qkv_grads(
        second, second_other, second_2, third, third_other, third_2, down_sent
    )

    mixed = mixed_output(router, middle, act, down_weight, qkv_sent)

    every = slice(None)
    grads = {}

    def down_done(*terms):
        grads["down"] = total(terms, every, slice(0, D))
        out = total(terms, every, slice(D, D + T))
        grads["out"] = out.reshape(4, 8, T).transpose(1, 0, 2).reshape(8, D)
        grads["down"], grads["out"] = lax.optimization_barrier((grads["down"], grads["out"]))
        return grads["out"]

    def up_done(*terms):
        grads["up"] = total(terms)
        return grads["up"]

    def qkv_done(*terms):
        grads["qkv"] = total(terms, every, slice(0, 3 * D))
        line = total(terms, every, slice(3 * D, 3 * D + 128))
        grads["gains"] = [line[:, n] for n in range(3)]
        bits = line[0, 3 : 3 + BITS * NEST].astype(jnp.int32).reshape(NEST, BITS)
        grads["counts"] = jnp.sum(bits << jnp.arange(BITS, dtype=jnp.int32)[None, :], 1)
        done = (grads["qkv"], grads["counts"], *grads["gains"])
        grads["qkv"], grads["counts"], *grads["gains"] = lax.optimization_barrier(done)
        return grads["qkv"]

    take_turns(
        mixed,
        TURNS,
        d=chain(down_sent, down_kept, "yxz", (4, 4, 32, D + T), down_done),
        u=chain(up_sent, up_kept, "xyz", (4, 4, 8, FF), up_done),
        q=chain(qkv_sent, qkv_kept, "zyx", (4, 4, 8, 3 * D + 128), qkv_done),
    )
    gain_grad, ln_gain_grad, ln_bias_grad = grads["gains"]
    return (
        mixed,
        input_grad,
        gain_grad,
        grads["qkv"],
        grads["out"],
        ln_gain_grad,
        ln_bias_grad,
        grads["up"],
        grads["down"],
        grads["counts"],
    )


def solution(mesh):
    finer = Mesh(mesh.devices.reshape(4, 4, 4, 2), AX)
    rows = P(AX, None)
    return jax.shard_map(
        body,
        mesh=finer,
        in_specs=(rows, P(), P(), P(), P(), P(), P(), P(), rows, P(AX), rows, rows, rows),
        out_specs=(rows, rows, P(AX), rows, rows, P(AX), P(AX), rows, rows, P()),
        check_vma=False,
    )
```

```python
import jax
import jax.numpy as jnp
import numpy as np
from jax import lax
from jax.experimental import pallas as pl
from jax.experimental.pallas import tpu as pltpu
from jax.sharding import Mesh
from jax.sharding import PartitionSpec as P

HD = 64
NEST = 4
AX = ("y", "x", "z", "c")

NEG = -1e30
EPS = 1e-05
F32 = jnp.float32
BF16 = jnp.bfloat16
T = 256
D = 1024
FF = 4096
GW = 256
GROUPS = D // GW
HEADS = GW // HD
ACT, MERGED, FIRST_OWN, GB, GA, FIRST = 0, 512, 640, 640, 896, 1152
ZED, NORMED, ZED_Z, SECOND_OWN, GP, SECOND = 0, 128, 256, 384, 384, 1408
LINES, THIRD_OWN, GQKV, THIRD = 0, 128, 128, 896
TURNS = "dquqduqduqduqdudqu"
UP = 3584
BITS = 9
MIB = 1024 * 1024


def nn(a, b):
    return lax.dot_general(a, b, (((1,), (0,)), ((), ())), preferred_element_type=F32)


def nt(a, b):
    return lax.dot_general(a, b, (((1,), (1,)), ((), ())), preferred_element_type=F32)


def tn(a, b):
    return lax.dot_general(a, b, (((0,), (0,)), ((), ())), preferred_element_type=F32)


def sds(shape, dtype):
    return jax.ShapeDtypeStruct(shape, dtype)


def smem():
    return pl.BlockSpec(memory_space=pltpu.SMEM)


def vmem():
    return pl.BlockSpec(memory_space=pltpu.VMEM)


def hbm():
    return pl.BlockSpec(memory_space=pltpu.HBM)


def call(kernel, name, flops, moved, room, anywhere=(), **kw):
    def in_hbm(spec):
        return spec.memory_space == pltpu.HBM

    kw["out_shape"] = [
        pltpu.HBM(s.shape, s.dtype) if in_hbm(spec) else s
        for s, spec in zip(kw["out_shape"], kw["out_specs"])
    ]
    run = pl.pallas_call(
        kernel,
        name=name,
        compiler_params=pltpu.CompilerParams(vmem_limit_bytes=room * MIB),
        cost_estimate=pl.CostEstimate(flops=flops, bytes_accessed=moved, transcendentals=0),
        **kw,
    )

    def placed(*args):
        return run(
            *(
                pltpu.with_memory_space_constraint(arg, pltpu.HBM)
                if in_hbm(spec) and n not in anywhere
                else arg
                for n, (arg, spec) in enumerate(zip(args, kw["in_specs"]))
            )
        )

    return placed


def first_halves():
    return lax.broadcasted_iota(jnp.int32, (T, 128), 1) % HD < HD // 2


def head_of(g):
    return HEADS * g + lax.broadcasted_iota(jnp.int32, (T, GW), 1) // HD


def by_head(x):
    lane = lax.broadcasted_iota(jnp.int32, (T, GW), 1)
    zero = jnp.zeros((T, GW), x.dtype)
    own = [(lane >= HD * h) & (lane < HD * h + HD) for h in range(HEADS)]
    return jnp.concatenate([jnp.where(keep, x, zero) for keep in own], 0)


def turned(x, cosine, sine, first):
    parts = []
    for at in range(0, x.shape[1], 128):
        part = x[:, at : at + 128]
        other = jnp.where(first, pltpu.roll(part, 128 - HD // 2, 1), pltpu.roll(part, HD // 2, 1))
        parts.append(part * cosine + other * sine)
    return jnp.concatenate(parts, 1)


def doc_ends(lengths):
    return lengths[0, 0], lengths[0, 0] + lengths[0, 1]


def doc_start(lengths, place):
    end_0, end_1 = doc_ends(lengths)
    return jnp.where(place >= end_1, end_1, jnp.where(place >= end_0, end_0, 0))


def of_doc(lengths, place, values):
    end_0, end_1 = doc_ends(lengths)
    late = jnp.where(place >= end_1, values[0, 2], values[0, 1])
    return jnp.where(place >= end_0, late, values[0, 0])


def normalized(middle):
    shifted = middle - jnp.mean(middle, -1, keepdims=True)
    rstd = lax.rsqrt(jnp.mean(shifted * shifted, -1, keepdims=True) + EPS)
    return shifted * rstd, rstd


def block_order(axis):
    p = lax.axis_index(axis)
    core = lax.axis_index("c")
    return [p ^ (1 + 2 * core), p ^ 2, p, p ^ (3 - 2 * core)]


def load(src, dst, sem):
    copy = pltpu.make_async_copy(src, dst, sem)
    copy.start()
    return copy


def columns(j, size):
    if isinstance(j, int):
        return pl.ds(j * size, size)
    return pl.ds(pl.multiple_of(j * size, size), size)


def upright(row):
    return jnp.broadcast_to(row, (8, T)).T[:, :1]


def places():
    return lax.broadcasted_iota(jnp.int32, (T, 128), 0)


def rotary(lengths, inverse):
    phase = (places() - doc_start(lengths, places())).astype(F32) * inverse[...]
    sine = jnp.sin(phase)
    return jnp.cos(phase), jnp.where(first_halves(), -sine, sine)


def start(copies):
    for copy in copies:
        copy.start()


def wait(copies):
    for copy in copies:
        copy.wait()


def front_kernel(
    lengths,
    heads,
    norm_gain,
    inverse,
    ln_gain,
    ln_bias,
    router,
    bucket,
    tokens_hbm,
    cot_hbm,
    wqkv_hbm,
    wo_hbm,
    up_hbm,
    down_hbm,
    parts_out,
    first_mine,
    first_other,
    second_mine,
    second_other,
    qkv_out,
    act_out,
    middle_out,
    parts,
    tokens,
    cot,
    wqkv,
    wo,
    up,
    down,
    qkv,
    normed,
    merged,
    zed,
    gb,
    act,
    act_turned,
    gp,
    turned_f,
    left,
    middle,
    ga,
    bias,
    active,
    level,
    in_sem,
    ffn_sem,
    act_sem,
    gp_sem,
    left_sem,
    out_sem,
):
    core = lax.axis_index("c")
    firsts, seconds = (first_mine, first_other), (second_mine, second_other)
    loads = [load(tokens_hbm, tokens, in_sem.at[0])]
    for n in range(3):
        src = wqkv_hbm.at[:, n * D : (n + 1) * D]
        loads.append(pltpu.make_async_copy(src, wqkv.at[n], in_sem.at[1 + n]))
    loads[1].start()

    def ffn_loads(j):
        at = columns(j, D)
        return (
            pltpu.make_async_copy(up_hbm.at[:, at], up.at[:, at], ffn_sem.at[0, j]),
            pltpu.make_async_copy(down_hbm.at[at, :], down.at[at, :], ffn_sem.at[1, j]),
        )

    stores = []

    def store_left(n, value, axis, refs, at):
        turned_f[...] = value.astype(F32).T.reshape(turned_f.shape)
        for side, ref in enumerate(refs):
            half = core if side == 0 else 1 - core
            for i in range(4):
                if axis == 0:
                    rows = turned_f[i, :, :, half]
                elif axis == 1:
                    rows = turned_f[:, i, :, half]
                else:
                    rows = turned_f[:, :, i, half]
                left[side, n, :, pl.ds(T * i, T)] = rows.reshape(128, T).astype(BF16)
            dst = ref.at[pl.ds(at, 128), :]
            stores.append(load(left.at[side, n], dst, left_sem.at[side, n]))

    first = first_halves()
    scale = jnp.asarray(HD**-0.5, BF16)
    cosine, sine = rotary(lengths, inverse)
    row = lax.broadcasted_iota(jnp.int32, (T, T), 0)
    col = lax.broadcasted_iota(jnp.int32, (T, T), 1)
    bias[...] = jnp.where((col >= doc_start(lengths, row)) & (col <= row), 0.0, NEG)
    active[...] = of_doc(lengths, lax.broadcasted_iota(jnp.int32, (T, GW), 0), heads)
    level[...] = upright(bucket[...])
    prob = upright(router[...])

    loads[0].wait()
    start(loads[2:4])
    resid = tokens[...].astype(F32)
    rscale = lax.rsqrt(jnp.mean(resid * resid, -1, keepdims=True) + EPS)
    normed[...] = (resid * rscale * norm_gain[...]).astype(BF16)
    for n in range(3):
        loads[1 + n].wait()
        if n == 1:
            loads.append(load(cot_hbm, cot, in_sem.at[4]))
        if n == 2:
            loads.append(load(wo_hbm, wo, in_sem.at[5]))
            for copy in ffn_loads(0) + ffn_loads(1):
                copy.start()
        part = nn(normed[...], wqkv[n])
        qkv[n] = (turned(part, cosine, sine, first) if n < 2 else part).astype(BF16)
    stores.append(load(qkv, qkv_out, out_sem.at[0]))

    def attend(g, carry):
        at = columns(g, GW)
        keys, values = by_head(qkv[1, :, at]), by_head(qkv[2, :, at])
        s = nt(qkv[0, :, at] * scale, keys)
        parts = []
        for h in range(HEADS):
            one = s[:, T * h : T * h + T] + bias[...]
            e = jnp.exp(one - jnp.max(one, -1, keepdims=True))
            parts.append((e / jnp.sum(e, -1, keepdims=True)).astype(BF16))
        out = nn(jnp.concatenate(parts, 1), values)
        merged[:, at] = jnp.where(head_of(g) < active[...], out, 0.0).astype(BF16)

        @pl.when((g > 0) & (g < NEST - 1))
        def _():
            for copy in ffn_loads(g + 1):
                copy.start()

        return carry

    lax.fori_loop(0, GROUPS, attend, 0)
    loads[5].wait()
    middle[...] = tokens[...].astype(F32) + nn(merged[...], wo[...])
    stores.append(load(middle, middle_out, out_sem.at[1]))
    normed_mid, _ = normalized(middle[...])
    zed[...] = (normed_mid * ln_gain[...] + ln_bias[...]).astype(BF16)
    loads[4].wait()
    gb[...] = (cot[...].astype(F32) * prob).astype(BF16)
    stores.append(load(gb, first_other.at[pl.ds(GB, T), :], out_sem.at[2]))

    def act_stores(j):
        at = (pl.ds(ACT, 512), columns(j, T))
        return [
            pltpu.make_async_copy(act_turned.at[side, :, at[1]], ref.at[at], act_sem.at[side, j])
            for side, ref in enumerate(firsts)
        ]

    def act_store(j):
        at = columns(j, D)
        return pltpu.make_async_copy(act.at[:, at], act_out.at[:, at], act_sem.at[2, j])

    def gp_store(j):
        rows = pl.ds(pl.multiple_of(GP + T * j, 128), T)
        return pltpu.make_async_copy(gp.at[:, columns(j, D)], second_other.at[rows, :], gp_sem.at[j])

    def hidden(j, carry):
        copy_up, copy_down = ffn_loads(j)
        at = columns(j, D)
        copy_up.wait()
        r = jnp.where(level[...] >= j, jnp.maximum(nn(zed[...], up[:, at]), 0.0), 0.0)
        a = (r * r).astype(BF16)
        act[:, at] = a
        by_core = a.T.reshape(16, 2, 32, T)
        low_rows, high_rows = by_core[:, 0].reshape(512, T), by_core[:, 1].reshape(512, T)
        act_store(j).start()
        act_turned[0, :, columns(j, T)] = jnp.where(core == 0, low_rows, high_rows)
        act_turned[1, :, columns(j, T)] = jnp.where(core == 0, high_rows, low_rows)
        for copy in act_stores(j):
            copy.start()
        copy_down.wait()
        gp[:, at] = (nt(gb[...], down[at, :]) * 2.0 * r).astype(BF16)
        gp_store(j).start()
        return carry

    lax.fori_loop(0, NEST, hidden, 0)
    store_left(0, zed[...], 1, seconds, ZED)
    store_left(3, zed[...], 2, seconds, ZED_Z)
    store_left(1, normed[...], 2, seconds, NORMED)
    store_left(2, merged[...], 0, firsts, MERGED)

    grad_zed = nt(gp[...], up[...]).astype(BF16).astype(F32)
    normed_mid, rstd = normalized(middle[...])
    parts[0:1, :] = jnp.sum(grad_zed * normed_mid, 0, keepdims=True)
    parts[1:2, :] = jnp.sum(grad_zed, 0, keepdims=True)
    grad_norm = grad_zed * ln_gain[...]
    grad = cot[...].astype(F32) + rstd * (
        grad_norm
        - jnp.mean(grad_norm, -1, keepdims=True)
        - normed_mid * jnp.mean(grad_norm * normed_mid, -1, keepdims=True)
    )
    ga[...] = grad.astype(BF16)
    stores.append(load(parts, parts_out, out_sem.at[3]))
    stores.append(load(ga, first_other.at[pl.ds(GA, T), :], out_sem.at[4]))
    for j in range(NEST):
        wait(act_stores(j) + [act_store(j), gp_store(j)])
    wait(stores)


def front(lengths, heads, norm_gain, inverse, ln_gain, ln_bias, router, bucket, *arrays):
    row_b = sds((T, D), BF16)
    scratch = [
        sds((8, D), F32),
        row_b,
        row_b,
        sds((3, D, D), BF16),
        sds((D, D), BF16),
        sds((D, FF), BF16),
        sds((FF, D), BF16),
        sds((3, T, D), BF16),
        row_b,
        row_b,
        row_b,
        row_b,
        sds((T, FF), BF16),
        sds((2, 512, D), BF16),
        sds((T, FF), BF16),
        sds((4, 4, 4, 2, 8, T), F32),
        sds((2, 4, 128, D), BF16),
        sds((T, D), F32),
        row_b,
        sds((T, T), F32),
        sds((T, GW), jnp.int32),
        sds((T, 1), jnp.int32),
    ]
    semaphores = [(6,), (2, NEST), (3, NEST), (NEST,), (2, 4), (5,)]
    return call(
        front_kernel,
        "front",
        2 * T * D * (4 * D + 3 * FF),
        40 * MIB,
        58,
        in_specs=[smem()] * 2 + [vmem()] * 6 + [hbm()] * 6,
        out_specs=[hbm()] * 8,
        out_shape=[
            sds((8, D), F32),
            sds((FIRST_OWN, D), BF16),
            sds((FIRST, D), BF16),
            sds((SECOND_OWN, D), BF16),
            sds((SECOND, D), BF16),
            sds((3, T, D), BF16),
            sds((T, FF), BF16),
            sds((T, D), F32),
        ],
        scratch_shapes=[pltpu.VMEM(s.shape, s.dtype) for s in scratch]
        + [pltpu.SemaphoreType.DMA(s) for s in semaphores],
    )(lengths, heads, norm_gain, inverse, ln_gain, ln_bias, router, bucket, *arrays)


def back_kernel(
    lengths,
    heads,
    norm_gain,
    inverse,
    bucket,
    parts_hbm,
    first_other,
    qkv_hbm,
    tokens_hbm,
    wqkv_hbm,
    wo_hbm,
    third_mine,
    third_other,
    input_grad_out,
    parts,
    ga,
    qkv,
    input_grad,
    tokens,
    wqkv,
    wo,
    gqkv,
    lines_f,
    lines,
    bias,
    active,
    in_sem,
    w_sem,
    group_sem,
    out_sem,
):
    core = lax.axis_index("c")
    thirds = (third_mine, third_other)
    loads = [
        load(first_other.at[pl.ds(GA, T), :], ga, in_sem.at[0]),
        load(wo_hbm.at[pl.ds(0, GW), :], wo.at[pl.ds(0, GW), :], in_sem.at[1]),
        load(qkv_hbm.at[:, :, pl.ds(0, GW)], qkv.at[:, :, pl.ds(0, GW)], in_sem.at[2]),
    ]
    others = pl.ds(GW, D - GW)
    more = [
        pltpu.make_async_copy(wo_hbm.at[others, :], wo.at[others, :], in_sem.at[5]),
        pltpu.make_async_copy(qkv_hbm.at[:, :, others], qkv.at[:, :, others], in_sem.at[6]),
    ]
    late = [
        pltpu.make_async_copy(tokens_hbm, tokens, in_sem.at[3]),
        pltpu.make_async_copy(parts_hbm, parts, in_sem.at[7]),
    ]
    for n in range(3):
        src = wqkv_hbm.at[:, n * D : (n + 1) * D]
        late.append(pltpu.make_async_copy(src, wqkv.at[n], w_sem.at[n]))

    first = first_halves()
    scale = jnp.asarray(HD**-0.5, BF16)
    cosine, sine = rotary(lengths, inverse)
    sine = -sine
    query = lax.broadcasted_iota(jnp.int32, (T, T), 1)
    key = lax.broadcasted_iota(jnp.int32, (T, T), 0)
    bias[...] = jnp.where((key >= doc_start(lengths, query)) & (key <= query), 0.0, NEG)
    active[...] = of_doc(lengths, lax.broadcasted_iota(jnp.int32, (T, GW), 0), heads)
    wait(loads)
    for copy in more:
        copy.start()

    def group_stores(g):
        at = columns(g, GW)
        return [
            pltpu.make_async_copy(
                gqkv.at[n, :, at], third_other.at[pl.ds(GQKV + T * n, T), at], group_sem.at[n, g]
            )
            for n in range(3)
        ]

    def attend_back(g, carry):
        @pl.when(g == 1)
        def _():
            wait(more)
            start(late)

        at = columns(g, GW)
        gm = nt(ga[...], wo[at, :])
        gm = jnp.where(head_of(g) < active[...], gm, 0.0).astype(BF16)
        gms, queries = by_head(gm), by_head(qkv[0, :, at] * scale)
        k = qkv[1, :, at]
        s = nt(k, queries)
        grad_p = nt(qkv[2, :, at], gms)
        parts_p, parts_s = [], []
        for h in range(HEADS):
            one = s[:, T * h : T * h + T] + bias[...]
            e = jnp.exp(one - jnp.max(one, 0, keepdims=True))
            p = e / jnp.sum(e, 0, keepdims=True)
            grad = grad_p[:, T * h : T * h + T]
            parts_p.append(p.astype(BF16))
            grad = p * (grad - jnp.sum(p * grad, 0, keepdims=True))
            parts_s.append(grad.astype(BF16))
        grad_s = jnp.concatenate(parts_s, 1)
        grad_v = nn(jnp.concatenate(parts_p, 1), gms)
        grad_k = nn(grad_s, queries)
        wide = nn((k * scale).T, grad_s)
        grad_q = [wide[HD * h : HD * h + HD, T * h : T * h + T] for h in range(HEADS)]
        grad_q = jnp.concatenate(grad_q, 0).T
        gqkv[0, :, at] = turned(grad_q, cosine, sine, first).astype(BF16)
        gqkv[1, :, at] = turned(grad_k, cosine, sine, first).astype(BF16)
        gqkv[2, :, at] = grad_v.astype(BF16)
        for copy in group_stores(g):
            copy.start()
        return carry

    lax.fori_loop(0, GROUPS, attend_back, 0)

    wait(late)
    grad_normed = nt(gqkv[0], wqkv[0]) + nt(gqkv[1], wqkv[1]) + nt(gqkv[2], wqkv[2])
    resid = tokens[...].astype(F32)
    rscale = lax.rsqrt(jnp.mean(resid * resid, -1, keepdims=True) + EPS)
    unit = resid * rscale
    gain_part = jnp.sum(grad_normed * unit, 0, keepdims=True)
    grad_unit = grad_normed * norm_gain[...]
    input_grad[...] = ga[...].astype(F32) + rscale * (
        grad_unit - unit * jnp.mean(grad_unit * unit, -1, keepdims=True)
    )
    stores = [load(input_grad, input_grad_out, out_sem.at[0])]

    item = lax.broadcasted_iota(jnp.int32, (128, 1), 0)
    count = jnp.zeros((128, 1), jnp.int32)
    for n in range(NEST):
        total = jnp.sum((bucket[...] == n).astype(jnp.int32), 1, keepdims=True)
        at = item - 3 - BITS * n
        bit = lax.shift_right_logical(total, jnp.clip(at, 0, BITS - 1)) & 1
        count = jnp.where((at >= 0) & (at < BITS), bit, count)
    wide = jnp.where(item == 0, gain_part, jnp.where(item == 1, parts[0:1, :], parts[1:2, :]))
    lines_f[...] = jnp.where(item < 3, wide, count.astype(F32)).T.reshape(lines_f.shape)
    for side, ref in enumerate(thirds):
        half = core if side == 0 else 1 - core
        for i in range(4):
            part = lines_f[:, :, i, half].reshape(128, 128).astype(BF16)
            lines[side, :, pl.ds(128 * i, 128)] = part
        dst = ref.at[pl.ds(LINES, 128), pl.ds(0, 512)]
        stores.append(load(lines.at[side], dst, out_sem.at[1 + side]))
    for g in range(GROUPS):
        wait(group_stores(g))
    wait(stores)


def back(lengths, heads, norm_gain, inverse, bucket, parts, *arrays):
    scratch = [
        sds((8, D), F32),
        sds((T, D), BF16),
        sds((3, T, D), BF16),
        sds((T, D), F32),
        sds((T, D), BF16),
        sds((3, D, D), BF16),
        sds((D, D), BF16),
        sds((3, T, D), BF16),
        sds((4, 4, 4, 2, 8, 128), F32),
        sds((2, 128, 512), BF16),
        sds((T, T), F32),
        sds((T, GW), jnp.int32),
    ]
    return call(
        back_kernel,
        "back",
        2 * T * D * 4 * D + 10 * 16 * T * T * 256,
        18 * MIB,
        32,
        in_specs=[smem()] * 2 + [vmem()] * 3 + [hbm()] * 6,
        out_specs=[hbm()] * 3,
        out_shape=[sds((THIRD_OWN, D), BF16), sds((THIRD, D), BF16), sds((T, D), F32)],
        scratch_shapes=[pltpu.VMEM(s.shape, s.dtype) for s in scratch]
        + [pltpu.SemaphoreType.DMA(s) for s in [(8,), (3,), (3, GROUPS), (3,)]],
    )(lengths, heads, norm_gain, inverse, bucket, parts, *arrays)


def mixed_kernel(
    router, middle_hbm, act_hbm, down_hbm, after, mixed_out, middle, act, down, mixed, sem, ffn_sem
):
    loads = [load(middle_hbm, middle, sem.at[0])]
    stages = []
    for j in range(NEST):
        at = pl.ds(j * D, D)
        stages.append(
            [
                pltpu.make_async_copy(act_hbm.at[:, at], act.at[:, at], ffn_sem.at[0, j]),
                pltpu.make_async_copy(down_hbm.at[at, :], down.at[at, :], ffn_sem.at[1, j]),
            ]
        )
        start(stages[j])
    for stage in stages:
        wait(stage)
    branch = nn(act[...], down[...]).astype(BF16).astype(F32)
    wait(loads)
    mixed[...] = (middle[...] + upright(router[...]) * branch).astype(BF16)
    load(mixed, mixed_out, sem.at[1]).wait()


def mixed_output(router, middle, act, down, after):
    (mixed,) = call(
        mixed_kernel,
        "mixed_output",
        2 * T * D * FF,
        12 * MIB,
        16,
        in_specs=[vmem()] + [hbm()] * 4,
        out_specs=[hbm()],
        out_shape=[sds((T, D), BF16)],
        scratch_shapes=[
            pltpu.VMEM((T, D), F32),
            pltpu.VMEM((T, FF), BF16),
            pltpu.VMEM((FF, D), BF16),
            pltpu.VMEM((T, D), BF16),
            pltpu.SemaphoreType.DMA((2,)),
            pltpu.SemaphoreType.DMA((2, NEST)),
        ],
    )(router, middle, act, down, after)
    return mixed


def load_left(refs, at, rows, axis, left, sem):
    return [
        pltpu.make_async_copy(
            ref.at[pl.ds(at, rows), columns(block, T)],
            left.at[pl.ds(rows * i, rows), pl.ds(T * m, T)],
            sem.at[i, m],
        )
        for i, block in enumerate(block_order(axis))
        for m, ref in enumerate(refs)
    ]


def load_right(refs, at, right, sem):
    return [
        pltpu.make_async_copy(ref.at[pl.ds(at, T), :], right.at[pl.ds(T * m, T), :], sem.at[m])
        for m, ref in enumerate(refs)
    ]


def store_out(out, at, sent, kept, sem):
    return [
        load(out.at[pl.ds(2 * side, 2), :, at], ref.at[:, :, at], sem.at[side])
        for side, ref in enumerate((sent, kept))
    ]


def down_grad_kernel(
    own, one, two, sent, kept, act, merged, gb, ga, out, act_sem, merged_sem, gb_sem, ga_sem, sem
):
    refs, split = (one, two), (own, two)
    gb_loads = load_right(refs, GB, gb, gb_sem)
    act_loads = load_left(split, ACT, 512, "y", act, act_sem)
    ga_loads = load_right(refs, GA, ga, ga_sem)
    merged_loads = load_left(split, MERGED, 128, "y", merged, merged_sem)
    stages = [gb_loads + act_loads[:2], act_loads[2:4], act_loads[4:6], act_loads[6:]]
    stages.append(ga_loads + merged_loads)
    stores = []
    start(stages[0] + stages[1])
    wide = pl.ds(0, D)
    for i in range(4):
        wait(stages[i])
        start(stages[i + 2] if i < 3 else [])
        out[i, :, wide] = nn(act[pl.ds(512 * i, 512), :], gb[...]).astype(BF16)
        dst = (sent, kept)[i // 2].at[i % 2, :, wide]
        stores.append(load(out.at[i, :, wide], dst, sem.at[0, i]))
    wait(stages[4])
    part = nn(merged[...], ga[...])
    more = pl.ds(D, T)
    for i in range(4):
        rows = part[128 * i : 128 * i + 128].reshape(16, 8, D)
        quarters = [rows[:, :, T * q : T * q + T] for q in range(4)]
        out[i, :, more] = jnp.concatenate(quarters, 1).reshape(512, T).astype(BF16)
    stores += store_out(out, more, sent, kept, sem.at[1])
    wait(stores)


def down_grads(own, one, two):
    part = sds((2, 512, D + T), BF16)
    return call(
        down_grad_kernel,
        "down_and_out_grad",
        2 * T * D * (FF + D),
        10 * MIB,
        18,
        (2,),
        in_specs=[hbm()] * 3,
        out_specs=[hbm()] * 2,
        out_shape=[part, part],
        scratch_shapes=[
            pltpu.VMEM((FF // 2, 2 * T), BF16),
            pltpu.VMEM((512, 2 * T), BF16),
            pltpu.VMEM((2 * T, D), BF16),
            pltpu.VMEM((2 * T, D), BF16),
            pltpu.VMEM((4, 512, D + T), BF16),
            pltpu.SemaphoreType.DMA((4, 2)),
            pltpu.SemaphoreType.DMA((4, 2)),
            pltpu.SemaphoreType.DMA((2,)),
            pltpu.SemaphoreType.DMA((2,)),
            pltpu.SemaphoreType.DMA((2, 4)),
        ],
    )(own, one, two)


def up_and_qkv_kernel(
    own,
    one,
    two,
    late_own,
    three,
    four,
    after,
    up_sent,
    up_kept,
    qkv_sent,
    qkv_kept,
    zed,
    zed_z,
    normed,
    gp,
    gqkv,
    lines,
    up_out,
    qkv_out,
    zed_sem,
    zed_z_sem,
    normed_sem,
    gp_sem,
    gqkv_sem,
    line_sem,
    up_sem,
    qkv_sem,
):
    refs, split = (one, two), (own, two)
    late = (three, four)
    zed_loads = load_left(split, ZED, 128, "x", zed, zed_sem)
    gp_loads = [load_right(refs, GP + T * n, gp.at[n], gp_sem.at[n]) for n in range(4)]
    line_loads = [
        pltpu.make_async_copy(
            ref.at[pl.ds(LINES, 128), columns(block, 128)],
            lines.at[i, m],
            line_sem.at[i, m],
        )
        for i, block in enumerate(block_order("z"))
        for m, ref in enumerate((late_own, four))
    ]
    zed_z_loads = load_left(split, ZED_Z, 128, "z", zed_z, zed_z_sem)
    normed_loads = load_left(split, NORMED, 128, "z", normed, normed_sem)
    gqkv_loads = [load_right(late, GQKV + T * n, gqkv.at[n], gqkv_sem.at[n]) for n in range(3)]
    stages = [zed_loads + gp_loads[0], *gp_loads[1:], normed_loads + gqkv_loads[0]]
    stages += [gqkv_loads[1], gqkv_loads[2] + zed_z_loads + line_loads, []]
    stores = []
    start(stages[0] + stages[1])
    for n in range(4):
        wait(stages[n])
        start(stages[n + 2])
        width = min(D, UP - n * D)
        at = pl.ds(n * D, width)
        part = nn(zed[...], gp[n, :, :width])
        up_out[:, :, at] = part.astype(BF16).reshape(4, 128, width)
        stores += store_out(up_out, at, up_sent, up_kept, up_sem.at[n])
    for n in range(3):
        wait(stages[4 + n])
        start(stages[6] if n == 0 else [])
        at = pl.ds(n * D, D)
        qkv_out[:, :, at] = nn(normed[...], gqkv[n]).astype(BF16).reshape(4, 128, D)
        stores += store_out(qkv_out, at, qkv_sent, qkv_kept, qkv_sem.at[n])
    more = FF - UP
    part = nn(zed_z[...], gp[3, :, D - more :])
    qkv_out[:, :, pl.ds(3 * D, more)] = part.astype(BF16).reshape(4, 128, more)
    both_lines = (lines[:, 0].astype(F32) + lines[:, 1].astype(F32)).astype(BF16)
    qkv_out[:, :, pl.ds(3 * D + more, 128)] = both_lines
    at = pl.ds(3 * D, more + 128)
    stores += store_out(qkv_out, at, qkv_sent, qkv_kept, qkv_sem.at[3])
    wait(stores)


def up_and_qkv_grads(own, one, two, late_own, three, four, after):
    up = sds((2, 128, UP), BF16)
    qkv = sds((2, 128, 3 * D + FF - UP + 128), BF16)
    return call(
        up_and_qkv_kernel,
        "up_and_qkv_grad",
        2 * T * D * (FF + 3 * D),
        16 * MIB,
        24,
        (2, 5),
        in_specs=[hbm()] * 7,
        out_specs=[hbm()] * 4,
        out_shape=[up, up, qkv, qkv],
        scratch_shapes=[
            pltpu.VMEM((512, 2 * T), BF16),
            pltpu.VMEM((512, 2 * T), BF16),
            pltpu.VMEM((512, 2 * T), BF16),
            pltpu.VMEM((4, 2 * T, D), BF16),
            pltpu.VMEM((3, 2 * T, D), BF16),
            pltpu.VMEM((4, 2, 128, 128), BF16),
            pltpu.VMEM((4, 128, UP), BF16),
            pltpu.VMEM((4, 128, 3 * D + FF - UP + 128), BF16),
            pltpu.SemaphoreType.DMA((4, 2)),
            pltpu.SemaphoreType.DMA((4, 2)),
            pltpu.SemaphoreType.DMA((4, 2)),
            pltpu.SemaphoreType.DMA((4, 2)),
            pltpu.SemaphoreType.DMA((3, 2)),
            pltpu.SemaphoreType.DMA((4, 2)),
            pltpu.SemaphoreType.DMA((4, 2)),
            pltpu.SemaphoreType.DMA((4, 2)),
        ],
    )(own, one, two, late_own, three, four, after)


def swap_cores(array):
    return lax.ppermute(array, "c", [(0, 1), (1, 0)])


def pairs(mask_0, mask_1):
    perm = []
    for p in range(4):
        perm.append((2 * p, 2 * (p ^ mask_0)))
        perm.append((2 * p + 1, 2 * (p ^ mask_1) + 1))
    return perm


def ordered(token, *arrays):
    return lax.optimization_barrier((*arrays, token))[:-1]


def chain(sent, kept, axes, shape, finish):
    left = [axis for axis in ("y", "x", "z") if axis != axes[0]]
    for axis in axes:
        got = lax.ppermute(sent, (axis, "c"), pairs(1, 3))
        token = yield sent
        got, kept = ordered(token, got, kept)
        more = (got[1].astype(F32) + kept[1].astype(F32)).astype(BF16)
        got_2 = lax.ppermute(more, (axis, "c"), pairs(3, 1))
        token = yield more
        got, kept, got_2 = ordered(token, got, kept, got_2)
        terms = [got.reshape(2, *shape), kept.reshape(2, *shape), got_2.reshape(1, *shape)]
        if not left:
            return finish(*terms)
        following = axes[axes.index(axis) + 1]
        dim = left.index(following)
        left.pop(dim)
        shape = shape[:dim] + shape[dim + 1 :]

        def block(at):
            total = 0.0
            for term in terms:
                start = [0] * term.ndim
                start[1 + dim] = at
                sizes = (1,) + term.shape[1 : 1 + dim] + (1,) + term.shape[2 + dim :]
                total = total + lax.dynamic_slice(term, start, sizes).astype(F32)
            return total.reshape(shape)

        first, across, own, second = [block(at) for at in block_order(following)]
        sent = jnp.stack([first, across]).astype(BF16)
        kept = jnp.stack([own, second])


def total(terms, *at):
    return sum(term[(0, *at)].astype(F32) for term in terms)


def take_turns(token, turns, **chains):
    for steps in chains.values():
        next(steps)
    for turn in turns:
        token = next_step(chains[turn], token)


def next_step(steps, token):
    try:
        return steps.send(token)
    except StopIteration as end:
        return end.value


def body(
    tokens,
    norm_gain,
    qkv_weight,
    out_weight,
    ln_gain,
    ln_bias,
    up_weight,
    down_weight,
    buckets,
    router_prob,
    heads_active,
    doc_lengths,
    cotangent,
):
    norm_gain, ln_gain, ln_bias = [v.reshape(1, D) for v in (norm_gain, ln_gain, ln_bias)]
    router = router_prob.reshape(1, T)
    levels = buckets.reshape(1, T)
    inverse = np.tile(10000.0 ** (-2.0 * np.arange(HD // 2) / HD), 4).reshape(1, 128)
    inverse = jnp.asarray(inverse, F32)

    parts, first, first_other, second, second_other, qkv, act, middle = front(
        doc_lengths,
        heads_active,
        norm_gain,
        inverse,
        ln_gain,
        ln_bias,
        router,
        levels,
        tokens,
        cotangent,
        qkv_weight,
        out_weight,
        up_weight,
        down_weight,
    )
    first_2, second_2 = swap_cores(first_other), swap_cores(second_other)
    third, third_other, input_grad = back(
        doc_lengths,
        heads_active,
        norm_gain,
        inverse,
        levels,
        parts,
        first_other,
        qkv,
        tokens,
        qkv_weight,
        out_weight,
    )
    third_2 = swap_cores(third_other)
    first_2, _ = lax.optimization_barrier((first_2, third))
    down_sent, down_kept = down_grads(first, first_other, first_2)
    up_sent, up_kept, qkv_sent, qkv_kept = up_and_qkv_grads(
        second, second_other, second_2, third, third_other, third_2, down_sent
    )

    mixed = mixed_output(router, middle, act, down_weight, qkv_sent)

    every = slice(None)
    grads = {}

    def down_done(*terms):
        grads["down"] = total(terms, every, slice(0, D))
        out = total(terms, every, slice(D, D + T))
        grads["out"] = out.reshape(4, 8, T).transpose(1, 0, 2).reshape(8, D)
        grads["down"], grads["out"] = lax.optimization_barrier((grads["down"], grads["out"]))
        return grads["out"]

    def up_done(*terms):
        grads["up"] = jnp.concatenate([total(terms), grads["more_up"]], 1)
        return grads["up"]

    def qkv_done(*terms):
        grads["qkv"] = total(terms, every, slice(0, 3 * D))
        end = 3 * D + FF - UP
        grads["more_up"] = total(terms, every, slice(3 * D, end))
        line = total(terms, every, slice(end, end + 128))
        grads["gains"] = [line[:, n] for n in range(3)]
        bits = line[0, 3 : 3 + BITS * NEST].astype(jnp.int32).reshape(NEST, BITS)
        grads["counts"] = jnp.sum(bits << jnp.arange(BITS, dtype=jnp.int32)[None, :], 1)
        done = (grads["qkv"], grads["more_up"], grads["counts"], *grads["gains"])
        done = lax.optimization_barrier(done)
        grads["qkv"], grads["more_up"], grads["counts"], *grads["gains"] = done
        return grads["qkv"]

    take_turns(
        mixed,
        TURNS,
        d=chain(down_sent, down_kept, "yxz", (4, 4, 32, D + T), down_done),
        u=chain(up_sent, up_kept, "xyz", (4, 4, 8, UP), up_done),
        q=chain(qkv_sent, qkv_kept, "zyx", (4, 4, 8, 3 * D + FF - UP + 128), qkv_done),
    )
    gain_grad, ln_gain_grad, ln_bias_grad = grads["gains"]
    return (
        mixed,
        input_grad,
        gain_grad,
        grads["qkv"],
        grads["out"],
        ln_gain_grad,
        ln_bias_grad,
        grads["up"],
        grads["down"],
        grads["counts"],
    )


def solution(mesh):
    finer = Mesh(mesh.devices.reshape(4, 4, 4, 2), AX)
    rows = P(AX, None)
    return jax.shard_map(
        body,
        mesh=finer,
        in_specs=(rows, P(), P(), P(), P(), P(), P(), P(), rows, P(AX), rows, rows, rows),
        out_specs=(rows, rows, P(AX), rows, rows, P(AX), P(AX), rows, rows, P()),
        check_vma=False,
    )
```

```python
import jax
import jax.numpy as jnp
import numpy as np
from jax import lax
from jax.experimental import pallas as pl
from jax.experimental.pallas import tpu as pltpu
from jax.sharding import Mesh
from jax.sharding import PartitionSpec as P

HD = 64
NEST = 4
AX = ("y", "x", "z", "c")

NEG = -1e30
EPS = 1e-05
F32 = jnp.float32
BF16 = jnp.bfloat16
T = 256
D = 1024
FF = 4096
GW = 256
GROUPS = D // GW
HEADS = GW // HD
ACT, MERGED, FIRST_OWN, GB, GA, FIRST = 0, 512, 640, 640, 896, 1152
ZED, NORMED, ZED_Z, SECOND_OWN, GP, SECOND = 0, 128, 256, 384, 384, 1408
LINES, THIRD_OWN, GQKV, THIRD = 0, 128, 128, 896
TURNS = "dquqduqduqduqdudqu"
UP = 3584
BITS = 9
MIB = 1024 * 1024


def nn(a, b):
    return lax.dot_general(a, b, (((1,), (0,)), ((), ())), preferred_element_type=F32)


def nt(a, b):
    return lax.dot_general(a, b, (((1,), (1,)), ((), ())), preferred_element_type=F32)


def tn(a, b):
    return lax.dot_general(a, b, (((0,), (0,)), ((), ())), preferred_element_type=F32)


def sds(shape, dtype):
    return jax.ShapeDtypeStruct(shape, dtype)


def smem():
    return pl.BlockSpec(memory_space=pltpu.SMEM)


def vmem():
    return pl.BlockSpec(memory_space=pltpu.VMEM)


def hbm():
    return pl.BlockSpec(memory_space=pltpu.HBM)


def call(kernel, name, flops, moved, room, anywhere=(), **kw):
    def in_hbm(spec):
        return spec.memory_space == pltpu.HBM

    kw["out_shape"] = [
        pltpu.HBM(s.shape, s.dtype) if in_hbm(spec) else s
        for s, spec in zip(kw["out_shape"], kw["out_specs"])
    ]
    run = pl.pallas_call(
        kernel,
        name=name,
        compiler_params=pltpu.CompilerParams(vmem_limit_bytes=room * MIB),
        cost_estimate=pl.CostEstimate(flops=flops, bytes_accessed=moved, transcendentals=0),
        **kw,
    )

    def placed(*args):
        return run(
            *(
                pltpu.with_memory_space_constraint(arg, pltpu.HBM)
                if in_hbm(spec) and n not in anywhere
                else arg
                for n, (arg, spec) in enumerate(zip(args, kw["in_specs"]))
            )
        )

    return placed


def first_halves():
    return lax.broadcasted_iota(jnp.int32, (T, 128), 1) % HD < HD // 2


def head_of(g):
    return HEADS * g + lax.broadcasted_iota(jnp.int32, (T, GW), 1) // HD


def by_head(x):
    lane = lax.broadcasted_iota(jnp.int32, (T, GW), 1)
    zero = jnp.zeros((T, GW), x.dtype)
    own = [(lane >= HD * h) & (lane < HD * h + HD) for h in range(HEADS)]
    return jnp.concatenate([jnp.where(keep, x, zero) for keep in own], 0)


def turned(x, cosine, sine, first):
    parts = []
    for at in range(0, x.shape[1], 128):
        part = x[:, at : at + 128]
        other = jnp.where(first, pltpu.roll(part, 128 - HD // 2, 1), pltpu.roll(part, HD // 2, 1))
        parts.append(part * cosine + other * sine)
    return jnp.concatenate(parts, 1)


def doc_ends(lengths):
    return lengths[0, 0], lengths[0, 0] + lengths[0, 1]


def doc_start(lengths, place):
    end_0, end_1 = doc_ends(lengths)
    return jnp.where(place >= end_1, end_1, jnp.where(place >= end_0, end_0, 0))


def of_doc(lengths, place, values):
    end_0, end_1 = doc_ends(lengths)
    late = jnp.where(place >= end_1, values[0, 2], values[0, 1])
    return jnp.where(place >= end_0, late, values[0, 0])


def normalized(middle):
    shifted = middle - jnp.mean(middle, -1, keepdims=True)
    rstd = lax.rsqrt(jnp.mean(shifted * shifted, -1, keepdims=True) + EPS)
    return shifted * rstd, rstd


def block_order(axis):
    p = lax.axis_index(axis)
    core = lax.axis_index("c")
    return [p ^ (1 + 2 * core), p ^ 2, p, p ^ (3 - 2 * core)]


def load(src, dst, sem):
    copy = pltpu.make_async_copy(src, dst, sem)
    copy.start()
    return copy


def columns(j, size):
    if isinstance(j, int):
        return pl.ds(j * size, size)
    return pl.ds(pl.multiple_of(j * size, size), size)


def upright(row):
    return jnp.broadcast_to(row, (8, T)).T[:, :1]


def places():
    return lax.broadcasted_iota(jnp.int32, (T, 128), 0)


def rotary(lengths, inverse):
    phase = (places() - doc_start(lengths, places())).astype(F32) * inverse[...]
    sine = jnp.sin(phase)
    return jnp.cos(phase), jnp.where(first_halves(), -sine, sine)


def start(copies):
    for copy in copies:
        copy.start()


def wait(copies):
    for copy in copies:
        copy.wait()


def front_kernel(
    lengths,
    heads,
    norm_gain,
    inverse,
    ln_gain,
    ln_bias,
    router,
    bucket,
    tokens_hbm,
    cot_hbm,
    wqkv_hbm,
    wo_hbm,
    up_hbm,
    down_hbm,
    parts_out,
    first_mine,
    first_other,
    second_mine,
    second_other,
    qkv_out,
    act_out,
    middle_out,
    parts,
    tokens,
    cot,
    wqkv,
    wo,
    up,
    down,
    qkv,
    normed,
    merged,
    zed,
    gb,
    act,
    act_turned,
    gp,
    turned_f,
    left,
    middle,
    ga,
    bias,
    active,
    level,
    in_sem,
    ffn_sem,
    act_sem,
    gp_sem,
    left_sem,
    out_sem,
):
    core = lax.axis_index("c")
    firsts, seconds = (first_mine, first_other), (second_mine, second_other)
    loads = [load(tokens_hbm, tokens, in_sem.at[0])]
    for n in range(3):
        src = wqkv_hbm.at[:, n * D : (n + 1) * D]
        loads.append(pltpu.make_async_copy(src, wqkv.at[n], in_sem.at[1 + n]))
    loads[1].start()

    def ffn_loads(j):
        at = columns(j, D)
        return (
            pltpu.make_async_copy(up_hbm.at[:, at], up.at[:, at], ffn_sem.at[0, j]),
            pltpu.make_async_copy(down_hbm.at[at, :], down.at[at, :], ffn_sem.at[1, j]),
        )

    stores = []

    def turn(value):
        turned_f[...] = value.astype(F32).T.reshape(turned_f.shape)

    def store_left(n, axis, refs, at):
        for side, ref in enumerate(refs):
            half = core if side == 0 else 1 - core
            for i in range(4):
                if axis == 0:
                    rows = turned_f[i, :, :, half]
                elif axis == 1:
                    rows = turned_f[:, i, :, half]
                else:
                    rows = turned_f[:, :, i, half]
                left[side, n, :, pl.ds(T * i, T)] = rows.reshape(128, T).astype(BF16)
            dst = ref.at[pl.ds(at, 128), :]
            stores.append(load(left.at[side, n], dst, left_sem.at[side, n]))

    first = first_halves()
    scale = jnp.asarray(HD**-0.5, BF16)
    cosine, sine = rotary(lengths, inverse)
    row = lax.broadcasted_iota(jnp.int32, (T, T), 0)
    col = lax.broadcasted_iota(jnp.int32, (T, T), 1)
    bias[...] = jnp.where((col >= doc_start(lengths, row)) & (col <= row), 0.0, NEG)
    active[...] = of_doc(lengths, lax.broadcasted_iota(jnp.int32, (T, GW), 0), heads)
    level[...] = upright(bucket[...])
    prob = upright(router[...])

    loads[0].wait()
    start(loads[2:4])
    resid = tokens[...].astype(F32)
    rscale = lax.rsqrt(jnp.mean(resid * resid, -1, keepdims=True) + EPS)
    normed[...] = (resid * rscale * norm_gain[...]).astype(BF16)
    for n in range(3):
        loads[1 + n].wait()
        if n == 1:
            loads.append(load(cot_hbm, cot, in_sem.at[4]))
        if n == 2:
            loads.append(load(wo_hbm, wo, in_sem.at[5]))
            for copy in ffn_loads(0) + ffn_loads(1):
                copy.start()
        part = nn(normed[...], wqkv[n])
        qkv[n] = (turned(part, cosine, sine, first) if n < 2 else part).astype(BF16)
    stores.append(load(qkv, qkv_out, out_sem.at[0]))

    def attend(g, carry):
        at = columns(g, GW)
        keys, values = by_head(qkv[1, :, at]), by_head(qkv[2, :, at])
        s = nt(qkv[0, :, at] * scale, keys)
        parts = []
        for h in range(HEADS):
            one = s[:, T * h : T * h + T] + bias[...]
            e = jnp.exp(one - jnp.max(one, -1, keepdims=True))
            parts.append((e / jnp.sum(e, -1, keepdims=True)).astype(BF16))
        out = nn(jnp.concatenate(parts, 1), values)
        merged[:, at] = jnp.where(head_of(g) < active[...], out, 0.0).astype(BF16)

        @pl.when((g > 0) & (g < NEST - 1))
        def _():
            for copy in ffn_loads(g + 1):
                copy.start()

        return carry

    lax.fori_loop(0, GROUPS, attend, 0)
    loads[5].wait()
    middle[...] = tokens[...].astype(F32) + nn(merged[...], wo[...])
    stores.append(load(middle, middle_out, out_sem.at[1]))
    normed_mid, _ = normalized(middle[...])
    zed[...] = (normed_mid * ln_gain[...] + ln_bias[...]).astype(BF16)
    loads[4].wait()
    gb[...] = (cot[...].astype(F32) * prob).astype(BF16)
    stores.append(load(gb, first_other.at[pl.ds(GB, T), :], out_sem.at[2]))

    def act_stores(j):
        at = (pl.ds(ACT, 512), columns(j, T))
        return [
            pltpu.make_async_copy(act_turned.at[side, :, at[1]], ref.at[at], act_sem.at[side, j])
            for side, ref in enumerate(firsts)
        ]

    def act_store(j):
        at = columns(j, D)
        return pltpu.make_async_copy(act.at[:, at], act_out.at[:, at], act_sem.at[2, j])

    def gp_store(j):
        rows = pl.ds(pl.multiple_of(GP + T * j, 128), T)
        return pltpu.make_async_copy(gp.at[:, columns(j, D)], second_other.at[rows, :], gp_sem.at[j])

    def hidden(j, carry):
        copy_up, copy_down = ffn_loads(j)
        at = columns(j, D)
        copy_up.wait()
        r = jnp.where(level[...] >= j, jnp.maximum(nn(zed[...], up[:, at]), 0.0), 0.0)
        a = (r * r).astype(BF16)
        act[:, at] = a
        by_core = a.T.reshape(16, 2, 32, T)
        low_rows, high_rows = by_core[:, 0].reshape(512, T), by_core[:, 1].reshape(512, T)
        act_store(j).start()
        act_turned[0, :, columns(j, T)] = jnp.where(core == 0, low_rows, high_rows)
        act_turned[1, :, columns(j, T)] = jnp.where(core == 0, high_rows, low_rows)
        for copy in act_stores(j):
            copy.start()
        copy_down.wait()
        gp[:, at] = (nt(gb[...], down[at, :]) * 2.0 * r).astype(BF16)
        gp_store(j).start()
        return carry

    lax.fori_loop(0, NEST, hidden, 0)
    turn(zed[...])
    store_left(0, 1, seconds, ZED)
    store_left(3, 2, seconds, ZED_Z)
    turn(normed[...])
    store_left(1, 2, seconds, NORMED)
    turn(merged[...])
    store_left(2, 0, firsts, MERGED)

    grad_zed = nt(gp[...], up[...]).astype(BF16).astype(F32)
    normed_mid, rstd = normalized(middle[...])
    parts[0:1, :] = jnp.sum(grad_zed * normed_mid, 0, keepdims=True)
    parts[1:2, :] = jnp.sum(grad_zed, 0, keepdims=True)
    grad_norm = grad_zed * ln_gain[...]
    grad = cot[...].astype(F32) + rstd * (
        grad_norm
        - jnp.mean(grad_norm, -1, keepdims=True)
        - normed_mid * jnp.mean(grad_norm * normed_mid, -1, keepdims=True)
    )
    ga[...] = grad.astype(BF16)
    stores.append(load(parts, parts_out, out_sem.at[3]))
    stores.append(load(ga, first_other.at[pl.ds(GA, T), :], out_sem.at[4]))
    for j in range(NEST):
        wait(act_stores(j) + [act_store(j), gp_store(j)])
    wait(stores)


def front(lengths, heads, norm_gain, inverse, ln_gain, ln_bias, router, bucket, *arrays):
    row_b = sds((T, D), BF16)
    scratch = [
        sds((8, D), F32),
        row_b,
        row_b,
        sds((3, D, D), BF16),
        sds((D, D), BF16),
        sds((D, FF), BF16),
        sds((FF, D), BF16),
        sds((3, T, D), BF16),
        row_b,
        row_b,
        row_b,
        row_b,
        sds((T, FF), BF16),
        sds((2, 512, D), BF16),
        sds((T, FF), BF16),
        sds((4, 4, 4, 2, 8, T), F32),
        sds((2, 4, 128, D), BF16),
        sds((T, D), F32),
        row_b,
        sds((T, T), F32),
        sds((T, GW), jnp.int32),
        sds((T, 1), jnp.int32),
    ]
    semaphores = [(6,), (2, NEST), (3, NEST), (NEST,), (2, 4), (5,)]
    return call(
        front_kernel,
        "front",
        2 * T * D * (4 * D + 3 * FF),
        40 * MIB,
        58,
        in_specs=[smem()] * 2 + [vmem()] * 6 + [hbm()] * 6,
        out_specs=[hbm()] * 8,
        out_shape=[
            sds((8, D), F32),
            sds((FIRST_OWN, D), BF16),
            sds((FIRST, D), BF16),
            sds((SECOND_OWN, D), BF16),
            sds((SECOND, D), BF16),
            sds((3, T, D), BF16),
            sds((T, FF), BF16),
            sds((T, D), F32),
        ],
        scratch_shapes=[pltpu.VMEM(s.shape, s.dtype) for s in scratch]
        + [pltpu.SemaphoreType.DMA(s) for s in semaphores],
    )(lengths, heads, norm_gain, inverse, ln_gain, ln_bias, router, bucket, *arrays)


def back_kernel(
    lengths,
    heads,
    inverse,
    bucket,
    parts_hbm,
    first_other,
    qkv_hbm,
    tokens_hbm,
    wqkv_hbm,
    wo_hbm,
    third_mine,
    third_other,
    grad_normed_out,
    parts,
    ga,
    qkv,
    grad_store,
    tokens,
    wqkv,
    wo,
    gqkv,
    lines_f,
    lines,
    bias,
    active,
    in_sem,
    w_sem,
    group_sem,
    out_sem,
):
    core = lax.axis_index("c")
    thirds = (third_mine, third_other)
    loads = [
        load(first_other.at[pl.ds(GA, T), :], ga, in_sem.at[0]),
        load(wo_hbm.at[pl.ds(0, GW), :], wo.at[pl.ds(0, GW), :], in_sem.at[1]),
        load(qkv_hbm.at[:, :, pl.ds(0, GW)], qkv.at[:, :, pl.ds(0, GW)], in_sem.at[2]),
    ]
    others = pl.ds(GW, D - GW)
    more = [
        pltpu.make_async_copy(wo_hbm.at[others, :], wo.at[others, :], in_sem.at[5]),
        pltpu.make_async_copy(qkv_hbm.at[:, :, others], qkv.at[:, :, others], in_sem.at[6]),
    ]
    late = [
        pltpu.make_async_copy(tokens_hbm, tokens, in_sem.at[3]),
        pltpu.make_async_copy(parts_hbm, parts, in_sem.at[7]),
    ]
    for n in range(3):
        src = wqkv_hbm.at[:, n * D : (n + 1) * D]
        late.append(pltpu.make_async_copy(src, wqkv.at[n], w_sem.at[n]))

    first = first_halves()
    scale = jnp.asarray(HD**-0.5, BF16)
    cosine, sine = rotary(lengths, inverse)
    sine = -sine
    query = lax.broadcasted_iota(jnp.int32, (T, T), 1)
    key = lax.broadcasted_iota(jnp.int32, (T, T), 0)
    bias[...] = jnp.where((key >= doc_start(lengths, query)) & (key <= query), 0.0, NEG)
    active[...] = of_doc(lengths, lax.broadcasted_iota(jnp.int32, (T, GW), 0), heads)
    wait(loads)
    for copy in more:
        copy.start()

    def group_stores(g):
        at = columns(g, GW)
        return [
            pltpu.make_async_copy(
                gqkv.at[n, :, at], third_other.at[pl.ds(GQKV + T * n, T), at], group_sem.at[n, g]
            )
            for n in range(3)
        ]

    def attend_back(g, carry):
        @pl.when(g == 1)
        def _():
            wait(more)
            start(late)

        at = columns(g, GW)
        gm = nt(ga[...], wo[at, :])
        gm = jnp.where(head_of(g) < active[...], gm, 0.0).astype(BF16)
        gms, queries = by_head(gm), by_head(qkv[0, :, at] * scale)
        k = qkv[1, :, at]
        s = nt(k, queries)
        grad_p = nt(qkv[2, :, at], gms)
        parts_p, parts_s = [], []
        for h in range(HEADS):
            one = s[:, T * h : T * h + T] + bias[...]
            e = jnp.exp(one - jnp.max(one, 0, keepdims=True))
            p = e / jnp.sum(e, 0, keepdims=True)
            grad = grad_p[:, T * h : T * h + T]
            parts_p.append(p.astype(BF16))
            grad = p * (grad - jnp.sum(p * grad, 0, keepdims=True))
            parts_s.append(grad.astype(BF16))
        grad_s = jnp.concatenate(parts_s, 1)
        grad_v = nn(jnp.concatenate(parts_p, 1), gms)
        grad_k = nn(grad_s, queries)
        wide = nn((k * scale).T, grad_s)
        grad_q = [wide[HD * h : HD * h + HD, T * h : T * h + T] for h in range(HEADS)]
        grad_q = jnp.concatenate(grad_q, 0).T
        gqkv[0, :, at] = turned(grad_q, cosine, sine, first).astype(BF16)
        gqkv[1, :, at] = turned(grad_k, cosine, sine, first).astype(BF16)
        gqkv[2, :, at] = grad_v.astype(BF16)
        for copy in group_stores(g):
            copy.start()
        return carry

    lax.fori_loop(0, GROUPS, attend_back, 0)

    wait(late)
    grad_normed = nt(gqkv[0], wqkv[0]) + nt(gqkv[1], wqkv[1]) + nt(gqkv[2], wqkv[2])
    resid = tokens[...].astype(F32)
    rscale = lax.rsqrt(jnp.mean(resid * resid, -1, keepdims=True) + EPS)
    unit = resid * rscale
    gain_part = jnp.sum(grad_normed * unit, 0, keepdims=True)
    grad_store[...] = grad_normed
    stores = [load(grad_store, grad_normed_out, out_sem.at[0])]

    item = lax.broadcasted_iota(jnp.int32, (128, 1), 0)
    count = jnp.zeros((128, 1), jnp.int32)
    for n in range(NEST):
        total = jnp.sum((bucket[...] == n).astype(jnp.int32), 1, keepdims=True)
        at = item - 3 - BITS * n
        bit = lax.shift_right_logical(total, jnp.clip(at, 0, BITS - 1)) & 1
        count = jnp.where((at >= 0) & (at < BITS), bit, count)
    wide = jnp.where(item == 0, gain_part, jnp.where(item == 1, parts[0:1, :], parts[1:2, :]))
    lines_f[...] = jnp.where(item < 3, wide, count.astype(F32)).T.reshape(lines_f.shape)
    for side, ref in enumerate(thirds):
        half = core if side == 0 else 1 - core
        for i in range(4):
            part = lines_f[:, :, i, half].reshape(128, 128).astype(BF16)
            lines[side, :, pl.ds(128 * i, 128)] = part
        dst = ref.at[pl.ds(LINES, 128), pl.ds(0, 512)]
        stores.append(load(lines.at[side], dst, out_sem.at[1 + side]))
    for g in range(GROUPS):
        wait(group_stores(g))
    wait(stores)


def back(lengths, heads, inverse, bucket, parts, *arrays):
    scratch = [
        sds((8, D), F32),
        sds((T, D), BF16),
        sds((3, T, D), BF16),
        sds((T, D), F32),
        sds((T, D), BF16),
        sds((3, D, D), BF16),
        sds((D, D), BF16),
        sds((3, T, D), BF16),
        sds((4, 4, 4, 2, 8, 128), F32),
        sds((2, 128, 512), BF16),
        sds((T, T), F32),
        sds((T, GW), jnp.int32),
    ]
    return call(
        back_kernel,
        "back",
        2 * T * D * 4 * D + 10 * 16 * T * T * 256,
        18 * MIB,
        32,
        in_specs=[smem()] * 2 + [vmem()] * 2 + [hbm()] * 6,
        out_specs=[hbm()] * 3,
        out_shape=[sds((THIRD_OWN, D), BF16), sds((THIRD, D), BF16), sds((T, D), F32)],
        scratch_shapes=[pltpu.VMEM(s.shape, s.dtype) for s in scratch]
        + [pltpu.SemaphoreType.DMA(s) for s in [(8,), (3,), (3, GROUPS), (3,)]],
    )(lengths, heads, inverse, bucket, parts, *arrays)


def ends_kernel(
    router,
    norm_gain,
    grad_normed_hbm,
    first_other,
    tokens_hbm,
    middle_hbm,
    act_hbm,
    down_hbm,
    after,
    mixed_out,
    input_grad_out,
    grad_normed,
    ga,
    tokens,
    middle,
    act,
    down,
    mixed,
    sem,
    ffn_sem,
):
    loads = [
        load(grad_normed_hbm, grad_normed, sem.at[0]),
        load(tokens_hbm, tokens, sem.at[1]),
        load(first_other.at[pl.ds(GA, T), :], ga, sem.at[2]),
    ]
    middle_load = load(middle_hbm, middle, sem.at[3])
    stages = []
    for j in range(NEST):
        at = pl.ds(j * D, D)
        stages.append(
            [
                pltpu.make_async_copy(act_hbm.at[:, at], act.at[:, at], ffn_sem.at[0, j]),
                pltpu.make_async_copy(down_hbm.at[at, :], down.at[at, :], ffn_sem.at[1, j]),
            ]
        )
        start(stages[j])
    wait(loads)
    resid = tokens[...].astype(F32)
    rscale = lax.rsqrt(jnp.mean(resid * resid, -1, keepdims=True) + EPS)
    unit = resid * rscale
    grad_unit = grad_normed[...] * norm_gain[...]
    grad_normed[...] = ga[...].astype(F32) + rscale * (
        grad_unit - unit * jnp.mean(grad_unit * unit, -1, keepdims=True)
    )
    stores = [load(grad_normed, input_grad_out, sem.at[4])]
    for stage in stages:
        wait(stage)
    branch = nn(act[...], down[...]).astype(BF16).astype(F32)
    middle_load.wait()
    mixed[...] = (middle[...] + upright(router[...]) * branch).astype(BF16)
    stores.append(load(mixed, mixed_out, sem.at[5]))
    wait(stores)


def ends(router, norm_gain, *arrays):
    return call(
        ends_kernel,
        "ends",
        2 * T * D * FF,
        16 * MIB,
        20,
        in_specs=[vmem()] * 2 + [hbm()] * 7,
        out_specs=[hbm()] * 2,
        out_shape=[sds((T, D), BF16), sds((T, D), F32)],
        scratch_shapes=[
            pltpu.VMEM((T, D), F32),
            pltpu.VMEM((T, D), BF16),
            pltpu.VMEM((T, D), BF16),
            pltpu.VMEM((T, D), F32),
            pltpu.VMEM((T, FF), BF16),
            pltpu.VMEM((FF, D), BF16),
            pltpu.VMEM((T, D), BF16),
            pltpu.SemaphoreType.DMA((6,)),
            pltpu.SemaphoreType.DMA((2, NEST)),
        ],
    )(router, norm_gain, *arrays)


def load_left(refs, at, rows, axis, left, sem):
    return [
        pltpu.make_async_copy(
            ref.at[pl.ds(at, rows), columns(block, T)],
            left.at[pl.ds(rows * i, rows), pl.ds(T * m, T)],
            sem.at[i, m],
        )
        for i, block in enumerate(block_order(axis))
        for m, ref in enumerate(refs)
    ]


def load_right(refs, at, right, sem):
    return [
        pltpu.make_async_copy(ref.at[pl.ds(at, T), :], right.at[pl.ds(T * m, T), :], sem.at[m])
        for m, ref in enumerate(refs)
    ]


def store_out(out, at, sent, kept, sem):
    return [
        load(out.at[pl.ds(2 * side, 2), :, at], ref.at[:, :, at], sem.at[side])
        for side, ref in enumerate((sent, kept))
    ]


def down_grad_kernel(
    own, one, two, sent, kept, act, merged, gb, ga, out, act_sem, merged_sem, gb_sem, ga_sem, sem
):
    refs, split = (one, two), (own, two)
    gb_loads = load_right(refs, GB, gb, gb_sem)
    act_loads = load_left(split, ACT, 512, "y", act, act_sem)
    ga_loads = load_right(refs, GA, ga, ga_sem)
    merged_loads = load_left(split, MERGED, 128, "y", merged, merged_sem)
    stages = [gb_loads + act_loads[:2], act_loads[2:4], act_loads[4:6], act_loads[6:]]
    stages.append(ga_loads + merged_loads)
    stores = []
    start(stages[0] + stages[1])
    wide = pl.ds(0, D)
    for i in range(4):
        wait(stages[i])
        start(stages[i + 2] if i < 3 else [])
        out[i, :, wide] = nn(act[pl.ds(512 * i, 512), :], gb[...]).astype(BF16)
        dst = (sent, kept)[i // 2].at[i % 2, :, wide]
        stores.append(load(out.at[i, :, wide], dst, sem.at[0, i]))
    wait(stages[4])
    part = nn(merged[...], ga[...])
    more = pl.ds(D, T)
    for i in range(4):
        rows = part[128 * i : 128 * i + 128].reshape(16, 8, D)
        quarters = [rows[:, :, T * q : T * q + T] for q in range(4)]
        out[i, :, more] = jnp.concatenate(quarters, 1).reshape(512, T).astype(BF16)
    stores += store_out(out, more, sent, kept, sem.at[1])
    wait(stores)


def down_grads(own, one, two):
    part = sds((2, 512, D + T), BF16)
    return call(
        down_grad_kernel,
        "down_and_out_grad",
        2 * T * D * (FF + D),
        10 * MIB,
        18,
        (2,),
        in_specs=[hbm()] * 3,
        out_specs=[hbm()] * 2,
        out_shape=[part, part],
        scratch_shapes=[
            pltpu.VMEM((FF // 2, 2 * T), BF16),
            pltpu.VMEM((512, 2 * T), BF16),
            pltpu.VMEM((2 * T, D), BF16),
            pltpu.VMEM((2 * T, D), BF16),
            pltpu.VMEM((4, 512, D + T), BF16),
            pltpu.SemaphoreType.DMA((4, 2)),
            pltpu.SemaphoreType.DMA((4, 2)),
            pltpu.SemaphoreType.DMA((2,)),
            pltpu.SemaphoreType.DMA((2,)),
            pltpu.SemaphoreType.DMA((2, 4)),
        ],
    )(own, one, two)


def up_and_qkv_kernel(
    own,
    one,
    two,
    late_own,
    three,
    four,
    after,
    up_sent,
    up_kept,
    qkv_sent,
    qkv_kept,
    zed,
    zed_z,
    normed,
    gp,
    gqkv,
    lines,
    up_out,
    qkv_out,
    zed_sem,
    zed_z_sem,
    normed_sem,
    gp_sem,
    gqkv_sem,
    line_sem,
    up_sem,
    qkv_sem,
):
    refs, split = (one, two), (own, two)
    late = (three, four)
    zed_loads = load_left(split, ZED, 128, "x", zed, zed_sem)
    gp_loads = [load_right(refs, GP + T * n, gp.at[n], gp_sem.at[n]) for n in range(4)]
    line_loads = [
        pltpu.make_async_copy(
            ref.at[pl.ds(LINES, 128), columns(block, 128)],
            lines.at[i, m],
            line_sem.at[i, m],
        )
        for i, block in enumerate(block_order("z"))
        for m, ref in enumerate((late_own, four))
    ]
    zed_z_loads = load_left(split, ZED_Z, 128, "z", zed_z, zed_z_sem)
    normed_loads = load_left(split, NORMED, 128, "z", normed, normed_sem)
    gqkv_loads = [load_right(late, GQKV + T * n, gqkv.at[n], gqkv_sem.at[n]) for n in range(3)]
    stages = [zed_loads + gp_loads[0], *gp_loads[1:], normed_loads + gqkv_loads[0]]
    stages += [gqkv_loads[1], gqkv_loads[2] + zed_z_loads + line_loads, []]
    stores = []
    start(stages[0] + stages[1])
    for n in range(4):
        wait(stages[n])
        start(stages[n + 2])
        width = min(D, UP - n * D)
        at = pl.ds(n * D, width)
        part = nn(zed[...], gp[n, :, :width])
        up_out[:, :, at] = part.astype(BF16).reshape(4, 128, width)
        stores += store_out(up_out, at, up_sent, up_kept, up_sem.at[n])
    for n in range(3):
        wait(stages[4 + n])
        start(stages[6] if n == 0 else [])
        at = pl.ds(n * D, D)
        qkv_out[:, :, at] = nn(normed[...], gqkv[n]).astype(BF16).reshape(4, 128, D)
        stores += store_out(qkv_out, at, qkv_sent, qkv_kept, qkv_sem.at[n])
    more = FF - UP
    part = nn(zed_z[...], gp[3, :, D - more :])
    qkv_out[:, :, pl.ds(3 * D, more)] = part.astype(BF16).reshape(4, 128, more)
    both_lines = (lines[:, 0].astype(F32) + lines[:, 1].astype(F32)).astype(BF16)
    qkv_out[:, :, pl.ds(3 * D + more, 128)] = both_lines
    at = pl.ds(3 * D, more + 128)
    stores += store_out(qkv_out, at, qkv_sent, qkv_kept, qkv_sem.at[3])
    wait(stores)


def up_and_qkv_grads(own, one, two, late_own, three, four, after):
    up = sds((2, 128, UP), BF16)
    qkv = sds((2, 128, 3 * D + FF - UP + 128), BF16)
    return call(
        up_and_qkv_kernel,
        "up_and_qkv_grad",
        2 * T * D * (FF + 3 * D),
        16 * MIB,
        24,
        (2, 5),
        in_specs=[hbm()] * 7,
        out_specs=[hbm()] * 4,
        out_shape=[up, up, qkv, qkv],
        scratch_shapes=[
            pltpu.VMEM((512, 2 * T), BF16),
            pltpu.VMEM((512, 2 * T), BF16),
            pltpu.VMEM((512, 2 * T), BF16),
            pltpu.VMEM((4, 2 * T, D), BF16),
            pltpu.VMEM((3, 2 * T, D), BF16),
            pltpu.VMEM((4, 2, 128, 128), BF16),
            pltpu.VMEM((4, 128, UP), BF16),
            pltpu.VMEM((4, 128, 3 * D + FF - UP + 128), BF16),
            pltpu.SemaphoreType.DMA((4, 2)),
            pltpu.SemaphoreType.DMA((4, 2)),
            pltpu.SemaphoreType.DMA((4, 2)),
            pltpu.SemaphoreType.DMA((4, 2)),
            pltpu.SemaphoreType.DMA((3, 2)),
            pltpu.SemaphoreType.DMA((4, 2)),
            pltpu.SemaphoreType.DMA((4, 2)),
            pltpu.SemaphoreType.DMA((4, 2)),
        ],
    )(own, one, two, late_own, three, four, after)


def swap_cores(array):
    return lax.ppermute(array, "c", [(0, 1), (1, 0)])


def pairs(mask_0, mask_1):
    perm = []
    for p in range(4):
        perm.append((2 * p, 2 * (p ^ mask_0)))
        perm.append((2 * p + 1, 2 * (p ^ mask_1) + 1))
    return perm


def ordered(token, *arrays):
    return lax.optimization_barrier((*arrays, token))[:-1]


def chain(sent, kept, axes, shape, finish):
    left = [axis for axis in ("y", "x", "z") if axis != axes[0]]
    for axis in axes:
        got = lax.ppermute(sent, (axis, "c"), pairs(1, 3))
        token = yield sent
        got, kept = ordered(token, got, kept)
        more = (got[1].astype(F32) + kept[1].astype(F32)).astype(BF16)
        got_2 = lax.ppermute(more, (axis, "c"), pairs(3, 1))
        token = yield more
        got, kept, got_2 = ordered(token, got, kept, got_2)
        terms = [got.reshape(2, *shape), kept.reshape(2, *shape), got_2.reshape(1, *shape)]
        if not left:
            return finish(*terms)
        following = axes[axes.index(axis) + 1]
        dim = left.index(following)
        left.pop(dim)
        shape = shape[:dim] + shape[dim + 1 :]

        def block(at):
            total = 0.0
            for term in terms:
                start = [0] * term.ndim
                start[1 + dim] = at
                sizes = (1,) + term.shape[1 : 1 + dim] + (1,) + term.shape[2 + dim :]
                total = total + lax.dynamic_slice(term, start, sizes).astype(F32)
            return total.reshape(shape)

        first, across, own, second = [block(at) for at in block_order(following)]
        sent = jnp.stack([first, across]).astype(BF16)
        kept = jnp.stack([own, second])


def total(terms, *at):
    return sum(term[(0, *at)].astype(F32) for term in terms)


def take_turns(token, turns, **chains):
    for steps in chains.values():
        next(steps)
    for turn in turns:
        token = next_step(chains[turn], token)


def next_step(steps, token):
    try:
        return steps.send(token)
    except StopIteration as end:
        return end.value


def body(
    tokens,
    norm_gain,
    qkv_weight,
    out_weight,
    ln_gain,
    ln_bias,
    up_weight,
    down_weight,
    buckets,
    router_prob,
    heads_active,
    doc_lengths,
    cotangent,
):
    norm_gain, ln_gain, ln_bias = [v.reshape(1, D) for v in (norm_gain, ln_gain, ln_bias)]
    router = router_prob.reshape(1, T)
    levels = buckets.reshape(1, T)
    inverse = np.tile(10000.0 ** (-2.0 * np.arange(HD // 2) / HD), 4).reshape(1, 128)
    inverse = jnp.asarray(inverse, F32)

    parts, first, first_other, second, second_other, qkv, act, middle = front(
        doc_lengths,
        heads_active,
        norm_gain,
        inverse,
        ln_gain,
        ln_bias,
        router,
        levels,
        tokens,
        cotangent,
        qkv_weight,
        out_weight,
        up_weight,
        down_weight,
    )
    first_2, second_2 = swap_cores(first_other), swap_cores(second_other)
    third, third_other, grad_normed = back(
        doc_lengths,
        heads_active,
        inverse,
        levels,
        parts,
        first_other,
        qkv,
        tokens,
        qkv_weight,
        out_weight,
    )
    third_2 = swap_cores(third_other)
    first_2, _ = lax.optimization_barrier((first_2, third))
    down_sent, down_kept = down_grads(first, first_other, first_2)
    up_sent, up_kept, qkv_sent, qkv_kept = up_and_qkv_grads(
        second, second_other, second_2, third, third_other, third_2, down_sent
    )

    mixed, input_grad = ends(
        router,
        norm_gain,
        grad_normed,
        first_other,
        tokens,
        middle,
        act,
        down_weight,
        qkv_sent,
    )

    every = slice(None)
    grads = {}

    def down_done(*terms):
        grads["down"] = total(terms, every, slice(0, D))
        out = total(terms, every, slice(D, D + T))
        grads["out"] = out.reshape(4, 8, T).transpose(1, 0, 2).reshape(8, D)
        grads["down"], grads["out"] = lax.optimization_barrier((grads["down"], grads["out"]))
        return grads["out"]

    def up_done(*terms):
        grads["up"] = jnp.concatenate([total(terms), grads["more_up"]], 1)
        return grads["up"]

    def qkv_done(*terms):
        grads["qkv"] = total(terms, every, slice(0, 3 * D))
        end = 3 * D + FF - UP
        grads["more_up"] = total(terms, every, slice(3 * D, end))
        line = total(terms, every, slice(end, end + 128))
        grads["gains"] = [line[:, n] for n in range(3)]
        bits = line[0, 3 : 3 + BITS * NEST].astype(jnp.int32).reshape(NEST, BITS)
        grads["counts"] = jnp.sum(bits << jnp.arange(BITS, dtype=jnp.int32)[None, :], 1)
        done = (grads["qkv"], grads["more_up"], grads["counts"], *grads["gains"])
        done = lax.optimization_barrier(done)
        grads["qkv"], grads["more_up"], grads["counts"], *grads["gains"] = done
        return grads["qkv"]

    take_turns(
        mixed,
        TURNS,
        d=chain(down_sent, down_kept, "yxz", (4, 4, 32, D + T), down_done),
        u=chain(up_sent, up_kept, "xyz", (4, 4, 8, UP), up_done),
        q=chain(qkv_sent, qkv_kept, "zyx", (4, 4, 8, 3 * D + FF - UP + 128), qkv_done),
    )
    gain_grad, ln_gain_grad, ln_bias_grad = grads["gains"]
    return (
        mixed,
        input_grad,
        gain_grad,
        grads["qkv"],
        grads["out"],
        ln_gain_grad,
        ln_bias_grad,
        grads["up"],
        grads["down"],
        grads["counts"],
    )


def solution(mesh):
    finer = Mesh(mesh.devices.reshape(4, 4, 4, 2), AX)
    rows = P(AX, None)
    return jax.shard_map(
        body,
        mesh=finer,
        in_specs=(rows, P(), P(), P(), P(), P(), P(), P(), rows, P(AX), rows, rows, rows),
        out_specs=(rows, rows, P(AX), rows, rows, P(AX), P(AX), rows, rows, P()),
        check_vma=False,
    )
```

```python
import jax
import jax.numpy as jnp
import numpy as np
from jax import lax
from jax.experimental import pallas as pl
from jax.experimental.pallas import tpu as pltpu
from jax.sharding import Mesh
from jax.sharding import PartitionSpec as P

HD = 64
NEST = 4
AX = ("y", "x", "z", "c")

NEG = -1e30
EPS = 1e-05
F32 = jnp.float32
BF16 = jnp.bfloat16
T = 256
D = 1024
FF = 4096
GW = 256
GROUPS = D // GW
HEADS = GW // HD
ACT, MERGED, FIRST_OWN, GB, GA, FIRST = 0, 512, 640, 640, 896, 1152
ZED, NORMED, ZED_Z, SECOND_OWN, GP, SECOND = 0, 128, 256, 384, 384, 1408
LINES, THIRD_OWN, GQKV, THIRD = 0, 128, 128, 896
TURNS = "dquqduqduqduqdudqu"
UP = 3584
BITS = 9
MIB = 1024 * 1024


def nn(a, b):
    return lax.dot_general(a, b, (((1,), (0,)), ((), ())), preferred_element_type=F32)


def nt(a, b):
    return lax.dot_general(a, b, (((1,), (1,)), ((), ())), preferred_element_type=F32)


def tn(a, b):
    return lax.dot_general(a, b, (((0,), (0,)), ((), ())), preferred_element_type=F32)


def sds(shape, dtype):
    return jax.ShapeDtypeStruct(shape, dtype)


def smem():
    return pl.BlockSpec(memory_space=pltpu.SMEM)


def vmem():
    return pl.BlockSpec(memory_space=pltpu.VMEM)


def hbm():
    return pl.BlockSpec(memory_space=pltpu.HBM)


def call(kernel, name, flops, moved, room, anywhere=(), **kw):
    def in_hbm(spec):
        return spec.memory_space == pltpu.HBM

    kw["out_shape"] = [
        pltpu.HBM(s.shape, s.dtype) if in_hbm(spec) else s
        for s, spec in zip(kw["out_shape"], kw["out_specs"])
    ]
    run = pl.pallas_call(
        kernel,
        name=name,
        compiler_params=pltpu.CompilerParams(vmem_limit_bytes=room * MIB),
        cost_estimate=pl.CostEstimate(flops=flops, bytes_accessed=moved, transcendentals=0),
        **kw,
    )

    def placed(*args):
        return run(
            *(
                pltpu.with_memory_space_constraint(arg, pltpu.HBM)
                if in_hbm(spec) and n not in anywhere
                else arg
                for n, (arg, spec) in enumerate(zip(args, kw["in_specs"]))
            )
        )

    return placed


def first_halves():
    return lax.broadcasted_iota(jnp.int32, (T, 128), 1) % HD < HD // 2


def head_of(g):
    return HEADS * g + lax.broadcasted_iota(jnp.int32, (T, GW), 1) // HD


def by_head(x):
    lane = lax.broadcasted_iota(jnp.int32, (T, GW), 1)
    zero = jnp.zeros((T, GW), x.dtype)
    own = [(lane >= HD * h) & (lane < HD * h + HD) for h in range(HEADS)]
    return jnp.concatenate([jnp.where(keep, x, zero) for keep in own], 0)


def turned(x, cosine, sine, first):
    parts = []
    for at in range(0, x.shape[1], 128):
        part = x[:, at : at + 128]
        other = jnp.where(first, pltpu.roll(part, 128 - HD // 2, 1), pltpu.roll(part, HD // 2, 1))
        parts.append(part * cosine + other * sine)
    return jnp.concatenate(parts, 1)


def doc_ends(lengths):
    return lengths[0, 0], lengths[0, 0] + lengths[0, 1]


def doc_start(lengths, place):
    end_0, end_1 = doc_ends(lengths)
    return jnp.where(place >= end_1, end_1, jnp.where(place >= end_0, end_0, 0))


def of_doc(lengths, place, values):
    end_0, end_1 = doc_ends(lengths)
    late = jnp.where(place >= end_1, values[0, 2], values[0, 1])
    return jnp.where(place >= end_0, late, values[0, 0])


def normalized(middle):
    shifted = middle - jnp.mean(middle, -1, keepdims=True)
    rstd = lax.rsqrt(jnp.mean(shifted * shifted, -1, keepdims=True) + EPS)
    return shifted * rstd, rstd


def block_order(axis):
    p = lax.axis_index(axis)
    core = lax.axis_index("c")
    return [p ^ (1 + 2 * core), p ^ 2, p, p ^ (3 - 2 * core)]


def load(src, dst, sem):
    copy = pltpu.make_async_copy(src, dst, sem)
    copy.start()
    return copy


def columns(j, size):
    if isinstance(j, int):
        return pl.ds(j * size, size)
    return pl.ds(pl.multiple_of(j * size, size), size)


def upright(row):
    return jnp.broadcast_to(row, (8, T)).T[:, :1]


def places():
    return lax.broadcasted_iota(jnp.int32, (T, 128), 0)


def rotary(lengths, inverse):
    phase = (places() - doc_start(lengths, places())).astype(F32) * inverse[...]
    sine = jnp.sin(phase)
    return jnp.cos(phase), jnp.where(first_halves(), -sine, sine)


def start(copies):
    for copy in copies:
        copy.start()


def wait(copies):
    for copy in copies:
        copy.wait()


def front_kernel(
    lengths,
    heads,
    norm_gain,
    inverse,
    ln_gain,
    ln_bias,
    router,
    bucket,
    tokens_hbm,
    cot_hbm,
    wqkv_hbm,
    wo_hbm,
    up_hbm,
    down_hbm,
    parts_out,
    first_mine,
    first_other,
    second_mine,
    second_other,
    qkv_out,
    act_out,
    middle_out,
    parts,
    tokens,
    cot,
    wqkv,
    wo,
    up,
    down,
    qkv,
    normed,
    merged,
    zed,
    gb,
    act,
    act_turned,
    gp,
    turned_f,
    left,
    middle,
    ga,
    bias,
    active,
    level,
    in_sem,
    ffn_sem,
    act_sem,
    gp_sem,
    left_sem,
    out_sem,
):
    core = lax.axis_index("c")
    firsts, seconds = (first_mine, first_other), (second_mine, second_other)
    loads = [load(tokens_hbm, tokens, in_sem.at[0])]
    for n in range(3):
        src = wqkv_hbm.at[:, n * D : (n + 1) * D]
        loads.append(pltpu.make_async_copy(src, wqkv.at[n], in_sem.at[1 + n]))
    loads[1].start()

    def ffn_loads(j):
        at = columns(j, D)
        return (
            pltpu.make_async_copy(up_hbm.at[:, at], up.at[:, at], ffn_sem.at[0, j]),
            pltpu.make_async_copy(down_hbm.at[at, :], down.at[at, :], ffn_sem.at[1, j]),
        )

    stores = []

    def turn(value):
        turned_f[...] = value.astype(F32).T.reshape(turned_f.shape)

    def store_left(n, axis, refs, at):
        for side, ref in enumerate(refs):
            half = core if side == 0 else 1 - core
            for i in range(4):
                if axis == 0:
                    rows = turned_f[i, :, :, half]
                elif axis == 1:
                    rows = turned_f[:, i, :, half]
                else:
                    rows = turned_f[:, :, i, half]
                left[side, n, :, pl.ds(T * i, T)] = rows.reshape(128, T).astype(BF16)
            dst = ref.at[pl.ds(at, 128), :]
            stores.append(load(left.at[side, n], dst, left_sem.at[side, n]))

    first = first_halves()
    scale = jnp.asarray(HD**-0.5, BF16)
    cosine, sine = rotary(lengths, inverse)
    row = lax.broadcasted_iota(jnp.int32, (T, T), 0)
    col = lax.broadcasted_iota(jnp.int32, (T, T), 1)
    bias[...] = jnp.where((col >= doc_start(lengths, row)) & (col <= row), 0.0, NEG)
    active[...] = of_doc(lengths, lax.broadcasted_iota(jnp.int32, (T, GW), 0), heads)
    level[...] = upright(bucket[...])
    prob = upright(router[...])

    loads[0].wait()
    start(loads[2:4])
    resid = tokens[...].astype(F32)
    rscale = lax.rsqrt(jnp.mean(resid * resid, -1, keepdims=True) + EPS)
    normed[...] = (resid * rscale * norm_gain[...]).astype(BF16)
    for n in range(3):
        loads[1 + n].wait()
        if n == 1:
            loads.append(load(cot_hbm, cot, in_sem.at[4]))
        if n == 2:
            loads.append(load(wo_hbm, wo, in_sem.at[5]))
            for copy in ffn_loads(0) + ffn_loads(1):
                copy.start()
        part = nn(normed[...], wqkv[n])
        qkv[n] = (turned(part, cosine, sine, first) if n < 2 else part).astype(BF16)
    stores.append(load(qkv, qkv_out, out_sem.at[0]))

    def attend(g, carry):
        at = columns(g, GW)
        keys, values = by_head(qkv[1, :, at]), by_head(qkv[2, :, at])
        s = nt(qkv[0, :, at] * scale, keys)
        parts = []
        for h in range(HEADS):
            one = s[:, T * h : T * h + T] + bias[...]
            e = jnp.exp(one - jnp.max(one, -1, keepdims=True))
            parts.append((e / jnp.sum(e, -1, keepdims=True)).astype(BF16))
        out = nn(jnp.concatenate(parts, 1), values)
        merged[:, at] = jnp.where(head_of(g) < active[...], out, 0.0).astype(BF16)

        @pl.when((g > 0) & (g < NEST - 1))
        def _():
            for copy in ffn_loads(g + 1):
                copy.start()

        return carry

    lax.fori_loop(0, GROUPS, attend, 0)
    loads[5].wait()
    middle[...] = tokens[...].astype(F32) + nn(merged[...], wo[...])
    stores.append(load(middle, middle_out, out_sem.at[1]))
    normed_mid, _ = normalized(middle[...])
    zed[...] = (normed_mid * ln_gain[...] + ln_bias[...]).astype(BF16)
    loads[4].wait()
    gb[...] = (cot[...].astype(F32) * prob).astype(BF16)
    stores.append(load(gb, first_other.at[pl.ds(GB, T), :], out_sem.at[2]))

    def act_stores(j):
        at = (pl.ds(ACT, 512), columns(j, T))
        return [
            pltpu.make_async_copy(act_turned.at[side, :, at[1]], ref.at[at], act_sem.at[side, j])
            for side, ref in enumerate(firsts)
        ]

    def act_store(j):
        at = columns(j, D)
        return pltpu.make_async_copy(act.at[:, at], act_out.at[:, at], act_sem.at[2, j])

    def gp_store(j):
        rows = pl.ds(pl.multiple_of(GP + T * j, 128), T)
        return pltpu.make_async_copy(gp.at[:, columns(j, D)], second_other.at[rows, :], gp_sem.at[j])

    def hidden(j, carry):
        copy_up, copy_down = ffn_loads(j)
        at = columns(j, D)
        copy_up.wait()
        r = jnp.where(level[...] >= j, jnp.maximum(nn(zed[...], up[:, at]), 0.0), 0.0)
        a = (r * r).astype(BF16)
        act[:, at] = a
        by_core = a.T.reshape(16, 2, 32, T)
        low_rows, high_rows = by_core[:, 0].reshape(512, T), by_core[:, 1].reshape(512, T)
        act_store(j).start()
        act_turned[0, :, columns(j, T)] = jnp.where(core == 0, low_rows, high_rows)
        act_turned[1, :, columns(j, T)] = jnp.where(core == 0, high_rows, low_rows)
        for copy in act_stores(j):
            copy.start()
        copy_down.wait()
        gp[:, at] = (nt(gb[...], down[at, :]) * 2.0 * r).astype(BF16)
        gp_store(j).start()
        return carry

    lax.fori_loop(0, NEST, hidden, 0)
    turn(zed[...])
    store_left(0, 1, seconds, ZED)
    store_left(3, 2, seconds, ZED_Z)
    turn(normed[...])
    store_left(1, 2, seconds, NORMED)
    turn(merged[...])
    store_left(2, 0, firsts, MERGED)

    grad_zed = nt(gp[...], up[...]).astype(BF16).astype(F32)
    normed_mid, rstd = normalized(middle[...])
    parts[0:1, :] = jnp.sum(grad_zed * normed_mid, 0, keepdims=True)
    parts[1:2, :] = jnp.sum(grad_zed, 0, keepdims=True)
    grad_norm = grad_zed * ln_gain[...]
    grad = cot[...].astype(F32) + rstd * (
        grad_norm
        - jnp.mean(grad_norm, -1, keepdims=True)
        - normed_mid * jnp.mean(grad_norm * normed_mid, -1, keepdims=True)
    )
    ga[...] = grad.astype(BF16)
    stores.append(load(parts, parts_out, out_sem.at[3]))
    stores.append(load(ga, first_other.at[pl.ds(GA, T), :], out_sem.at[4]))
    for j in range(NEST):
        wait(act_stores(j) + [act_store(j), gp_store(j)])
    wait(stores)


def front(lengths, heads, norm_gain, inverse, ln_gain, ln_bias, router, bucket, *arrays):
    row_b = sds((T, D), BF16)
    scratch = [
        sds((8, D), F32),
        row_b,
        row_b,
        sds((3, D, D), BF16),
        sds((D, D), BF16),
        sds((D, FF), BF16),
        sds((FF, D), BF16),
        sds((3, T, D), BF16),
        row_b,
        row_b,
        row_b,
        row_b,
        sds((T, FF), BF16),
        sds((2, 512, D), BF16),
        sds((T, FF), BF16),
        sds((4, 4, 4, 2, 8, T), F32),
        sds((2, 4, 128, D), BF16),
        sds((T, D), F32),
        row_b,
        sds((T, T), F32),
        sds((T, GW), jnp.int32),
        sds((T, 1), jnp.int32),
    ]
    semaphores = [(6,), (2, NEST), (3, NEST), (NEST,), (2, 4), (5,)]
    return call(
        front_kernel,
        "front",
        2 * T * D * (4 * D + 3 * FF),
        40 * MIB,
        58,
        in_specs=[smem()] * 2 + [vmem()] * 6 + [hbm()] * 6,
        out_specs=[hbm()] * 8,
        out_shape=[
            sds((8, D), F32),
            sds((FIRST_OWN, D), BF16),
            sds((FIRST, D), BF16),
            sds((SECOND_OWN, D), BF16),
            sds((SECOND, D), BF16),
            sds((3, T, D), BF16),
            sds((T, FF), BF16),
            sds((T, D), F32),
        ],
        scratch_shapes=[pltpu.VMEM(s.shape, s.dtype) for s in scratch]
        + [pltpu.SemaphoreType.DMA(s) for s in semaphores],
    )(lengths, heads, norm_gain, inverse, ln_gain, ln_bias, router, bucket, *arrays)


def back_kernel(
    lengths,
    heads,
    inverse,
    bucket,
    parts_hbm,
    first_other,
    qkv_hbm,
    tokens_hbm,
    wqkv_hbm,
    wo_hbm,
    third_mine,
    third_other,
    grad_normed_out,
    parts,
    ga,
    qkv,
    grad_store,
    tokens,
    wqkv,
    wo,
    gqkv,
    lines_f,
    lines,
    bias,
    active,
    in_sem,
    w_sem,
    group_sem,
    out_sem,
):
    core = lax.axis_index("c")
    thirds = (third_mine, third_other)
    loads = [
        load(first_other.at[pl.ds(GA, T), :], ga, in_sem.at[0]),
        load(wo_hbm.at[pl.ds(0, GW), :], wo.at[pl.ds(0, GW), :], in_sem.at[1]),
        load(qkv_hbm.at[:, :, pl.ds(0, GW)], qkv.at[:, :, pl.ds(0, GW)], in_sem.at[2]),
    ]
    others = pl.ds(GW, D - GW)
    more = [
        pltpu.make_async_copy(wo_hbm.at[others, :], wo.at[others, :], in_sem.at[5]),
        pltpu.make_async_copy(qkv_hbm.at[:, :, others], qkv.at[:, :, others], in_sem.at[6]),
    ]
    late = [
        pltpu.make_async_copy(tokens_hbm, tokens, in_sem.at[3]),
        pltpu.make_async_copy(parts_hbm, parts, in_sem.at[7]),
    ]
    for n in range(3):
        src = wqkv_hbm.at[:, n * D : (n + 1) * D]
        late.append(pltpu.make_async_copy(src, wqkv.at[n], w_sem.at[n]))

    first = first_halves()
    scale = jnp.asarray(HD**-0.5, BF16)
    cosine, sine = rotary(lengths, inverse)
    sine = -sine
    query = lax.broadcasted_iota(jnp.int32, (T, T), 1)
    key = lax.broadcasted_iota(jnp.int32, (T, T), 0)
    bias[...] = jnp.where((key >= doc_start(lengths, query)) & (key <= query), 0.0, NEG)
    active[...] = of_doc(lengths, lax.broadcasted_iota(jnp.int32, (T, GW), 0), heads)
    wait(loads)
    for copy in more:
        copy.start()

    def group_stores(g):
        at = columns(g, GW)
        return [
            pltpu.make_async_copy(
                gqkv.at[n, :, at], third_other.at[pl.ds(GQKV + T * n, T), at], group_sem.at[n, g]
            )
            for n in range(3)
        ]

    def attend_back(g, carry):
        @pl.when(g == 1)
        def _():
            wait(more)
            start(late)

        at = columns(g, GW)
        gm = nt(ga[...], wo[at, :])
        gm = jnp.where(head_of(g) < active[...], gm, 0.0).astype(BF16)
        gms, queries = by_head(gm), by_head(qkv[0, :, at] * scale)
        k = qkv[1, :, at]
        s = nt(k, queries)
        grad_p = nt(qkv[2, :, at], gms)
        parts_p, parts_s = [], []
        for h in range(HEADS):
            one = s[:, T * h : T * h + T] + bias[...]
            e = jnp.exp(one - jnp.max(one, 0, keepdims=True))
            p = e / jnp.sum(e, 0, keepdims=True)
            grad = grad_p[:, T * h : T * h + T]
            parts_p.append(p.astype(BF16))
            grad = p * (grad - jnp.sum(p * grad, 0, keepdims=True))
            parts_s.append(grad.astype(BF16))
        grad_s = jnp.concatenate(parts_s, 1)
        grad_v = nn(jnp.concatenate(parts_p, 1), gms)
        grad_k = nn(grad_s, queries)
        wide = nn((k * scale).T, grad_s)
        grad_q = [wide[HD * h : HD * h + HD, T * h : T * h + T] for h in range(HEADS)]
        grad_q = jnp.concatenate(grad_q, 0).T
        gqkv[0, :, at] = turned(grad_q, cosine, sine, first).astype(BF16)
        gqkv[1, :, at] = turned(grad_k, cosine, sine, first).astype(BF16)
        gqkv[2, :, at] = grad_v.astype(BF16)
        for copy in group_stores(g):
            copy.start()
        return carry

    lax.fori_loop(0, GROUPS, attend_back, 0)

    wait(late)
    grad_normed = nt(gqkv[0], wqkv[0]) + nt(gqkv[1], wqkv[1]) + nt(gqkv[2], wqkv[2])
    resid = tokens[...].astype(F32)
    rscale = lax.rsqrt(jnp.mean(resid * resid, -1, keepdims=True) + EPS)
    unit = resid * rscale
    gain_part = jnp.sum(grad_normed * unit, 0, keepdims=True)
    grad_store[...] = grad_normed
    stores = [load(grad_store, grad_normed_out, out_sem.at[0])]

    item = lax.broadcasted_iota(jnp.int32, (128, 1), 0)
    count = jnp.zeros((128, 1), jnp.int32)
    for n in range(NEST):
        total = jnp.sum((bucket[...] == n).astype(jnp.int32), 1, keepdims=True)
        at = item - 3 - BITS * n
        bit = lax.shift_right_logical(total, jnp.clip(at, 0, BITS - 1)) & 1
        count = jnp.where((at >= 0) & (at < BITS), bit, count)
    wide = jnp.where(item == 0, gain_part, jnp.where(item == 1, parts[0:1, :], parts[1:2, :]))
    lines_f[...] = jnp.where(item < 3, wide, count.astype(F32)).T.reshape(lines_f.shape)
    for side, ref in enumerate(thirds):
        half = core if side == 0 else 1 - core
        for i in range(4):
            part = lines_f[:, :, i, half].reshape(128, 128).astype(BF16)
            lines[side, :, pl.ds(128 * i, 128)] = part
        dst = ref.at[pl.ds(LINES, 128), pl.ds(0, 512)]
        stores.append(load(lines.at[side], dst, out_sem.at[1 + side]))
    for g in range(GROUPS):
        wait(group_stores(g))
    wait(stores)


def back(lengths, heads, inverse, bucket, parts, *arrays):
    scratch = [
        sds((8, D), F32),
        sds((T, D), BF16),
        sds((3, T, D), BF16),
        sds((T, D), F32),
        sds((T, D), BF16),
        sds((3, D, D), BF16),
        sds((D, D), BF16),
        sds((3, T, D), BF16),
        sds((4, 4, 4, 2, 8, 128), F32),
        sds((2, 128, 512), BF16),
        sds((T, T), F32),
        sds((T, GW), jnp.int32),
    ]
    return call(
        back_kernel,
        "back",
        2 * T * D * 4 * D + 10 * 16 * T * T * 256,
        18 * MIB,
        32,
        in_specs=[smem()] * 2 + [vmem()] * 2 + [hbm()] * 6,
        out_specs=[hbm()] * 3,
        out_shape=[sds((THIRD_OWN, D), BF16), sds((THIRD, D), BF16), sds((T, D), F32)],
        scratch_shapes=[pltpu.VMEM(s.shape, s.dtype) for s in scratch]
        + [pltpu.SemaphoreType.DMA(s) for s in [(8,), (3,), (3, GROUPS), (3,)]],
    )(lengths, heads, inverse, bucket, parts, *arrays)


def ends_kernel(
    router,
    norm_gain,
    grad_normed_hbm,
    first_other,
    tokens_hbm,
    middle_hbm,
    act_hbm,
    down_hbm,
    after,
    mixed_out,
    input_grad_out,
    grad_normed,
    ga,
    tokens,
    middle,
    act,
    down,
    mixed,
    sem,
    ffn_sem,
):
    loads = [
        load(grad_normed_hbm, grad_normed, sem.at[0]),
        load(tokens_hbm, tokens, sem.at[1]),
        load(first_other.at[pl.ds(GA, T), :], ga, sem.at[2]),
    ]
    middle_load = load(middle_hbm, middle, sem.at[3])
    stages = []
    for j in range(NEST):
        at = pl.ds(j * D, D)
        stages.append(
            [
                pltpu.make_async_copy(act_hbm.at[:, at], act.at[:, at], ffn_sem.at[0, j]),
                pltpu.make_async_copy(down_hbm.at[at, :], down.at[at, :], ffn_sem.at[1, j]),
            ]
        )
        start(stages[j])
    wait(loads)
    resid = tokens[...].astype(F32)
    rscale = lax.rsqrt(jnp.mean(resid * resid, -1, keepdims=True) + EPS)
    unit = resid * rscale
    grad_unit = grad_normed[...] * norm_gain[...]
    grad_normed[...] = ga[...].astype(F32) + rscale * (
        grad_unit - unit * jnp.mean(grad_unit * unit, -1, keepdims=True)
    )
    stores = [load(grad_normed, input_grad_out, sem.at[4])]
    for stage in stages:
        wait(stage)
    branch = nn(act[...], down[...]).astype(BF16).astype(F32)
    middle_load.wait()
    mixed[...] = (middle[...] + upright(router[...]) * branch).astype(BF16)
    stores.append(load(mixed, mixed_out, sem.at[5]))
    wait(stores)


def ends(router, norm_gain, *arrays):
    return call(
        ends_kernel,
        "ends",
        2 * T * D * FF,
        16 * MIB,
        20,
        in_specs=[vmem()] * 2 + [hbm()] * 7,
        out_specs=[hbm()] * 2,
        out_shape=[sds((T, D), BF16), sds((T, D), F32)],
        scratch_shapes=[
            pltpu.VMEM((T, D), F32),
            pltpu.VMEM((T, D), BF16),
            pltpu.VMEM((T, D), BF16),
            pltpu.VMEM((T, D), F32),
            pltpu.VMEM((T, FF), BF16),
            pltpu.VMEM((FF, D), BF16),
            pltpu.VMEM((T, D), BF16),
            pltpu.SemaphoreType.DMA((6,)),
            pltpu.SemaphoreType.DMA((2, NEST)),
        ],
    )(router, norm_gain, *arrays)


def load_left(refs, at, rows, axis, left, sem):
    return [
        pltpu.make_async_copy(
            ref.at[pl.ds(at, rows), columns(block, T)],
            left.at[pl.ds(rows * i, rows), pl.ds(T * m, T)],
            sem.at[i, m],
        )
        for i, block in enumerate(block_order(axis))
        for m, ref in enumerate(refs)
    ]


def load_right(refs, at, right, sem):
    return [
        pltpu.make_async_copy(ref.at[pl.ds(at, T), :], right.at[pl.ds(T * m, T), :], sem.at[m])
        for m, ref in enumerate(refs)
    ]


def store_out(out, at, sent, kept, sem):
    return [
        load(out.at[pl.ds(2 * side, 2), :, at], ref.at[:, :, at], sem.at[side])
        for side, ref in enumerate((sent, kept))
    ]


def down_grad_kernel(
    own, one, two, sent, kept, act, merged, gb, ga, out, act_sem, merged_sem, gb_sem, ga_sem, sem
):
    refs, split = (one, two), (own, two)
    gb_loads = load_right(refs, GB, gb, gb_sem)
    act_loads = load_left(split, ACT, 512, "y", act, act_sem)
    ga_loads = load_right(refs, GA, ga, ga_sem)
    merged_loads = load_left(split, MERGED, 128, "y", merged, merged_sem)
    stages = [gb_loads + act_loads[:2], act_loads[2:4], act_loads[4:6], act_loads[6:]]
    stages.append(ga_loads + merged_loads)
    stores = []
    start(stages[0] + stages[1])
    wide = pl.ds(0, D)
    for i in range(4):
        wait(stages[i])
        start(stages[i + 2] if i < 3 else [])
        out[i, :, wide] = nn(act[pl.ds(512 * i, 512), :], gb[...]).astype(BF16)
        dst = (sent, kept)[i // 2].at[i % 2, :, wide]
        stores.append(load(out.at[i, :, wide], dst, sem.at[0, i]))
    wait(stages[4])
    part = nn(merged[...], ga[...])
    more = pl.ds(D, T)
    for i in range(4):
        rows = part[128 * i : 128 * i + 128].reshape(16, 8, D)
        quarters = [rows[:, :, T * q : T * q + T] for q in range(4)]
        out[i, :, more] = jnp.concatenate(quarters, 1).reshape(512, T).astype(BF16)
    stores += store_out(out, more, sent, kept, sem.at[1])
    wait(stores)


def down_grads(own, one, two):
    part = sds((2, 512, D + T), BF16)
    return call(
        down_grad_kernel,
        "down_and_out_grad",
        2 * T * D * (FF + D),
        10 * MIB,
        18,
        (2,),
        in_specs=[hbm()] * 3,
        out_specs=[hbm()] * 2,
        out_shape=[part, part],
        scratch_shapes=[
            pltpu.VMEM((FF // 2, 2 * T), BF16),
            pltpu.VMEM((512, 2 * T), BF16),
            pltpu.VMEM((2 * T, D), BF16),
            pltpu.VMEM((2 * T, D), BF16),
            pltpu.VMEM((4, 512, D + T), BF16),
            pltpu.SemaphoreType.DMA((4, 2)),
            pltpu.SemaphoreType.DMA((4, 2)),
            pltpu.SemaphoreType.DMA((2,)),
            pltpu.SemaphoreType.DMA((2,)),
            pltpu.SemaphoreType.DMA((2, 4)),
        ],
    )(own, one, two)


def up_and_qkv_kernel(
    own,
    one,
    two,
    late_own,
    three,
    four,
    after,
    up_sent,
    up_kept,
    qkv_sent,
    qkv_kept,
    zed,
    zed_z,
    normed,
    gp,
    gqkv,
    lines,
    up_out,
    qkv_out,
    zed_sem,
    zed_z_sem,
    normed_sem,
    gp_sem,
    gqkv_sem,
    line_sem,
    up_sem,
    qkv_sem,
):
    refs, split = (one, two), (own, two)
    late = (three, four)
    zed_loads = load_left(split, ZED, 128, "x", zed, zed_sem)
    gp_loads = [load_right(refs, GP + T * n, gp.at[n], gp_sem.at[n]) for n in range(4)]
    line_loads = [
        pltpu.make_async_copy(
            ref.at[pl.ds(LINES, 128), columns(block, 128)],
            lines.at[i, m],
            line_sem.at[i, m],
        )
        for i, block in enumerate(block_order("z"))
        for m, ref in enumerate((late_own, four))
    ]
    zed_z_loads = load_left(split, ZED_Z, 128, "z", zed_z, zed_z_sem)
    normed_loads = load_left(split, NORMED, 128, "z", normed, normed_sem)
    gqkv_loads = [load_right(late, GQKV + T * n, gqkv.at[n], gqkv_sem.at[n]) for n in range(3)]
    stages = [zed_loads + gp_loads[0], *gp_loads[1:], normed_loads + gqkv_loads[0]]
    stages += [gqkv_loads[1], gqkv_loads[2] + zed_z_loads + line_loads, []]
    stores = []
    start(stages[0] + stages[1])
    for n in range(4):
        wait(stages[n])
        start(stages[n + 2])
        width = min(D, UP - n * D)
        at = pl.ds(n * D, width)
        part = nn(zed[...], gp[n, :, :width])
        up_out[:, :, at] = part.astype(BF16).reshape(4, 128, width)
        stores += store_out(up_out, at, up_sent, up_kept, up_sem.at[n])
    for n in range(3):
        wait(stages[4 + n])
        start(stages[6] if n == 0 else [])
        at = pl.ds(n * D, D)
        qkv_out[:, :, at] = nn(normed[...], gqkv[n]).astype(BF16).reshape(4, 128, D)
        stores += store_out(qkv_out, at, qkv_sent, qkv_kept, qkv_sem.at[n])
    more = FF - UP
    part = nn(zed_z[...], gp[3, :, D - more :])
    qkv_out[:, :, pl.ds(3 * D, more)] = part.astype(BF16).reshape(4, 128, more)
    both_lines = (lines[:, 0].astype(F32) + lines[:, 1].astype(F32)).astype(BF16)
    qkv_out[:, :, pl.ds(3 * D + more, 128)] = both_lines
    at = pl.ds(3 * D, more + 128)
    stores += store_out(qkv_out, at, qkv_sent, qkv_kept, qkv_sem.at[3])
    wait(stores)


def up_and_qkv_grads(own, one, two, late_own, three, four, after):
    up = sds((2, 128, UP), BF16)
    qkv = sds((2, 128, 3 * D + FF - UP + 128), BF16)
    return call(
        up_and_qkv_kernel,
        "up_and_qkv_grad",
        2 * T * D * (FF + 3 * D),
        16 * MIB,
        24,
        (2, 5),
        in_specs=[hbm()] * 7,
        out_specs=[hbm()] * 4,
        out_shape=[up, up, qkv, qkv],
        scratch_shapes=[
            pltpu.VMEM((512, 2 * T), BF16),
            pltpu.VMEM((512, 2 * T), BF16),
            pltpu.VMEM((512, 2 * T), BF16),
            pltpu.VMEM((4, 2 * T, D), BF16),
            pltpu.VMEM((3, 2 * T, D), BF16),
            pltpu.VMEM((4, 2, 128, 128), BF16),
            pltpu.VMEM((4, 128, UP), BF16),
            pltpu.VMEM((4, 128, 3 * D + FF - UP + 128), BF16),
            pltpu.SemaphoreType.DMA((4, 2)),
            pltpu.SemaphoreType.DMA((4, 2)),
            pltpu.SemaphoreType.DMA((4, 2)),
            pltpu.SemaphoreType.DMA((4, 2)),
            pltpu.SemaphoreType.DMA((3, 2)),
            pltpu.SemaphoreType.DMA((4, 2)),
            pltpu.SemaphoreType.DMA((4, 2)),
            pltpu.SemaphoreType.DMA((4, 2)),
        ],
    )(own, one, two, late_own, three, four, after)


def swap_cores(array):
    return lax.ppermute(array, "c", [(0, 1), (1, 0)])


def pairs(mask_0, mask_1):
    perm = []
    for p in range(4):
        perm.append((2 * p, 2 * (p ^ mask_0)))
        perm.append((2 * p + 1, 2 * (p ^ mask_1) + 1))
    return perm


def ordered(token, *arrays):
    return lax.optimization_barrier((*arrays, token))[:-1]


def chain(sent, kept, axes, shape, finish):
    left = [axis for axis in ("y", "x", "z") if axis != axes[0]]
    for axis in axes:
        got = lax.ppermute(sent, (axis, "c"), pairs(1, 3))
        token = yield sent
        got, kept = ordered(token, got, kept)
        more = (got[1].astype(F32) + kept[1].astype(F32)).astype(BF16)
        got_2 = lax.ppermute(more, (axis, "c"), pairs(3, 1))
        token = yield more
        got, kept, got_2 = ordered(token, got, kept, got_2)
        terms = [got.reshape(2, *shape), kept.reshape(2, *shape), got_2.reshape(1, *shape)]
        if not left:
            return finish(*terms)
        following = axes[axes.index(axis) + 1]
        dim = left.index(following)
        left.pop(dim)
        shape = shape[:dim] + shape[dim + 1 :]

        def block(at):
            total = 0.0
            for term in terms:
                start = [0] * term.ndim
                start[1 + dim] = at
                sizes = (1,) + term.shape[1 : 1 + dim] + (1,) + term.shape[2 + dim :]
                total = total + lax.dynamic_slice(term, start, sizes).astype(F32)
            return total.reshape(shape)

        first, across, own, second = [block(at) for at in block_order(following)]
        sent = jnp.stack([first, across]).astype(BF16)
        kept = jnp.stack([own, second])


def total(terms, *at):
    return sum(term[(0, *at)].astype(F32) for term in terms)


def take_turns(token, turns, **chains):
    for steps in chains.values():
        next(steps)
    for turn in turns:
        token = next_step(chains[turn], token)


def next_step(steps, token):
    try:
        return steps.send(token)
    except StopIteration as end:
        return end.value


def body(
    tokens,
    norm_gain,
    qkv_weight,
    out_weight,
    ln_gain,
    ln_bias,
    up_weight,
    down_weight,
    buckets,
    router_prob,
    heads_active,
    doc_lengths,
    cotangent,
):
    norm_gain, ln_gain, ln_bias = [v.reshape(1, D) for v in (norm_gain, ln_gain, ln_bias)]
    router = router_prob.reshape(1, T)
    levels = buckets.reshape(1, T)
    inverse = np.tile(10000.0 ** (-2.0 * np.arange(HD // 2) / HD), 4).reshape(1, 128)
    inverse = jnp.asarray(inverse, F32)

    parts, first, first_other, second, second_other, qkv, act, middle = front(
        doc_lengths,
        heads_active,
        norm_gain,
        inverse,
        ln_gain,
        ln_bias,
        router,
        levels,
        tokens,
        cotangent,
        qkv_weight,
        out_weight,
        up_weight,
        down_weight,
    )
    first_2, second_2 = swap_cores(first_other), swap_cores(second_other)
    third, third_other, grad_normed = back(
        doc_lengths,
        heads_active,
        inverse,
        levels,
        parts,
        first_other,
        qkv,
        tokens,
        qkv_weight,
        out_weight,
    )
    third_2 = swap_cores(third_other)
    first_2, _ = lax.optimization_barrier((first_2, third))
    down_sent, down_kept = down_grads(first, first_other, first_2)
    up_sent, up_kept, qkv_sent, qkv_kept = up_and_qkv_grads(
        second, second_other, second_2, third, third_other, third_2, down_sent
    )

    mixed, input_grad = ends(
        router,
        norm_gain,
        grad_normed,
        first_other,
        tokens,
        middle,
        act,
        down_weight,
        qkv_sent,
    )

    every = slice(None)
    grads = {}

    def down_done(*terms):
        grads["down"] = total(terms, every, slice(0, D))
        out = total(terms, every, slice(D, D + T))
        grads["out"] = out.reshape(4, 8, T).transpose(1, 0, 2).reshape(8, D)
        grads["down"], grads["out"] = lax.optimization_barrier((grads["down"], grads["out"]))
        return grads["out"]

    def up_done(*terms):
        grads["up"] = jnp.concatenate([total(terms), grads["more_up"]], 1)
        return grads["up"]

    def qkv_done(*terms):
        grads["qkv"] = total(terms, every, slice(0, 3 * D))
        end = 3 * D + FF - UP
        grads["more_up"] = total(terms, every, slice(3 * D, end))
        line = total(terms, every, slice(end, end + 128))
        grads["gains"] = [line[:, n] for n in range(3)]
        bits = line[0, 3 : 3 + BITS * NEST].astype(jnp.int32).reshape(NEST, BITS)
        grads["counts"] = jnp.sum(bits << jnp.arange(BITS, dtype=jnp.int32)[None, :], 1)
        done = (grads["qkv"], grads["more_up"], grads["counts"], *grads["gains"])
        done = lax.optimization_barrier(done)
        grads["qkv"], grads["more_up"], grads["counts"], *grads["gains"] = done
        return grads["qkv"]

    take_turns(
        mixed,
        TURNS,
        d=chain(down_sent, down_kept, "yxz", (4, 4, 32, D + T), down_done),
        u=chain(up_sent, up_kept, "xzy", (4, 4, 8, UP), up_done),
        q=chain(qkv_sent, qkv_kept, "zyx", (4, 4, 8, 3 * D + FF - UP + 128), qkv_done),
    )
    gain_grad, ln_gain_grad, ln_bias_grad = grads["gains"]
    return (
        mixed,
        input_grad,
        gain_grad,
        grads["qkv"],
        grads["out"],
        ln_gain_grad,
        ln_bias_grad,
        grads["up"],
        grads["down"],
        grads["counts"],
    )


def solution(mesh):
    finer = Mesh(mesh.devices.reshape(4, 4, 4, 2), AX)
    rows = P(AX, None)
    return jax.shard_map(
        body,
        mesh=finer,
        in_specs=(rows, P(), P(), P(), P(), P(), P(), P(), rows, P(AX), rows, rows, rows),
        out_specs=(rows, rows, P(AX), rows, rows, P(AX), P(AX), rows, rows, P()),
        check_vma=False,
    )
```
